32 devices in a mesh: dp: 8 (over z, y), head: 4 (over x, core).
Axes of the slice: x: 2, y: 2, z: 4, core: 2. Of those that a mesh axis runs over, the one named last changes fastest.
Arguments:
- tokens: bfloat16 [16384, 1024], P('dp'), may hold values from -6 to 6
- segments: int32 [16, 1024], P('dp'), may hold values from 0 to 15, never falling along the last dimension, each value on 1 to 512 neighbouring positions
- cotangent: bfloat16 [16384, 1024], P('dp'), may hold values from -6 to 6
- gain_in: float32 [1024], replicated, may hold values from 0.5 to 1.5
- mamba_gate_weight: float32 [1024, 1536], P('dp', 'head'), may hold values from -0.1875 to 0.1875
- mamba_input_weight: float32 [1024, 1536], P('dp', 'head'), may hold values from -0.1875 to 0.1875
- w_dt: float32 [1024, 24], P('dp', 'head'), may hold values from -0.1875 to 0.1875
- w_bc: float32 [1024, 256], P('dp'), may hold values from -0.1875 to 0.1875
- convolution_input_taps: float32 [4, 1536], P(None, 'head'), may hold values from -3 to 3
- convolution_input_bias: float32 [1536], P('head'), may hold values from -0.5 to 0.5
- conv_bc: float32 [4, 256], replicated, may hold values from -3 to 3
- conv_bc_bias: float32 [256], replicated, may hold values from -0.5 to 0.5
- dt_bias: float32 [24], P('head'), may hold values from -4 to -1
- a_log: float32 [24], P('head'), may hold values from -3 to 1
- d_skip: float32 [24], P('head'), may hold values from 0.5 to 1.5
- w_q: float32 [1024, 512], P('dp', 'head'), may hold values from -0.1875 to 0.1875
- w_k: float32 [1024, 128], P('dp'), may hold values from -0.1875 to 0.1875
- w_v: float32 [1024, 128], P('dp'), may hold values from -0.1875 to 0.1875
- w_o: float32 [512, 1024], P('head', 'dp'), may hold values from -0.75 to 0.75
- mamba_output_weight: float32 [1536, 1024], P('head', 'dp'), may hold values from -0.15625 to 0.15625
- gain_ffn: float32 [1024], replicated, may hold values from 0.5 to 1.5
- w_gate: float32 [1024, 2048], P('dp', 'head'), may hold values from -0.1875 to 0.1875
- w_up: float32 [1024, 2048], P('dp', 'head'), may hold values from -0.1875 to 0.1875
- w_down: float32 [2048, 1024], P('head', 'dp'), may hold values from -0.125 to 0.125
Outputs:
- output: bfloat16 [16384, 1024], P('dp')
- grad_tokens: bfloat16 [16384, 1024], P('dp')
- grad_gain_in: float32 [1024], P('dp')
- grad_w_z: float32 [1024, 1536], P('dp', 'head')
- grad_w_x: float32 [1024, 1536], P('dp', 'head')
- grad_w_dt: float32 [1024, 24], P('dp', 'head')
- grad_w_bc: float32 [1024, 256], P(('dp', 'head'))
- grad_conv_x: float32 [4, 1536], P(None, 'head')
- grad_conv_x_bias: float32 [1536], P('head')
- grad_conv_bc: float32 [4, 256], P(None, ('dp', 'head'))
- grad_conv_bc_bias: float32 [256], P(('dp', 'head'))
- grad_dt_bias: float32 [24], P('head')
- grad_a_log: float32 [24], P('head')
- grad_d_skip: float32 [24], P('head')
- grad_w_q: float32 [1024, 512], P('dp', 'head')
- grad_w_k: float32 [1024, 128], P(('dp', 'head'))
- grad_w_v: float32 [1024, 128], P(('dp', 'head'))
- grad_w_o: float32 [512, 1024], P('head', 'dp')
- grad_w_out: float32 [1536, 1024], P('head', 'dp')
- grad_gain_ffn: float32 [1024], P('dp')
- grad_w_gate: float32 [1024, 2048], P('dp', 'head')
- grad_w_up: float32 [1024, 2048], P('dp', 'head')
- grad_w_down: float32 [2048, 1024], P('head', 'dp')
The draws below stay inside these ranges and needn't reach their ends.
Inputs may be any that keep to these rules, and one draw needn't show every extreme that they name: `segments`: document numbers never fall along a sequence, and a document has at most 512 tokens.
All inputs are finite; a program needn't handle non-finite values.
Results may differ from the reference program's by a relative error of at most 0.025.
Values may be sent and summed in bfloat16 or wider, within the bound.
No kernel may reach another device: no remote copies, remote signals or barrier semaphores. Data moves between devices by JAX's collectives and lax.ppermute only.
A program may use at most 320 MiB of HBM per device.

```python
import math
import jax
import jax.numpy as jnp
import numpy as np
from jax import lax

MODEL_WIDTH = 1024
MAMBA_HEADS = 24
MAMBA_HEAD_WIDTH = 64
STATE = 128
QHEADS = 8
KVHEADS = 2
HD = 64
FF = 2048
CONV_TAPS = 4
LEN = 1024
SEQS = 16
TOKENS = 16384


def shard_levels(own_key, dims, cuts, least, high):
    level, own = 1.0, jax.random.fold_in(own_key, 6)
    for dim, shards_of in cuts:
        draws = jnp.exp(jax.random.uniform(jax.random.fold_in(own, dim), (shards_of,), jnp.float32, least / len(cuts), high / len(cuts)))
        level = level * jnp.repeat(draws, dims[dim] // shards_of).reshape([-1 if axis == dim else 1 for axis in range(len(dims))])
    return level


def split_up(amount, total, most, skew):
    portions = [(1 << 20) // math.isqrt(rank ** skew) + 1 for rank in range(2, amount + 1)]
    rest, counts = total - most - (amount - 1), [1] * (amount - 1)
    while rest > 0:
        free = [i for i in range(amount - 1) if counts[i] < most]
        mass, left = sum([portions[i] for i in free]), rest
        for i in free:
            extra = min(most - counts[i], max(1, left * portions[i] // mass), rest)
            counts[i] = counts[i] + extra
            rest = rest - extra
    return np.array([most] + counts)


def ragged(key, number_of, total, bound, lean):
    if number_of == 2:
        one = jax.random.randint(key, (), max(1, total - bound), min(bound, total - 1) + 1)
        return jnp.stack([one, total - one])
    tallies = jnp.asarray(split_up(number_of, total, bound, lean), jnp.int32)
    twos = (number_of - 1) // 2
    giver, sink = tallies[1:1 + 2 * twos:2], tallies[2:2 + 2 * twos:2]
    room = jnp.minimum(giver - 1, bound - sink)
    moved = jax.random.randint(jax.random.fold_in(key, 1), (twos,), 0, 1 << 20) % (room + 1)
    tallies = tallies.at[1:1 + 2 * twos:2].set(giver - moved).at[2:2 + 2 * twos:2].set(sink + moved)
    return tallies[jax.random.permutation(jax.random.fold_in(key, 2), number_of)]


def gaussian(rng, extent, scale, reach, shards=(), kind=jnp.bfloat16):
    drawn = jax.random.normal(rng, extent, jnp.float32) * scale
    if len(shards) > 0:
        drawn = shard_levels(rng, extent, shards, -0.22, 0.18) * drawn
    return jnp.clip(drawn, min=-reach, max=reach).astype(kind)


def setup_inputs(seed: int = 0) -> dict:
    streams_of = jax.random.split(jax.random.key(seed), 25)
    tokens = gaussian(streams_of[0], (TOKENS, MODEL_WIDTH), 1.0, 6.0, ((0, 8),))
    segments = jax.vmap(lambda own: jnp.searchsorted(jnp.cumsum(ragged(own, max(LEN // 64, 4), LEN, LEN // 2, 2)), jnp.arange(LEN), side="right"))(jax.random.split(streams_of[1], SEQS)).reshape((SEQS, LEN)).astype(jnp.int32)
    cotangent = gaussian(streams_of[2], (TOKENS, MODEL_WIDTH), 1.0, 6.0, ((0, 8),))
    gain_in = jnp.clip(1.0 + 0.1 * jax.random.normal(streams_of[3], (MODEL_WIDTH,), jnp.float32), 0.5, 1.5)
    mamba_gate_weight = gaussian(streams_of[4], (MODEL_WIDTH, MAMBA_HEADS * MAMBA_HEAD_WIDTH), MODEL_WIDTH ** -0.5, 0.1875, ((0, 8), (1, 4)), jnp.float32)
    mamba_input_weight = gaussian(streams_of[5], (MODEL_WIDTH, MAMBA_HEADS * MAMBA_HEAD_WIDTH), MODEL_WIDTH ** -0.5, 0.1875, ((0, 8), (1, 4)), jnp.float32)
    w_dt = gaussian(streams_of[6], (MODEL_WIDTH, MAMBA_HEADS), MODEL_WIDTH ** -0.5, 0.1875, ((0, 8), (1, 4)), jnp.float32)
    w_bc = gaussian(streams_of[7], (MODEL_WIDTH, 2 * STATE), MODEL_WIDTH ** -0.5, 0.1875, ((0, 8),), jnp.float32)
    convolution_input_taps = gaussian(streams_of[8], (CONV_TAPS, MAMBA_HEADS * MAMBA_HEAD_WIDTH), 0.5, 3.0, ((1, 4),), jnp.float32)
    convolution_input_bias = jnp.clip(jax.random.uniform(streams_of[9], (MAMBA_HEADS * MAMBA_HEAD_WIDTH,), jnp.float32, -0.5, 0.5) * shard_levels(streams_of[9], (MAMBA_HEADS * MAMBA_HEAD_WIDTH,), ((0, 4),), -0.4, 0.0), -0.5, 0.5)
    conv_bc = gaussian(streams_of[10], (CONV_TAPS, 2 * STATE), 0.5, 3.0, (), jnp.float32)
    conv_bc_bias = jnp.clip(jax.random.uniform(streams_of[11], (2 * STATE,), jnp.float32, -0.5, 0.5), -0.5, 0.5)
    dt_bias = jnp.clip(-4.0 + 3.0 * jax.random.uniform(streams_of[12], (MAMBA_HEADS,), jnp.float32) ** shard_levels(streams_of[12], (MAMBA_HEADS,), ((0, 4),), -0.2, 0.2), -4.0, -1.0)
    a_log = jnp.clip(-3.0 + 4.0 * jax.random.uniform(streams_of[13], (MAMBA_HEADS,), jnp.float32) ** shard_levels(streams_of[13], (MAMBA_HEADS,), ((0, 4),), -0.2, 0.2), -3.0, 1.0)
    d_skip = jnp.clip(0.5 + 1.0 * jax.random.uniform(streams_of[14], (MAMBA_HEADS,), jnp.float32) ** shard_levels(streams_of[14], (MAMBA_HEADS,), ((0, 4),), -0.2, 0.2), 0.5, 1.5)
    w_q = gaussian(streams_of[15], (MODEL_WIDTH, QHEADS * HD), MODEL_WIDTH ** -0.5, 0.1875, ((0, 8), (1, 4)), jnp.float32)
    w_k = gaussian(streams_of[16], (MODEL_WIDTH, KVHEADS * HD), MODEL_WIDTH ** -0.5, 0.1875, ((0, 8),), jnp.float32)
    w_v = gaussian(streams_of[17], (MODEL_WIDTH, KVHEADS * HD), MODEL_WIDTH ** -0.5, 0.1875, ((0, 8),), jnp.float32)
    w_o = gaussian(streams_of[18], (QHEADS * HD, MODEL_WIDTH), HD ** -0.5, 0.75, ((0, 4), (1, 8)), jnp.float32)
    mamba_output_weight = gaussian(streams_of[19], (MAMBA_HEADS * MAMBA_HEAD_WIDTH, MODEL_WIDTH), (MAMBA_HEADS * MAMBA_HEAD_WIDTH) ** -0.5, 0.15625, ((0, 4), (1, 8)), jnp.float32)
    gain_ffn = jnp.clip(1.0 + 0.1 * jax.random.normal(streams_of[20], (MODEL_WIDTH,), jnp.float32), 0.5, 1.5)
    w_gate = gaussian(streams_of[21], (MODEL_WIDTH, FF), MODEL_WIDTH ** -0.5, 0.1875, ((0, 8), (1, 4)), jnp.float32)
    w_up = gaussian(streams_of[22], (MODEL_WIDTH, FF), MODEL_WIDTH ** -0.5, 0.1875, ((0, 8), (1, 4)), jnp.float32)
    w_down = gaussian(streams_of[23], (FF, MODEL_WIDTH), FF ** -0.5, 0.125, ((0, 4), (1, 8)), jnp.float32)
    return dict(tokens=tokens, segments=segments, cotangent=cotangent, gain_in=gain_in, mamba_gate_weight=mamba_gate_weight, mamba_input_weight=mamba_input_weight, w_dt=w_dt, w_bc=w_bc, convolution_input_taps=convolution_input_taps, convolution_input_bias=convolution_input_bias, conv_bc=conv_bc, conv_bc_bias=conv_bc_bias, dt_bias=dt_bias, a_log=a_log, d_skip=d_skip, w_q=w_q, w_k=w_k, w_v=w_v, w_o=w_o, mamba_output_weight=mamba_output_weight, gain_ffn=gain_ffn, w_gate=w_gate, w_up=w_up, w_down=w_down)


@jax.custom_vjp
def low(v):
    return lax.optimization_barrier(v.astype(jnp.bfloat16)).astype(jnp.float32)

@jax.custom_vjp
def low_back(v):
    return v

def low_keep(v):
    return (low(v), None)

def low_pass(kept, grad):
    return (grad,)

def back_keep(v):
    return (v, None)

def back_low(kept, grad):
    return (low(grad),)
low.defvjp(low_keep, low_pass)
low_back.defvjp(back_keep, back_low)
HIGHEST = lax.Precision.HIGHEST
EPSILON = 1e-05
THETA = 100000000000.0
LARGE_SLOTS = (1, 2, 3, 4, 12, 13, 14, 15, 16, 18, 19, 20)

def matmul_high(left, right):
    return jnp.dot(left, right, precision=HIGHEST)

def silu_value(values):
    return values * jax.nn.sigmoid(values)

def softplus_value(values):
    return jnp.log1p(jnp.exp(values))

def norm_round(values, gain):
    return low(values * lax.rsqrt(lax.optimization_barrier(jnp.mean(values * values, axis=-1, keepdims=True)) + EPSILON) * gain)

def rope_tables(length, width):
    position = jnp.arange(length).astype(jnp.float32)
    freqs = jnp.exp(-(jnp.arange(0, width, 2).astype(jnp.float32) / width) * math.log(THETA))
    angle = position[:, None] * freqs[None, :]
    angle = jnp.concatenate([angle, angle], axis=-1)
    return (jnp.cos(angle), jnp.sin(angle))

def rotary(values, cosine, sine):
    half = values.shape[-1] // 2
    turned = jnp.concatenate([-values[..., half:], values[..., :half]], axis=-1)
    return values * cosine[:, None, :] + turned * sine[:, None, :]

def doc_mask(seg):
    places = jnp.arange(seg.shape[0])
    return (places[:, None] >= places[None, :]) & (seg[:, None] == seg[None, :])

def causal_conv(values, taps, bias, seg):
    result = bias + taps[0] * values
    for offset in range(1, taps.shape[0]):
        shifted = jnp.concatenate([jnp.zeros((offset, values.shape[1]), values.dtype), values[:-offset]], axis=0)
        keep = jnp.concatenate([jnp.zeros((offset,), jnp.bool_), seg[offset:] == seg[:-offset]])
        result = result + taps[offset] * jnp.where(keep[:, None], shifted, 0.0)
    return result

def ssd_core(conv_inner, conv_pair, step, a_log, d_skip, seg):
    length, heads = step.shape
    state = conv_pair.shape[1] // 2
    input_b = low(conv_pair[:, :state])
    output_c = low(conv_pair[:, state:])
    intersection = low_back(matmul_high(output_c, input_b.T))
    decay_log = jnp.cumsum(step * -jnp.exp(a_log), axis=0).T
    mask = doc_mask(seg)
    decay = jnp.exp(jnp.where(mask[None], decay_log[:, :, None] - decay_log[:, None, :], -1e+30))
    mixing = low(intersection[None] * decay)
    inner_heads = conv_inner.reshape(length, heads, -1)
    driven = low(step[:, :, None] * inner_heads)
    scanned = jnp.einsum('hij,jhd->ihd', mixing, driven, precision=HIGHEST) + d_skip[None, :, None] * inner_heads
    return low_back(scanned).reshape(length, -1)

def attention_core(query_raw, key_raw, value_raw, kv_map, seg):
    length = query_raw.shape[0]
    cosine, sine = rope_tables(length, HD)
    query = low(rotary(query_raw.reshape(length, -1, HD), cosine, sine))
    key = low(rotary(key_raw.reshape(length, -1, HD), cosine, sine))
    value = low(value_raw).reshape(length, -1, HD)
    key_sel = jnp.einsum('lkd,hk->lhd', key, kv_map, precision=HIGHEST)
    value_sel = jnp.einsum('lkd,hk->lhd', value, kv_map, precision=HIGHEST)
    scores = low_back(jnp.einsum('qhd,khd->hqk', query, key_sel, precision=HIGHEST) * HD ** (-0.5))
    scores = jnp.where(doc_mask(seg)[None], scores, -1e+30)
    peak = lax.optimization_barrier(jnp.max(scores, axis=-1, keepdims=True))
    weights = jnp.exp(scores - peak)
    probs = low(weights / lax.optimization_barrier(jnp.sum(weights, axis=-1, keepdims=True)))
    attended = jnp.einsum('hqk,khd->qhd', probs, value_sel, precision=HIGHEST)
    return low(low_back(attended.reshape(length, -1)))

def mixer(normed, mamba_gate_weight, mamba_input_weight, w_dt, w_bc, w_q, w_k, w_v, w_o, mamba_output_weight, convolution_input_taps, convolution_input_bias, conv_bc, conv_bc_bias, dt_bias, a_log, d_skip, seg, kv_map):
    gate_z = low_back(matmul_high(normed, mamba_gate_weight))
    inner = low_back(matmul_high(normed, mamba_input_weight))
    pair = low_back(matmul_high(normed, w_bc))
    step_raw = low_back(matmul_high(normed, w_dt))
    conv_inner = silu_value(causal_conv(inner, convolution_input_taps, convolution_input_bias, seg))
    conv_pair = silu_value(causal_conv(pair, conv_bc, conv_bc_bias, seg))
    step = softplus_value(step_raw + dt_bias)
    scanned = ssd_core(conv_inner, conv_pair, step, a_log, d_skip, seg)
    gated = low(scanned * silu_value(gate_z))
    attended = attention_core(low_back(matmul_high(normed, w_q)), low_back(matmul_high(normed, w_k)), low_back(matmul_high(normed, w_v)), kv_map, seg)
    return matmul_high(gated, mamba_output_weight) + matmul_high(attended, w_o)

def feed_forward(normed, w_gate, w_up, w_down):
    gate = low_back(matmul_high(normed, w_gate))
    upward = low_back(matmul_high(normed, w_up))
    hidden = low(silu_value(gate) * upward)
    return matmul_high(hidden, w_down)

def layer(params, rows, seg, kv_map):
    gain_in, mamba_gate_weight, mamba_input_weight, w_dt, w_bc, convolution_input_taps, convolution_input_bias, conv_bc, conv_bc_bias, dt_bias, a_log, d_skip, w_q, w_k, w_v, w_o, mamba_output_weight, gain_ffn, w_gate, w_up, w_down = params
    normed = norm_round(rows, gain_in)
    mixed = mixer(normed, mamba_gate_weight, mamba_input_weight, w_dt, w_bc, w_q, w_k, w_v, w_o, mamba_output_weight, convolution_input_taps, convolution_input_bias, conv_bc, conv_bc_bias, dt_bias, a_log, d_skip, seg, kv_map)
    state = rows + low_back(mixed)
    return state + feed_forward(norm_round(state, gain_ffn), w_gate, w_up, w_down)

def reference(tokens, segments, cotangent, gain_in, mamba_gate_weight, mamba_input_weight, w_dt, w_bc, convolution_input_taps, convolution_input_bias, conv_bc, conv_bc_bias, dt_bias, a_log, d_skip, w_q, w_k, w_v, w_o, mamba_output_weight, gain_ffn, w_gate, w_up, w_down):
    count, length = segments.shape
    width = tokens.shape[1]
    kv_map = (jnp.arange(QHEADS)[:, None] // (QHEADS // KVHEADS) == jnp.arange(KVHEADS)[None, :]).astype(jnp.float32)
    params = (gain_in, mamba_gate_weight, mamba_input_weight, w_dt, w_bc, convolution_input_taps, convolution_input_bias, conv_bc, conv_bc_bias, dt_bias, a_log, d_skip, w_q, w_k, w_v, w_o, mamba_output_weight, gain_ffn, w_gate, w_up, w_down)
    rows = tokens.astype(jnp.float32).reshape(count, length, width)

    def forward(rows_in, params_in):
        fixed = tuple((low(value) if place in LARGE_SLOTS else value for place, value in enumerate(params_in)))

        def single(item):
            return layer(fixed, item[0], item[1], kv_map)
        return lax.map(jax.checkpoint(single), (rows_in, segments))
    result, pull = jax.vjp(forward, rows, params)
    grad_rows, grads = pull(cotangent.astype(jnp.float32).reshape(count, length, width))
    output = result.reshape(-1, width).astype(jnp.bfloat16)
    grad_tokens = grad_rows.reshape(-1, width).astype(jnp.bfloat16)
    return (output, grad_tokens, grads[0], grads[1], grads[2], grads[3], grads[4], grads[5], grads[6], grads[7], grads[8], grads[9], grads[10], grads[11], grads[12], grads[13], grads[14], grads[15], grads[16], grads[17], grads[18], grads[19], grads[20])
```

```python
import math

import jax
import jax.numpy as jnp
from jax import lax
from jax.experimental import pallas as pl
from jax.experimental.pallas import tpu as pltpu
from jax.sharding import PartitionSpec as P

QHEADS = 8
KVHEADS = 2
HD = 64
STATE = 128
CHUNK = 128
TAPS = 4
EPSILON = 1e-05
THETA = 100000000000.0
NEG = -1e30
HIGHEST = lax.Precision.HIGHEST
BF = jnp.bfloat16
F32 = jnp.float32
VMEM_LIMIT = 48 * 1024 * 1024


def dot(left, right, dims=((1,), (0,))):
    return lax.dot_general(left, right, (dims, ((), ())), preferred_element_type=F32)


def dot_exact(left, right):
    return lax.dot_general(
        left, right, (((1,), (0,)), ((), ())), precision=HIGHEST, preferred_element_type=F32
    )


def sigmoid(values):
    return 1.0 / (1.0 + jnp.exp(-values))


def pick(low_half, table, first):
    return jnp.where(low_half, table[:, first : first + 1], table[:, first + 1 : first + 2])


def halves(low_half, tile):
    zero = jnp.zeros_like(tile)
    return jnp.concatenate(
        [jnp.where(low_half, tile, zero), jnp.where(low_half, zero, tile)], axis=0
    )


def ssd_tables(dt_raw, dt_bias, rate, emask, fmask, total, lower):
    step = jnp.log1p(jnp.exp(dt_raw + dt_bias))
    decay = dot_exact(lower, step * rate)
    last = decay[CHUNK - 1 : CHUNK, :]
    enter = jnp.exp(decay) * emask
    leave = jnp.exp(last - decay) * fmask
    whole = jnp.exp(last) * total
    return step, decay, enter, leave, whole


def conv_rows(buf, width, aux, taps, bias):
    result = bias + taps[0:1] * buf[8 : 8 + CHUNK, width]
    for k in range(1, TAPS):
        result = result + taps[k : k + 1] * (aux[:, k : k + 1] * buf[8 - k : 8 - k + CHUNK, width])
    return result


def ssd_forward_kernel(
    h_ref, z_ref, aux_ref, segrow_ref, xpar_ref, bcpar_ref, hpar_ref,
    gated_ref, scan_ref, start_ref, xbuf, pbuf, state,
):
    inner = z_ref.shape[1]
    pairs = inner // 128
    lane = lax.broadcasted_iota(jnp.int32, (CHUNK, 128), 1)
    sub = lax.broadcasted_iota(jnp.int32, (CHUNK, 128), 0)
    low_half = lane < 64

    @pl.when(pl.program_id(0) == 0)
    def _():
        xbuf[0:8, :] = jnp.zeros((8, inner), F32)
        pbuf[0:8, :] = jnp.zeros((8, 2 * STATE), F32)
        state[...] = jnp.zeros_like(state)

    xbuf[8 : 8 + CHUNK, :] = h_ref[:, :inner]
    pbuf[8 : 8 + CHUNK, :] = h_ref[:, inner : inner + 2 * STATE]
    aux = aux_ref[...]
    pre_pair = conv_rows(pbuf, slice(None), aux, bcpar_ref[0:4, :], bcpar_ref[4:5, :])
    act_pair = pre_pair * sigmoid(pre_pair)
    in_b = act_pair[:, :STATE].astype(BF)
    out_c = act_pair[:, STATE:].astype(BF)
    inter = dot(out_c, in_b, ((1,), (1,)))
    allowed = (sub >= lane) & (aux[:, 0:1] == segrow_ref[0])
    hide = jnp.where(allowed, 0.0, NEG)
    lower = (sub >= lane).astype(F32)
    emask = aux[:, 7:8]
    step, decay, enter, leave, whole = ssd_tables(
        h_ref[:, inner + 2 * STATE :], hpar_ref[0:1, :], hpar_ref[1:2, :],
        emask, aux[:, 8:9], emask[CHUNK - 1 : CHUNK, :], lower,
    )
    decay_t = decay.T
    for p in range(pairs):
        cols = slice(128 * p, 128 * p + 128)
        pre = conv_rows(xbuf, cols, aux, xpar_ref[0:4, cols], xpar_ref[4:5, cols])
        act = pre * sigmoid(pre)
        driven = (pick(low_half, step, 2 * p) * act).astype(BF)
        mixes = []
        for head in (2 * p, 2 * p + 1):
            gap = decay[:, head : head + 1] - decay_t[head : head + 1, :]
            mixes.append((inter * jnp.exp(gap + hide)).astype(BF))
        before = state[:, cols]
        start = before.astype(BF)
        start_ref[:, cols] = start
        scanned = dot(jnp.concatenate(mixes, axis=1), halves(low_half, driven))
        scanned = scanned + dot(out_c, start) * pick(low_half, enter, 2 * p)
        scanned = scanned + xpar_ref[5:6, cols] * act
        scan_ref[:, cols] = scanned.astype(scan_ref.dtype)
        gate = z_ref[:, cols].astype(F32)
        gated_ref[:, cols] = (scanned * (gate * sigmoid(gate))).astype(BF)
        sent = (pick(low_half, leave, 2 * p) * driven.astype(F32)).astype(BF)
        state[:, cols] = pick(low_half[0:1], whole, 2 * p) * before + dot(
            in_b, sent, ((0,), (0,))
        )
    xbuf[0:8, :] = xbuf[CHUNK : CHUNK + 8, :]
    pbuf[0:8, :] = pbuf[CHUNK : CHUNK + 8, :]


def ssd_forward(h1, z, aux, segrow, xpar, bcpar, hpar):
    length, inner = z.shape
    chunks = length // CHUNK
    width = h1.shape[1]
    whole = lambda arr: pl.BlockSpec(arr.shape, lambda c: (0,) * arr.ndim)
    rows = lambda cols: pl.BlockSpec((CHUNK, cols), lambda c: (c, 0))
    return pl.pallas_call(
        ssd_forward_kernel,
        grid=(chunks,),
        in_specs=[
            rows(width), rows(inner), rows(128),
            pl.BlockSpec((1, 1, CHUNK), lambda c: (c, 0, 0)),
            whole(xpar), whole(bcpar), whole(hpar),
        ],
        out_specs=[rows(inner), rows(inner), rows(inner)],
        out_shape=[
            jax.ShapeDtypeStruct((length, inner), BF),
            jax.ShapeDtypeStruct((length, inner), F32),
            jax.ShapeDtypeStruct((chunks * STATE, inner), BF),
        ],
        scratch_shapes=[
            pltpu.VMEM((CHUNK + 8, inner), F32),
            pltpu.VMEM((CHUNK + 8, 2 * STATE), F32),
            pltpu.VMEM((STATE, inner), F32),
        ],
        compiler_params=pltpu.CompilerParams(vmem_limit_bytes=VMEM_LIMIT),
        name="ssd_forward",
    )(h1, z, aux, segrow, xpar, bcpar, hpar)


def head_sums(low_half, tile):
    zero = jnp.zeros_like(tile)
    return (
        jnp.sum(jnp.where(low_half, tile, zero), axis=1, keepdims=True),
        jnp.sum(jnp.where(low_half, zero, tile), axis=1, keepdims=True),
    )


def ssd_backward_kernel(
    h_ref, prev_ref, z_ref, scan_ref, dgated_ref, start_ref, aux_ref, segrow_ref,
    xpar_ref, bcpar_ref, hpar_ref,
    dh_ref, dz_ref, xacc_ref, bcacc_ref, hacc_ref, xbuf, pbuf, dxbuf, dpbuf, dstate,
):
    inner = z_ref.shape[1]
    pairs = inner // 128
    lane = lax.broadcasted_iota(jnp.int32, (CHUNK, 128), 1)
    sub = lax.broadcasted_iota(jnp.int32, (CHUNK, 128), 0)
    low_half = lane < 64
    low_row = low_half[0:1]

    @pl.when(pl.program_id(0) == 0)
    def _():
        dxbuf[CHUNK : CHUNK + 8, :] = jnp.zeros((8, inner), F32)
        dpbuf[CHUNK : CHUNK + 8, :] = jnp.zeros((8, 2 * STATE), F32)
        dstate[...] = jnp.zeros_like(dstate)
        xacc_ref[...] = jnp.zeros_like(xacc_ref)
        bcacc_ref[...] = jnp.zeros_like(bcacc_ref)
        hacc_ref[...] = jnp.zeros_like(hacc_ref)

    xbuf[0:8, :] = prev_ref[:, :inner]
    xbuf[8 : 8 + CHUNK, :] = h_ref[:, :inner]
    pbuf[0:8, :] = prev_ref[:, inner : inner + 2 * STATE]
    pbuf[8 : 8 + CHUNK, :] = h_ref[:, inner : inner + 2 * STATE]
    aux = aux_ref[...]
    pre_pair = conv_rows(pbuf, slice(None), aux, bcpar_ref[0:4, :], bcpar_ref[4:5, :])
    sig_pair = sigmoid(pre_pair)
    act_pair = pre_pair * sig_pair
    in_b = act_pair[:, :STATE].astype(BF)
    out_c = act_pair[:, STATE:].astype(BF)
    inter_t = dot(in_b, out_c, ((1,), (1,)))
    allowed_t = (lane >= sub) & (aux[:, 0:1] == segrow_ref[0])
    hide_t = jnp.where(allowed_t, 0.0, NEG)
    lower = (sub >= lane).astype(F32)
    upper = (sub <= lane).astype(F32)
    strict = (sub > lane).astype(F32)
    emask = aux[:, 7:8]
    rate = hpar_ref[1:2, :]
    dt_full = h_ref[:, inner + 2 * STATE :] + hpar_ref[0:1, :]
    step, decay, enter, leave, whole = ssd_tables(
        h_ref[:, inner + 2 * STATE :], hpar_ref[0:1, :], rate,
        emask, aux[:, 8:9], emask[CHUNK - 1 : CHUNK, :], lower,
    )
    decay_t = decay.T
    zeros = jnp.zeros((CHUNK, 128), F32)
    grad_inter_t = zeros
    grad_b = zeros
    grad_c = zeros
    col_intra = zeros
    row_inter = zeros
    direct = zeros
    direct_inter = zeros
    across = jnp.zeros((1, 128), F32)
    row_list = []
    for p in range(pairs):
        cols = slice(128 * p, 128 * p + 128)
        pre = conv_rows(xbuf, cols, aux, xpar_ref[0:4, cols], xpar_ref[4:5, cols])
        sig = sigmoid(pre)
        act = pre * sig
        gate = z_ref[:, cols].astype(F32)
        sig_gate = sigmoid(gate)
        dgated = dgated_ref[:, cols]
        scanned = scan_ref[:, cols]
        dz_ref[:, cols] = (
            dgated * scanned * (sig_gate * (1.0 + gate * (1.0 - sig_gate)))
        ).astype(BF)
        dscan = (dgated * (gate * sig_gate)).astype(BF)
        dscan_f = dscan.astype(F32)
        step_p = pick(low_half, step, 2 * p)
        driven = (step_p * act).astype(BF)
        zero_b = jnp.zeros_like(driven)
        mixes = []
        for head in (2 * p, 2 * p + 1):
            gap = decay_t[head : head + 1, :] - decay[:, head : head + 1]
            damp = jnp.exp(gap + hide_t)
            mixed = inter_t * damp
            mixes.append(mixed.astype(BF))
            own = jnp.where(low_half == (head % 2 == 0), driven, zero_b)
            grad_mix = dot(own, dscan, ((1,), (1,)))
            grad_inter_t = grad_inter_t + grad_mix * damp
            flow = grad_mix * mixed
            row_list.append(jnp.sum(flow, axis=0, keepdims=True))
            col_intra = jnp.where(lane == head, jnp.sum(flow, axis=1, keepdims=True), col_intra)
        start = start_ref[:, cols]
        dst = dstate[:, cols]
        dst_b = dst.astype(BF)
        enter_p = pick(low_half, enter, 2 * p)
        leave_p = pick(low_half, leave, 2 * p)
        whole_p = pick(low_row, whole, 2 * p)
        from_inter = dot(in_b, dst_b) * leave_p
        ddriven = dot(jnp.concatenate(mixes, axis=1), halves(low_half, dscan)) + from_inter
        dact = xpar_ref[5:6, cols] * dscan_f + step_p * ddriven
        came = dot(out_c, start) * enter_p
        sums = (
            head_sums(low_half, act * ddriven),
            head_sums(low_half, act * from_inter),
            head_sums(low_half, dscan_f * came),
            head_sums(low_row, whole_p * jnp.sum(dst * start.astype(F32), axis=0, keepdims=True)),
        )
        for side in (0, 1):
            here = lane == 2 * p + side
            direct = jnp.where(here, sums[0][side], direct)
            direct_inter = jnp.where(here, sums[1][side], direct_inter)
            row_inter = jnp.where(here, sums[2][side], row_inter)
            across = jnp.where(here[0:1], sums[3][side], across)
        dcame = (enter_p * dscan_f).astype(BF)
        sent = (leave_p * driven.astype(F32)).astype(BF)
        grad_c = grad_c + dot(dcame, start, ((1,), (1,)))
        grad_b = grad_b + dot(sent, dst_b, ((1,), (1,)))
        dstate[:, cols] = whole_p * dst + dot(out_c, dcame, ((0,), (0,)))
        dpre = dact * (sig * (1.0 + pre * (1.0 - sig)))
        dxbuf[0:CHUNK, cols] = dpre
        dval = xpar_ref[0:1, cols] * dpre
        xacc_ref[0:1, cols] += jnp.sum(dpre * xbuf[8 : 8 + CHUNK, cols], axis=0, keepdims=True)
        for k in range(1, TAPS):
            dval = dval + xpar_ref[k : k + 1, cols] * (
                aux[:, 3 + k : 4 + k] * dxbuf[k : k + CHUNK, cols]
            )
            xacc_ref[k : k + 1, cols] += jnp.sum(
                dpre * (aux[:, k : k + 1] * xbuf[8 - k : 8 - k + CHUNK, cols]),
                axis=0, keepdims=True,
            )
        xacc_ref[4:5, cols] += jnp.sum(dpre, axis=0, keepdims=True)
        xacc_ref[5:6, cols] += jnp.sum(dscan_f * act, axis=0, keepdims=True)
        dh_ref[:, cols] = dval.astype(BF)
    dxbuf[CHUNK : CHUNK + 8, :] = dxbuf[0:8, :]
    grad_inter_b = grad_inter_t.astype(BF)
    grad_b = grad_b + dot(grad_inter_b, out_c)
    grad_c = grad_c + dot(grad_inter_b, in_b, ((0,), (0,)))
    grad_act = jnp.concatenate([grad_b, grad_c], axis=1)
    dpre = grad_act * (sig_pair * (1.0 + pre_pair * (1.0 - sig_pair)))
    dpbuf[0:CHUNK, :] = dpre
    dval = bcpar_ref[0:1, :] * dpre
    bcacc_ref[0:1, :] += jnp.sum(dpre * pbuf[8 : 8 + CHUNK, :], axis=0, keepdims=True)
    for k in range(1, TAPS):
        dval = dval + bcpar_ref[k : k + 1, :] * (
            aux[:, 3 + k : 4 + k] * dpbuf[k : k + CHUNK, :]
        )
        bcacc_ref[k : k + 1, :] += jnp.sum(
            dpre * (aux[:, k : k + 1] * pbuf[8 - k : 8 - k + CHUNK, :]), axis=0, keepdims=True
        )
    bcacc_ref[4:5, :] += jnp.sum(dpre, axis=0, keepdims=True)
    dh_ref[:, inner : inner + 2 * STATE] = dval.astype(BF)
    dpbuf[CHUNK : CHUNK + 8, :] = dpbuf[0:8, :]
    rows = jnp.concatenate(row_list + [jnp.zeros((CHUNK - 2 * pairs, 128), F32)], axis=0).T
    grad_decay = dot_exact(upper, rows - col_intra + row_inter) + across
    grad_decay = grad_decay + dot_exact(strict, step * direct_inter)
    dstep = direct + grad_decay * rate
    draw = dstep * sigmoid(dt_full)
    hacc_ref[0:1, :] += jnp.sum(draw, axis=0, keepdims=True)
    hacc_ref[1:2, :] += jnp.sum(grad_decay * step, axis=0, keepdims=True) * rate
    dh_ref[:, inner + 2 * STATE :] = draw.astype(BF)


def ssd_backward(h1, z, scan, dgated, start, aux, segrow, xpar, bcpar, hpar):
    length, inner = z.shape
    chunks = length // CHUNK
    width = h1.shape[1]
    whole = lambda arr: pl.BlockSpec(arr.shape, lambda c: (0,) * arr.ndim)
    rows = lambda cols: pl.BlockSpec((CHUNK, cols), lambda c: (chunks - 1 - c, 0))
    fixed = lambda r, cols: pl.BlockSpec((r, cols), lambda c: (0, 0))
    return pl.pallas_call(
        ssd_backward_kernel,
        grid=(chunks,),
        in_specs=[
            rows(width),
            pl.BlockSpec((8, width), lambda c: (jnp.maximum((chunks - 1 - c) * (CHUNK // 8) - 1, 0), 0)),
            rows(inner), rows(inner), rows(inner), rows(inner), rows(128),
            pl.BlockSpec((1, 1, CHUNK), lambda c: (chunks - 1 - c, 0, 0)),
            whole(xpar), whole(bcpar), whole(hpar),
        ],
        out_specs=[
            rows(width), rows(inner),
            fixed(8, inner), fixed(8, 2 * STATE), fixed(8, 128),
        ],
        out_shape=[
            jax.ShapeDtypeStruct((length, width), BF),
            jax.ShapeDtypeStruct((length, inner), BF),
            jax.ShapeDtypeStruct((8, inner), F32),
            jax.ShapeDtypeStruct((8, 2 * STATE), F32),
            jax.ShapeDtypeStruct((8, 128), F32),
        ],
        scratch_shapes=[
            pltpu.VMEM((CHUNK + 8, inner), F32),
            pltpu.VMEM((CHUNK + 8, 2 * STATE), F32),
            pltpu.VMEM((CHUNK + 8, inner), F32),
            pltpu.VMEM((CHUNK + 8, 2 * STATE), F32),
            pltpu.VMEM((STATE, inner), F32),
        ],
        compiler_params=pltpu.CompilerParams(vmem_limit_bytes=VMEM_LIMIT),
        name="ssd_backward",
    )(h1, h1, z, scan, dgated, start, aux, segrow, xpar, bcpar, hpar)


def segment_tables(seg):
    length = seg.shape[0]
    chunks = length // CHUNK
    value = seg.astype(F32)
    far = jnp.full((TAPS,), -1.0, F32)
    cols = [value]
    for k in range(1, TAPS):
        cols.append((value == jnp.concatenate([far[:k], value[:-k]])).astype(F32))
    for k in range(1, TAPS):
        cols.append((value == jnp.concatenate([value[k:], far[:k]])).astype(F32))
    by_chunk = value.reshape(chunks, CHUNK)
    ends = by_chunk[:, -1:]
    before = jnp.concatenate([far[:1, None], ends[:-1]], axis=0)
    cols.append((by_chunk == before).astype(F32).reshape(-1))
    cols.append((by_chunk == ends).astype(F32).reshape(-1))
    aux = jnp.stack(cols, axis=1)
    return jnp.pad(aux, ((0, 0), (0, 128 - aux.shape[1]))), by_chunk[:, None, :]


BLOCK = 256
REACH = 512


def rope_tables(length):
    position = jnp.arange(length).astype(F32)
    freqs = jnp.exp(-(jnp.arange(0, HD, 2).astype(F32) / HD) * math.log(THETA))
    angle = position[:, None] * freqs[None, :]
    cosine, sine = jnp.cos(angle), jnp.sin(angle)
    return (
        jnp.concatenate([cosine] * 4, axis=1),
        jnp.concatenate([-sine, sine, -sine, sine], axis=1),
    )


def turn(values, cosine, sine):
    lane = lax.broadcasted_iota(jnp.int32, values.shape, 1)
    swapped = jnp.where(
        lane % HD < HD // 2, pltpu.roll(values, 128 - HD // 2, 1), pltpu.roll(values, HD // 2, 1)
    )
    return values * cosine + swapped * sine


def attention_forward_kernel(
    qkv_ref, cos_ref, sin_ref, segcol_ref, segrow_ref, out_ref, turned_ref, lse_ref
):
    length = qkv_ref.shape[0]
    groups = KVHEADS
    cosine, sine = cos_ref[...], sin_ref[...]
    for t in range(groups + 1):
        cols = slice(128 * t, 128 * t + 128)
        turned_ref[:, cols] = turn(qkv_ref[:, cols].astype(F32), cosine, sine).astype(BF)
    key_at, value_at = 128 * groups, 128 * (groups + 1)
    lane = lax.broadcasted_iota(jnp.int32, (BLOCK, 128), 1)
    for b in range(length // BLOCK):
        rows = slice(b * BLOCK, (b + 1) * BLOCK)
        first = max(0, b * BLOCK - REACH)
        keys = slice(first, (b + 1) * BLOCK)
        many = (b + 1) * BLOCK - first
        at_row = lax.broadcasted_iota(jnp.int32, (BLOCK, many), 0) + b * BLOCK
        at_col = lax.broadcasted_iota(jnp.int32, (BLOCK, many), 1) + first
        allowed = (at_row >= at_col) & (segcol_ref[rows, 0:1] == segrow_ref[:, keys])
        lse = jnp.zeros((BLOCK, 128), F32)
        for g in range(groups):
            key = turned_ref[keys, key_at + 64 * g : key_at + 64 * g + 64]
            value = qkv_ref[keys, value_at + 64 * g : value_at + 64 * g + 64]
            parts = []
            for s in range(2):
                query = turned_ref[rows, 128 * g + 64 * s : 128 * g + 64 * s + 64]
                scores = dot(query, key, ((1,), (1,))) * HD ** (-0.5)
                scores = jnp.where(allowed, scores, NEG)
                peak = jnp.max(scores, axis=1, keepdims=True)
                weights = jnp.exp(scores - peak)
                total = jnp.sum(weights, axis=1, keepdims=True)
                probs = (weights * (1.0 / total)).astype(BF)
                parts.append(dot(probs, value))
                lse = jnp.where(lane == 2 * g + s, peak + jnp.log(total), lse)
            out_ref[rows, 128 * g : 128 * g + 128] = jnp.concatenate(parts, axis=1).astype(BF)
        lse_ref[rows, :] = lse


def attention_forward(qkv, cosine, sine, aux, segrow):
    length = qkv.shape[0]
    return pl.pallas_call(
        attention_forward_kernel,
        out_shape=[
            jax.ShapeDtypeStruct((length, 128 * KVHEADS), BF),
            jax.ShapeDtypeStruct((length, 128 * (KVHEADS + 1)), BF),
            jax.ShapeDtypeStruct((length, 128), F32),
        ],
        compiler_params=pltpu.CompilerParams(vmem_limit_bytes=VMEM_LIMIT),
        name="attention_forward",
    )(qkv, cosine, sine, aux, segrow)


def attention_backward_kernel(
    qkv_ref, turned_ref, datt_ref, lse_ref, delta_ref, cos_ref, sin_ref, segcol_ref, segrow_ref,
    dqkv_ref, dkey, dvalue,
):
    length = qkv_ref.shape[0]
    groups = KVHEADS
    key_at, value_at = 128 * groups, 128 * (groups + 1)
    dkey[...] = jnp.zeros_like(dkey)
    dvalue[...] = jnp.zeros_like(dvalue)
    for b in range(length // BLOCK):
        rows = slice(b * BLOCK, (b + 1) * BLOCK)
        first = max(0, b * BLOCK - REACH)
        keys = slice(first, (b + 1) * BLOCK)
        many = (b + 1) * BLOCK - first
        at_key = lax.broadcasted_iota(jnp.int32, (many, BLOCK), 0) + first
        at_row = lax.broadcasted_iota(jnp.int32, (many, BLOCK), 1) + b * BLOCK
        allowed = (at_row >= at_key) & (segcol_ref[keys, 0:1] == segrow_ref[:, rows])
        dquery = []
        for g in range(groups):
            key = turned_ref[keys, key_at + 64 * g : key_at + 64 * g + 64]
            value = qkv_ref[keys, value_at + 64 * g : value_at + 64 * g + 64]
            dk = jnp.zeros((many, HD), F32)
            dv = jnp.zeros((many, HD), F32)
            for s in range(2):
                head = 2 * g + s
                half = slice(128 * g + 64 * s, 128 * g + 64 * s + 64)
                query = turned_ref[rows, half]
                datt = datt_ref[rows, half]
                scores = dot(key, query, ((1,), (1,))) * HD ** (-0.5)
                probs = jnp.exp(jnp.where(allowed, scores, NEG) - lse_ref[head : head + 1, rows])
                dprobs = dot(value, datt, ((1,), (1,)))
                dscores = (probs * (dprobs - delta_ref[head : head + 1, rows])).astype(BF)
                dk = dk + dot(dscores, query)
                dv = dv + dot(probs.astype(BF), datt)
                dquery.append(dot(dscores, key, ((0,), (0,))) * HD ** (-0.5))
            dkey[keys, 64 * g : 64 * g + 64] += dk * HD ** (-0.5)
            dvalue[keys, 64 * g : 64 * g + 64] += dv
        for g in range(groups):
            tile = jnp.concatenate([dquery[2 * g], dquery[2 * g + 1]], axis=1)
            dqkv_ref[rows, 128 * g : 128 * g + 128] = turn(
                tile, cos_ref[rows, :], -sin_ref[rows, :]
            ).astype(BF)
    dqkv_ref[:, key_at : key_at + 128] = turn(dkey[...], cos_ref[...], -sin_ref[...]).astype(BF)
    dqkv_ref[:, value_at : value_at + 128] = dvalue[...].astype(BF)


def attention_backward(qkv, turned, datt, lse, delta, cosine, sine, aux, segrow):
    length = qkv.shape[0]
    return pl.pallas_call(
        attention_backward_kernel,
        out_shape=jax.ShapeDtypeStruct(qkv.shape, BF),
        scratch_shapes=[pltpu.VMEM((length, 128), F32), pltpu.VMEM((length, 128), F32)],
        compiler_params=pltpu.CompilerParams(vmem_limit_bytes=VMEM_LIMIT),
        name="attention_backward",
    )(qkv, turned, datt, lse, delta, cosine, sine, aux, segrow)


def core_swap(value):
    return lax.ppermute(value, "head", [(0, 1), (1, 0), (2, 3), (3, 2)])


def half_swap(value):
    return lax.ppermute(value, "head", [(0, 2), (2, 0), (1, 3), (3, 1)])


def half_groups(dp):
    return [[d * 4 + 2 * half + core for d in range(dp) for half in range(2)] for core in range(2)]


def ordered(is_first, mine, other, axis):
    return jnp.where(
        is_first,
        jnp.concatenate([mine, other], axis=axis),
        jnp.concatenate([other, mine], axis=axis),
    )


def gather(piece, dp, is_first):
    rows, cols = piece.shape
    both = lax.all_gather(
        piece, ("dp", "head"), axis=0, tiled=False, axis_index_groups=half_groups(dp)
    ).reshape(dp, 2, rows, cols)
    zero, one = both[:, 0], both[:, 1]
    mine = jnp.where(is_first, zero, one).reshape(dp * rows, cols)
    other = jnp.where(is_first, one, zero).reshape(dp * rows, cols)
    return mine, other


def scatter_sum(mine, other, dp, is_first):
    cols = mine.shape[1]
    rows = mine.shape[0] // dp
    mine = mine.astype(BF).reshape(dp, 1, rows, cols)
    other = other.astype(BF).reshape(dp, 1, rows, cols)
    both = ordered(is_first, mine, other, 1).reshape(dp * 2 * rows, cols)
    return lax.psum_scatter(
        both, ("dp", "head"), scatter_dimension=0, tiled=True, axis_index_groups=half_groups(dp)
    )


def core_sum(part):
    part = part.astype(BF)
    return part.astype(F32) + core_swap(part).astype(F32)


def wide(mine, other, width):
    return jnp.concatenate([mine[:, :width], other[:, :width]], axis=1)


def norm_back(grad, values, scale, gain):
    weighted = grad * gain
    inner = jnp.mean(weighted * values, axis=-1, keepdims=True)
    return scale * weighted - values * (scale * scale * scale * inner), jnp.sum(
        grad * (values * scale), axis=0
    )


def body(
    tokens, segments, cotangent, gain_in, mamba_gate_weight, mamba_input_weight, w_dt, w_bc,
    convolution_input_taps, convolution_input_bias, conv_bc, conv_bc_bias, dt_bias, a_log, d_skip,
    w_q, w_k, w_v, w_o, mamba_output_weight, gain_ffn, w_gate, w_up, w_down,
):
    length = segments.shape[1]
    width = tokens.shape[1]
    rows_here = mamba_gate_weight.shape[0]
    dp = width // rows_here
    inner = mamba_gate_weight.shape[1]
    heads = w_dt.shape[1]
    qcols = w_q.shape[1]
    hidden_cols = w_gate.shape[1]
    slot = lax.axis_index("head")
    half = slot // 2
    core = slot % 2
    is_first = half == 0
    seg = lax.dynamic_index_in_dim(segments, half, 0, keepdims=False)
    rows = lax.dynamic_slice_in_dim(tokens, half * length, length, 0).astype(F32)
    upstream = lax.dynamic_slice_in_dim(cotangent, half * length, length, 0)

    shared = jnp.concatenate([w_bc, w_k, w_v], axis=1).astype(BF)
    quarter = lax.dynamic_slice_in_dim(shared, slot * 128, 128, 1)
    short = lambda value: value.astype(BF)
    pad_dt = jnp.zeros((rows_here, 128 - heads), BF)
    piece1 = jnp.concatenate([short(mamba_input_weight), short(w_dt), pad_dt, quarter], axis=1)
    piece2 = jnp.concatenate([short(mamba_gate_weight), short(w_q)], axis=1)
    piece3 = jnp.concatenate([short(mamba_output_weight).T, short(w_o).T], axis=1)
    piece4 = jnp.concatenate([short(w_gate), short(w_up)], axis=1)
    piece5 = short(w_down).T
    full1 = gather(piece1, dp, is_first)
    full2 = gather(piece2, dp, is_first)
    full3 = gather(piece3, dp, is_first)
    full4 = gather(piece4, dp, is_first)
    full5 = gather(piece5, dp, is_first)

    at = inner + 128
    quarters = jnp.concatenate(
        [jnp.where(is_first, full1[0][:, at:], full1[1][:, at:]),
         jnp.where(is_first, full1[1][:, at:], full1[0][:, at:])], axis=1)
    others = core_swap(quarters)
    first_core = core == 0
    bc_full = jnp.concatenate(
        [jnp.where(first_core, quarters[:, :128], others[:, :128]),
         jnp.where(first_core, others[:, :128], quarters[:, :128])], axis=1)
    flip = lambda tile: jnp.where(is_first, tile, jnp.concatenate([tile[:, HD:], tile[:, :HD]], axis=1))
    key_full = flip(jnp.where(first_core, quarters[:, 128:], others[:, 128:]))
    value_full = flip(jnp.where(first_core, others[:, 128:], quarters[:, 128:]))
    dt_full = jnp.concatenate(
        [full1[0][:, inner : inner + heads], full1[1][:, inner : inner + heads],
         jnp.zeros((width, 128 - 2 * heads), BF)], axis=1)
    weight1 = jnp.concatenate([wide(*full1, inner), bc_full, dt_full], axis=1)
    weight_z = wide(*full2, inner)
    weight_qkv = jnp.concatenate([full2[0][:, inner:], full2[1][:, inner:], key_full, value_full], axis=1)
    weight_out = wide(*full3, inner)
    weight_o = jnp.concatenate([full3[0][:, inner:], full3[1][:, inner:]], axis=1)
    weight_gate = wide(*full4, hidden_cols)
    weight_up = jnp.concatenate([full4[0][:, hidden_cols:], full4[1][:, hidden_cols:]], axis=1)
    weight_down = jnp.concatenate(full5, axis=1)

    per_head = jnp.pad(jnp.stack([dt_bias, a_log, d_skip]), ((0, 5), (0, 128 - heads)))
    small = jnp.concatenate(
        [jnp.concatenate([convolution_input_taps, convolution_input_bias[None],
                          jnp.repeat(d_skip, HD)[None], jnp.zeros((2, inner), F32)], axis=0), per_head],
        axis=1)
    small_other = half_swap(small)
    xpar = jnp.concatenate([small[:, :inner], small_other[:, :inner]], axis=1)
    head_par = jnp.concatenate(
        [small[:2, inner : inner + heads], small_other[:2, inner : inner + heads],
         jnp.zeros((2, 128 - 2 * heads), F32)], axis=1)
    lane = jnp.arange(128) < 2 * heads
    hpar = jnp.concatenate(
        [head_par[:1], jnp.where(lane, -jnp.exp(head_par[1:]), 0.0), jnp.zeros((6, 128), F32)], axis=0)
    bcpar = jnp.concatenate([conv_bc, conv_bc_bias[None], jnp.zeros((3, conv_bc.shape[1]), F32)], axis=0)
    aux, segrow = segment_tables(seg)
    seg_line = aux[:, 0][None]
    cosine, sine = rope_tables(length)

    scale = lax.rsqrt(jnp.mean(rows * rows, axis=-1, keepdims=True) + EPSILON)
    normed = short(rows * scale * gain_in)
    h1 = dot(normed, weight1)
    z = short(dot(normed, weight_z))
    qkv = short(dot(normed, weight_qkv))
    gated, scan, start = ssd_forward(h1, z, aux, segrow, xpar, bcpar, hpar)
    attended, turned, lse = attention_forward(qkv, cosine, sine, aux, seg_line)
    mixed = dot(gated, weight_out, ((1,), (1,))) + dot(attended, weight_o, ((1,), (1,)))
    state = rows + core_sum(mixed)
    scale_ffn = lax.rsqrt(jnp.mean(state * state, axis=-1, keepdims=True) + EPSILON)
    normed_ffn = short(state * scale_ffn * gain_ffn)
    gate = dot(normed_ffn, weight_gate)
    up = dot(normed_ffn, weight_up)
    sig = jax.nn.sigmoid(gate)
    hidden = short(gate * sig * up)
    whole = core_sum(dot(hidden, weight_down, ((1,), (1,))))
    out_mine = short(state + whole)

    dhidden = dot(upstream, weight_down)
    dgate = short(dhidden * up * (sig * (1.0 + gate * (1.0 - sig))))
    dup = short(dhidden * (gate * sig))
    dnormed_ffn = core_sum(
        dot(dgate, weight_gate, ((1,), (1,))) + dot(dup, weight_up, ((1,), (1,))))
    cols = ((0,), (0,))
    grad_down = short(dot(upstream, hidden, cols))
    grad_gate = short(dot(normed_ffn, dgate, cols))
    grad_up = short(dot(normed_ffn, dup, cols))
    dstate_norm, grad_gain_ffn = norm_back(dnormed_ffn, state, scale_ffn, gain_ffn)
    dstate = upstream.astype(F32) + dstate_norm
    dmixed = short(dstate)

    split = lambda grad, size: (grad[:, :size], grad[:, size:])
    sent5 = scatter_sum(*split(grad_down, hidden_cols), dp, is_first)
    gate_m, gate_o = split(grad_gate, hidden_cols)
    up_m, up_o = split(grad_up, hidden_cols)
    sent4 = scatter_sum(
        jnp.concatenate([gate_m, up_m], axis=1), jnp.concatenate([gate_o, up_o], axis=1), dp, is_first)

    dgated = dot(dmixed, weight_out)
    datt = short(dot(dmixed, weight_o))
    grad_out = short(dot(dmixed, gated, cols))
    grad_o = short(dot(dmixed, attended, cols))
    out_m, out_o = split(grad_out, inner)
    o_m, o_o = split(grad_o, qcols)
    sent3 = scatter_sum(
        jnp.concatenate([out_m, o_m], axis=1), jnp.concatenate([out_o, o_o], axis=1), dp, is_first)
    delta = jnp.sum(
        (datt.astype(F32) * attended.astype(F32)).reshape(length, -1, HD), axis=-1).T
    delta = jnp.pad(delta, ((0, 8 - delta.shape[0]), (0, 0)))
    dqkv = attention_backward(
        qkv, turned, datt, lse[:, :8].T, delta, cosine, sine, aux, seg_line)
    dh1, dz, xacc, bcacc, hacc = ssd_backward(
        h1, z, scan, dgated, start, aux, segrow, xpar, bcpar, hpar)
    dnormed = core_sum(
        dot(dh1, weight1, ((1,), (1,)))
        + dot(dz, weight_z, ((1,), (1,)))
        + dot(dqkv, weight_qkv, ((1,), (1,))))
    grad1 = short(dot(normed, dh1, cols))
    grad_z = short(dot(normed, dz, cols))
    grad_qkv = short(dot(normed, dqkv, cols))
    drows, grad_gain_in = norm_back(dnormed, rows, scale, gain_in)
    grad_mine = short(dstate + drows)

    unflip = flip
    shared_grad = jnp.concatenate(
        [grad1[:, 2 * inner : 2 * inner + 2 * STATE],
         unflip(grad_qkv[:, 2 * qcols : 2 * qcols + 128]), unflip(grad_qkv[:, 2 * qcols + 128 :])], axis=1)
    quarter_rows = rows_here // 4
    by_slot = shared_grad.reshape(dp, 2, 2, quarter_rows, shared_grad.shape[1])
    to_keep = jnp.where(first_core, by_slot[:, :, 0], by_slot[:, :, 1])
    to_send = jnp.where(first_core, by_slot[:, :, 1], by_slot[:, :, 0])
    kept = short(to_keep.astype(F32) + core_swap(to_send).astype(F32))
    kept = kept.reshape(dp, 2, quarter_rows, 4, 128).swapaxes(2, 3).reshape(dp, 2, rows_here, 128)
    shared_m = jnp.where(is_first, kept[:, 0], kept[:, 1]).reshape(width, 128)
    shared_o = jnp.where(is_first, kept[:, 1], kept[:, 0]).reshape(width, 128)
    gains = jnp.stack([grad_gain_in, grad_gain_ffn], axis=1)
    dt_at = 2 * inner + 2 * STATE
    fill = jnp.zeros((width, 128 - heads - 2), BF)
    extra = lambda cols_dt: jnp.concatenate([cols_dt, short(gains), fill], axis=1)
    sent1 = scatter_sum(
        jnp.concatenate(
            [grad1[:, :inner], extra(grad1[:, dt_at : dt_at + heads]), shared_m], axis=1),
        jnp.concatenate(
            [grad1[:, inner : 2 * inner], extra(grad1[:, dt_at + heads : dt_at + 2 * heads]), shared_o],
            axis=1),
        dp, is_first)
    z_m, z_o = split(grad_z, inner)
    sent2 = scatter_sum(
        jnp.concatenate([z_m, grad_qkv[:, :qcols]], axis=1),
        jnp.concatenate([z_o, grad_qkv[:, qcols : 2 * qcols]], axis=1), dp, is_first)

    skip = xacc[5].reshape(2, heads, HD).sum(axis=-1)
    stretches = []
    for side in range(2):
        stretches.append(jnp.concatenate([
            xacc[:5, side * inner : (side + 1) * inner].reshape(-1),
            hacc[0, side * heads : (side + 1) * heads], hacc[1, side * heads : (side + 1) * heads],
            skip[side]]))
    stretch = stretches[0].shape[0]
    table = jnp.where(
        jnp.arange(4)[:, None] == slot, stretches[0][None],
        jnp.where(jnp.arange(4)[:, None] == (slot + 2) % 4, stretches[1][None], 0.0))
    vector = lax.psum(jnp.concatenate([table.reshape(-1), bcacc[:5].reshape(-1)]), ("dp", "head"))
    own = lax.dynamic_slice_in_dim(vector, slot * stretch, stretch, 0)
    taps = own[: 5 * inner].reshape(5, inner)
    per = own[5 * inner :].reshape(3, heads)
    place = lax.axis_index("dp") * 4 + slot
    bc_cols = conv_bc.shape[1] // (4 * dp)
    bc_own = lax.dynamic_slice_in_dim(
        vector[4 * stretch :].reshape(5, -1), place * bc_cols, bc_cols, 1)

    swap_out = half_swap(out_mine)
    swap_grad = half_swap(grad_mine)
    output = ordered(is_first, out_mine, swap_out, 0)
    grad_tokens = ordered(is_first, grad_mine, swap_grad, 0)

    sent1, sent2, sent3, sent4, sent5 = [v.astype(F32) for v in (sent1, sent2, sent3, sent4, sent5)]
    shared_own = sent1[:, inner + 128 :].reshape(4, quarter_rows, 128).swapaxes(0, 1).reshape(quarter_rows, -1)
    return (
        output,
        grad_tokens,
        sent1[:, inner + heads],
        sent2[:, :inner],
        sent1[:, :inner],
        sent1[:, inner : inner + heads],
        shared_own[:, : 2 * STATE],
        taps[:4],
        taps[4],
        bc_own[:4],
        bc_own[4],
        per[0],
        per[1],
        per[2],
        sent2[:, inner:],
        shared_own[:, 2 * STATE : 2 * STATE + 128],
        shared_own[:, 2 * STATE + 128 :],
        sent3[:, inner:].T,
        sent3[:, :inner].T,
        sent1[:, inner + heads + 1],
        sent4[:, :hidden_cols],
        sent4[:, hidden_cols:],
        sent5.T,
    )


def solution(mesh):
    in_specs = (
        P("dp", None),
        P("dp", None),
        P("dp", None),
        P(),
        P("dp", "head"),
        P("dp", "head"),
        P("dp", "head"),
        P("dp", None),
        P(None, "head"),
        P("head"),
        P(),
        P(),
        P("head"),
        P("head"),
        P("head"),
        P("dp", "head"),
        P("dp", None),
        P("dp", None),
        P("head", "dp"),
        P("head", "dp"),
        P(),
        P("dp", "head"),
        P("dp", "head"),
        P("head", "dp"),
    )
    out_specs = (
        P("dp", None),
        P("dp", None),
        P("dp"),
        P("dp", "head"),
        P("dp", "head"),
        P("dp", "head"),
        P(("dp", "head"), None),
        P(None, "head"),
        P("head"),
        P(None, ("dp", "head")),
        P(("dp", "head")),
        P("head"),
        P("head"),
        P("head"),
        P("dp", "head"),
        P(("dp", "head"), None),
        P(("dp", "head"), None),
        P("head", "dp"),
        P("head", "dp"),
        P("dp"),
        P("dp", "head"),
        P("dp", "head"),
        P("head", "dp"),
    )
    return jax.shard_map(body, mesh=mesh, in_specs=in_specs, out_specs=out_specs, check_vma=False)
```

```python
import functools
import math

import jax
import jax.numpy as jnp
from jax import lax
from jax.experimental import pallas as pl
from jax.experimental.pallas import tpu as pltpu
from jax.sharding import PartitionSpec as P

QHEADS = 8
KVHEADS = 2
HD = 64
STATE = 128
CHUNK = 128
TAPS = 4
EPSILON = 1e-05
THETA = 100000000000.0
NEG = -1e30
HIGHEST = lax.Precision.HIGHEST
BF = jnp.bfloat16
F32 = jnp.float32
VMEM_LIMIT = 48 * 1024 * 1024


def dot(left, right, dims=((1,), (0,))):
    return lax.dot_general(left, right, (dims, ((), ())), preferred_element_type=F32)


def dot_exact(left, right):
    return lax.dot_general(
        left, right, (((1,), (0,)), ((), ())), precision=HIGHEST, preferred_element_type=F32
    )


def sigmoid(values):
    return 0.5 + 0.5 * jnp.tanh(0.5 * values)


def pick(low_half, table, first):
    return jnp.where(low_half, table[:, first : first + 1], table[:, first + 1 : first + 2])


def halves(low_half, tile):
    zero = jnp.zeros_like(tile)
    return jnp.concatenate(
        [jnp.where(low_half, tile, zero), jnp.where(low_half, zero, tile)], axis=0
    )


def ssd_tables(dt_raw, dt_bias, rate, emask, fmask, total, lower):
    step = jnp.log1p(jnp.exp(dt_raw + dt_bias))
    decay = dot_exact(lower, step * rate)
    last = decay[CHUNK - 1 : CHUNK, :]
    enter = jnp.exp(decay) * emask
    leave = jnp.exp(last - decay) * fmask
    whole = jnp.exp(last) * total
    return step, decay, enter, leave, whole


def shifted_rows(buf, cols, keeps):
    return [keep * buf[8 - k : 8 - k + CHUNK, cols] for k, keep in enumerate(keeps, 1)]


def conv_rows(now, shifted, taps, bias):
    result = bias + taps[0:1] * now
    for k, earlier in enumerate(shifted, 1):
        result = result + taps[k : k + 1] * earlier
    return result


def column(table, at):
    return jnp.broadcast_to(table[:, at : at + 1], (table.shape[0], 128))


def wide_column(tile):
    return jnp.concatenate([tile, tile], axis=1)


def head_lanes(inner):
    head = lax.broadcasted_iota(jnp.int32, (128, inner), 0)
    channel = lax.broadcasted_iota(jnp.int32, (128, inner), 1)
    return (head == channel // 64).astype(BF)


def spread(table, lanes2):
    high = table.astype(BF)
    rest = (table - high.astype(F32)).astype(BF)
    return dot(jnp.concatenate([high, rest], axis=1), lanes2)


def place_of(cols, inner):
    return slice(cols.start + 128 * (2 * cols.start // inner), cols.stop + 128 * (2 * cols.start // inner))


def steps_of(h_ref, inner, lane, heads):
    mid = inner // 2
    mine, other = h_ref[:, mid : mid + 128], h_ref[:, inner + 128 :]
    return jnp.where(lane < heads, mine, jnp.where(lane < 2 * heads, other, 0.0))


def ssd_forward_kernel(
    h_ref, pair_ref, z_ref, aux_ref, segrow_ref, xpar_ref, bcpar_ref, hpar_ref,
    gated_ref, scan_ref, start_ref, xbuf, pbuf, state, lanes2, step_s, enter_s, leave_s,
):
    inner = z_ref.shape[1]
    pairs = inner // 128
    lane = lax.broadcasted_iota(jnp.int32, (CHUNK, 128), 1)
    sub = lax.broadcasted_iota(jnp.int32, (CHUNK, 128), 0)
    low_half = lane < 64

    @pl.when(pl.program_id(0) == 0)
    def _():
        xbuf[0:8, :] = jnp.zeros((8, inner), F32)
        pbuf[0:8, :] = jnp.zeros((8, 2 * STATE), F32)
        state[...] = jnp.zeros_like(state)
        lanes2[0:128, :] = head_lanes(inner)
        lanes2[128:256, :] = head_lanes(inner)

    for first in (0, inner // 2):
        cols = slice(first, first + inner // 2)
        xbuf[8 : 8 + CHUNK, cols] = h_ref[:, place_of(cols, inner)]
    pbuf[8 : 8 + CHUNK, :] = pair_ref[...]
    aux = aux_ref[...]
    keeps = [column(aux, k) for k in range(1, TAPS)]
    pre_pair = conv_rows(
        pbuf[8 : 8 + CHUNK, :], shifted_rows(pbuf, slice(None), [wide_column(v) for v in keeps]),
        bcpar_ref[0:4, :], bcpar_ref[4:5, :])
    act_pair = pre_pair * sigmoid(pre_pair)
    in_b = act_pair[:, :STATE].astype(BF)
    out_c = act_pair[:, STATE:].astype(BF)
    inter = dot(out_c, in_b, ((1,), (1,)))
    allowed = (sub >= lane) & (column(aux, 0) == segrow_ref[0])
    hide = jnp.where(allowed, 0.0, NEG)
    lower = (sub >= lane).astype(F32)
    emask = aux[:, 7:8]
    step, decay, enter, leave, whole = ssd_tables(
        steps_of(h_ref, inner, lane, pairs), hpar_ref[0:1, :], hpar_ref[1:2, :],
        emask, aux[:, 8:9], emask[CHUNK - 1 : CHUNK, :], lower,
    )
    step_s[...] = spread(step, lanes2[...])
    enter_s[...] = spread(enter, lanes2[...])
    leave_s[...] = spread(leave, lanes2[...])
    decay_t = decay.T
    start = state[...].astype(BF)
    start_ref[...] = start
    enter_s[...] = dot(out_c, start) * enter_s[...]
    for p in range(pairs):
        cols = slice(128 * p, 128 * p + 128)
        pre = conv_rows(
            xbuf[8 : 8 + CHUNK, cols], shifted_rows(xbuf, cols, keeps),
            xpar_ref[0:4, cols], xpar_ref[4:5, cols])
        act = pre * sigmoid(pre)
        driven = (step_s[:, cols] * act).astype(BF)
        mixes = []
        for head in (2 * p, 2 * p + 1):
            gap = column(decay, head) - decay_t[head : head + 1, :]
            mixes.append((inter * jnp.exp(gap + hide)).astype(BF))
        scanned = dot(jnp.concatenate(mixes, axis=1), halves(low_half, driven))
        scanned = scanned + enter_s[:, cols] + xpar_ref[5:6, cols] * act
        scan_ref[:, cols] = scanned.astype(scan_ref.dtype)
        gate = z_ref[:, cols].astype(F32)
        gated_ref[:, cols] = (scanned * (gate * sigmoid(gate))).astype(BF)
        sent = (leave_s[:, cols] * driven.astype(F32)).astype(BF)
        state[:, cols] = pick(low_half[0:1], whole, 2 * p) * state[:, cols] + dot(
            in_b, sent, ((0,), (0,))
        )
    xbuf[0:8, :] = xbuf[CHUNK : CHUNK + 8, :]
    pbuf[0:8, :] = pbuf[CHUNK : CHUNK + 8, :]


def ssd_forward(h1, pair, z, aux, segrow, xpar, bcpar, hpar):
    length, inner = z.shape
    chunks = length // CHUNK
    width = h1.shape[1]
    whole = lambda arr: pl.BlockSpec(arr.shape, lambda c: (0,) * arr.ndim)
    rows = lambda cols: pl.BlockSpec((CHUNK, cols), lambda c: (c, 0))
    return pl.pallas_call(
        ssd_forward_kernel,
        grid=(chunks,),
        in_specs=[
            rows(width), rows(2 * STATE), rows(inner), rows(128),
            pl.BlockSpec((1, 1, CHUNK), lambda c: (c, 0, 0)),
            whole(xpar), whole(bcpar), whole(hpar),
        ],
        out_specs=[rows(inner), rows(inner), rows(inner)],
        out_shape=[
            jax.ShapeDtypeStruct((length, inner), BF),
            jax.ShapeDtypeStruct((length, inner), BF),
            jax.ShapeDtypeStruct((chunks * STATE, inner), BF),
        ],
        scratch_shapes=[
            pltpu.VMEM((CHUNK + 8, inner), F32),
            pltpu.VMEM((CHUNK + 8, 2 * STATE), F32),
            pltpu.VMEM((STATE, inner), F32),
            pltpu.VMEM((256, inner), BF),
            pltpu.VMEM((CHUNK, inner), F32),
            pltpu.VMEM((CHUNK, inner), F32),
            pltpu.VMEM((CHUNK, inner), F32),
        ],
        compiler_params=pltpu.CompilerParams(vmem_limit_bytes=VMEM_LIMIT),
        name="ssd_forward",
    )(h1, pair, z, aux, segrow, xpar, bcpar, hpar)


def ssd_backward_kernel(
    h_ref, prev_ref, pair_ref, pair_prev_ref, z_ref, dgated_ref, start_ref, aux_ref,
    segrow_ref, xpar_ref, bcpar_ref, hpar_ref,
    dh_ref, dpair_ref, xacc_ref, bcacc_ref, hacc_ref,
    xbuf, pbuf, dxbuf, dpbuf, dstate, lanes2, step_s, enter_s, leave_s, came_s, dcame_s, sent_s,
    direct_s, inter_s, row_s, across_s,
):
    inner = z_ref.shape[1]
    pairs = inner // 128
    lane = lax.broadcasted_iota(jnp.int32, (CHUNK, 128), 1)
    sub = lax.broadcasted_iota(jnp.int32, (CHUNK, 128), 0)
    low_half = lane < 64
    low_row = low_half[0:1]

    @pl.when(pl.program_id(0) == 0)
    def _():
        dxbuf[CHUNK : CHUNK + 8, :] = jnp.zeros((8, inner), F32)
        dpbuf[CHUNK : CHUNK + 8, :] = jnp.zeros((8, 2 * STATE), F32)
        dstate[...] = jnp.zeros_like(dstate)
        xacc_ref[...] = jnp.zeros_like(xacc_ref)
        bcacc_ref[...] = jnp.zeros_like(bcacc_ref)
        hacc_ref[...] = jnp.zeros_like(hacc_ref)
        across_s[...] = jnp.zeros_like(across_s)
        lanes2[0:128, :] = head_lanes(inner)
        lanes2[128:256, :] = head_lanes(inner)

    for first in (0, inner // 2):
        cols = slice(first, first + inner // 2)
        xbuf[0:8, cols] = prev_ref[:, place_of(cols, inner)]
        xbuf[8 : 8 + CHUNK, cols] = h_ref[:, place_of(cols, inner)]
    pbuf[0:8, :] = pair_prev_ref[...]
    pbuf[8 : 8 + CHUNK, :] = pair_ref[...]
    aux = aux_ref[...]
    keeps = [column(aux, k) for k in range(1, TAPS)]
    later = [column(aux, 3 + k) for k in range(1, TAPS)]
    shifted_pair = shifted_rows(pbuf, slice(None), [wide_column(v) for v in keeps])
    pre_pair = conv_rows(
        pbuf[8 : 8 + CHUNK, :], shifted_pair, bcpar_ref[0:4, :], bcpar_ref[4:5, :])
    sig_pair = sigmoid(pre_pair)
    act_pair = pre_pair * sig_pair
    in_b = act_pair[:, :STATE].astype(BF)
    out_c = act_pair[:, STATE:].astype(BF)
    inter_t = dot(in_b, out_c, ((1,), (1,)))
    allowed_t = (lane >= sub) & (column(aux, 0) == segrow_ref[0])
    hide_t = jnp.where(allowed_t, 0.0, NEG)
    lower = sub >= lane
    emask = aux[:, 7:8]
    rate = hpar_ref[1:2, :]
    dt_raw = steps_of(h_ref, inner, lane, pairs)
    step, decay, enter, leave, whole = ssd_tables(
        dt_raw, hpar_ref[0:1, :], rate,
        emask, aux[:, 8:9], emask[CHUNK - 1 : CHUNK, :], lower.astype(F32),
    )
    step_s[...] = spread(step, lanes2[...])
    enter_s[...] = spread(enter, lanes2[...])
    leave_s[...] = spread(leave, lanes2[...])
    came_s[...] = dot(out_c, start_ref[...]) * enter_s[...]
    leave_b = leave_s[...]
    row_s[...] = (dot(in_b, dstate[...].astype(BF)) * leave_b).astype(BF)
    decay_t = decay.T
    lower_b = lower.astype(BF)
    grad_inter_t = jnp.zeros((CHUNK, 128), F32)
    row_list = []
    for p in range(pairs):
        cols = slice(128 * p, 128 * p + 128)
        shifted = shifted_rows(xbuf, cols, keeps)
        now = xbuf[8 : 8 + CHUNK, cols]
        pre = conv_rows(now, shifted, xpar_ref[0:4, cols], xpar_ref[4:5, cols])
        sig = sigmoid(pre)
        act = pre * sig
        gate = z_ref[:, cols].astype(F32)
        dscan = (dgated_ref[:, cols].astype(F32) * (gate * sigmoid(gate))).astype(BF)
        dscan_f = dscan.astype(F32)
        step_p = step_s[:, cols]
        driven = (step_p * act).astype(BF)
        zero_b = jnp.zeros_like(driven)
        mixes = []
        for head in (2 * p, 2 * p + 1):
            gap = decay_t[head : head + 1, :] - column(decay, head)
            damp = jnp.exp(gap + hide_t)
            mixed = inter_t * damp
            mixes.append(mixed.astype(BF))
            own = jnp.where(low_half == (head % 2 == 0), driven, zero_b)
            grad_mix = dot(own, dscan, ((1,), (1,)))
            grad_inter_t = grad_inter_t + grad_mix * damp
            flow = dot((grad_mix * mixed).astype(BF), lower_b)
            row_list.append(jnp.sum(jnp.where(lane > sub, flow, 0.0), axis=0, keepdims=True))
        from_inter = row_s[:, cols].astype(F32)
        ddriven = dot(jnp.concatenate(mixes, axis=1), halves(low_half, dscan)) + from_inter
        dact = xpar_ref[5:6, cols] * dscan_f + step_p * ddriven
        direct_s[:, cols] = (act * ddriven).astype(BF)
        inter_s[:, cols] = (act * from_inter).astype(BF)
        row_s[:, cols] = (dscan_f * came_s[:, cols]).astype(BF)
        dst = dstate[:, cols]
        whole_p = pick(low_row, whole, 2 * p)
        across_s[0:1, cols] = whole_p * jnp.sum(
            dst * start_ref[:, cols].astype(F32), axis=0, keepdims=True)
        dcame_s[:, cols] = (enter_s[:, cols] * dscan_f).astype(BF)
        sent_s[:, cols] = (leave_s[:, cols] * driven.astype(F32)).astype(BF)
        dpre = dact * (sig * (1.0 + pre * (1.0 - sig)))
        dxbuf[0:CHUNK, cols] = dpre
        dval = xpar_ref[0:1, cols] * dpre
        sums = [jnp.sum(dpre * now, axis=0, keepdims=True)]
        for k in range(1, TAPS):
            dval = dval + xpar_ref[k : k + 1, cols] * (later[k - 1] * dxbuf[k : k + CHUNK, cols])
            sums.append(jnp.sum(dpre * shifted[k - 1], axis=0, keepdims=True))
        sums.append(jnp.sum(dpre, axis=0, keepdims=True))
        sums.append(jnp.sum(dscan_f * act, axis=0, keepdims=True))
        sums.append(jnp.zeros((2, 128), F32))
        xacc_ref[:, cols] += jnp.concatenate(sums, axis=0)
        dh_ref[:, place_of(cols, inner)] = dval.astype(BF)
    dxbuf[CHUNK : CHUNK + 8, :] = dxbuf[0:8, :]
    grad_inter_b = grad_inter_t.astype(BF)
    dstate_b = dstate[...].astype(BF)
    grad_b = dot(grad_inter_b, out_c) + dot(sent_s[...], dstate_b, ((1,), (1,)))
    grad_c = dot(grad_inter_b, in_b, ((0,), (0,))) + dot(dcame_s[...], start_ref[...], ((1,), (1,)))
    for p in range(pairs):
        cols = slice(128 * p, 128 * p + 128)
        dstate[:, cols] = pick(low_row, whole, 2 * p) * dstate[:, cols] + dot(
            out_c, dcame_s[:, cols], ((0,), (0,)))
    grad_act = jnp.concatenate([grad_b, grad_c], axis=1)
    dpre = grad_act * (sig_pair * (1.0 + pre_pair * (1.0 - sig_pair)))
    dpbuf[0:CHUNK, :] = dpre
    dval = bcpar_ref[0:1, :] * dpre
    sums = [jnp.sum(dpre * pbuf[8 : 8 + CHUNK, :], axis=0, keepdims=True)]
    for k in range(1, TAPS):
        dval = dval + bcpar_ref[k : k + 1, :] * (wide_column(later[k - 1]) * dpbuf[k : k + CHUNK, :])
        sums.append(jnp.sum(dpre * shifted_pair[k - 1], axis=0, keepdims=True))
    sums.append(jnp.sum(dpre, axis=0, keepdims=True))
    sums.append(jnp.zeros((3, 2 * STATE), F32))
    bcacc_ref[...] += jnp.concatenate(sums, axis=0)
    dpair_ref[...] = dval.astype(BF)
    dpbuf[CHUNK : CHUNK + 8, :] = dpbuf[0:8, :]
    lanes = lanes2[0:128, :]
    by_head = lambda value: dot(value, lanes, ((1,), (1,)))
    direct = by_head(direct_s[...])
    direct_inter = by_head(inter_s[...])
    row_inter = by_head(row_s[...])
    across = lax.dot_general(
        across_s[...], lanes.astype(F32), (((1,), (1,)), ((), ())), precision=HIGHEST,
        preferred_element_type=F32)[0:1]
    rows = jnp.concatenate(row_list + [jnp.zeros((CHUNK - 2 * pairs, 128), F32)], axis=0).T
    upper_b = (sub <= lane).astype(BF)
    strict_b = (sub > lane).astype(BF)
    grad_decay = rows + across + dot(upper_b, row_inter.astype(BF))
    grad_decay = grad_decay + dot(strict_b, (step * direct_inter).astype(BF))
    dstep = direct + grad_decay * rate
    draw = dstep * sigmoid(dt_raw + hpar_ref[0:1, :])
    hacc_ref[0:1, :] += jnp.sum(draw, axis=0, keepdims=True)
    hacc_ref[1:2, :] += jnp.sum(grad_decay * step, axis=0, keepdims=True) * rate
    mid = inner // 2
    dh_ref[:, mid : mid + 128] = jnp.where(lane < pairs, draw, 0.0).astype(BF)
    dh_ref[:, inner + 128 :] = jnp.where(lane >= pairs, draw, 0.0).astype(BF)


def ssd_backward(h1, pair, z, dgated, start, aux, segrow, xpar, bcpar, hpar):
    length, inner = z.shape
    chunks = length // CHUNK
    width = h1.shape[1]
    whole = lambda arr: pl.BlockSpec(arr.shape, lambda c: (0,) * arr.ndim)
    rows = lambda cols: pl.BlockSpec((CHUNK, cols), lambda c: (chunks - 1 - c, 0))
    before = lambda cols: pl.BlockSpec(
        (8, cols), lambda c: (jnp.maximum((chunks - 1 - c) * (CHUNK // 8) - 1, 0), 0))
    fixed = lambda r, cols: pl.BlockSpec((r, cols), lambda c: (0, 0))
    return pl.pallas_call(
        ssd_backward_kernel,
        grid=(chunks,),
        in_specs=[
            rows(width), before(width), rows(2 * STATE), before(2 * STATE),
            rows(inner), rows(inner), rows(inner), rows(128),
            pl.BlockSpec((1, 1, CHUNK), lambda c: (chunks - 1 - c, 0, 0)),
            whole(xpar), whole(bcpar), whole(hpar),
        ],
        out_specs=[
            rows(width), rows(2 * STATE),
            fixed(8, inner), fixed(8, 2 * STATE), fixed(8, 128),
        ],
        out_shape=[
            jax.ShapeDtypeStruct((length, width), BF),
            jax.ShapeDtypeStruct((length, 2 * STATE), BF),
            jax.ShapeDtypeStruct((8, inner), F32),
            jax.ShapeDtypeStruct((8, 2 * STATE), F32),
            jax.ShapeDtypeStruct((8, 128), F32),
        ],
        scratch_shapes=[
            pltpu.VMEM((CHUNK + 8, inner), F32),
            pltpu.VMEM((CHUNK + 8, 2 * STATE), F32),
            pltpu.VMEM((CHUNK + 8, inner), F32),
            pltpu.VMEM((CHUNK + 8, 2 * STATE), F32),
            pltpu.VMEM((STATE, inner), F32),
            pltpu.VMEM((256, inner), BF),
            pltpu.VMEM((CHUNK, inner), F32),
            pltpu.VMEM((CHUNK, inner), F32),
            pltpu.VMEM((CHUNK, inner), F32),
            pltpu.VMEM((CHUNK, inner), F32),
            pltpu.VMEM((CHUNK, inner), BF),
            pltpu.VMEM((CHUNK, inner), BF),
            pltpu.VMEM((CHUNK, inner), BF),
            pltpu.VMEM((CHUNK, inner), BF),
            pltpu.VMEM((CHUNK, inner), BF),
            pltpu.VMEM((8, inner), F32),
        ],
        compiler_params=pltpu.CompilerParams(vmem_limit_bytes=VMEM_LIMIT),
        name="ssd_backward",
    )(h1, h1, pair, pair, z, dgated, start, aux, segrow, xpar, bcpar, hpar)


def segment_tables(seg):
    length = seg.shape[0]
    chunks = length // CHUNK
    value = seg.astype(F32)
    far = jnp.full((TAPS,), -1.0, F32)
    cols = [value]
    for k in range(1, TAPS):
        cols.append((value == jnp.concatenate([far[:k], value[:-k]])).astype(F32))
    for k in range(1, TAPS):
        cols.append((value == jnp.concatenate([value[k:], far[:k]])).astype(F32))
    by_chunk = value.reshape(chunks, CHUNK)
    ends = by_chunk[:, -1:]
    before = jnp.concatenate([far[:1, None], ends[:-1]], axis=0)
    cols.append((by_chunk == before).astype(F32).reshape(-1))
    cols.append((by_chunk == ends).astype(F32).reshape(-1))
    aux = jnp.stack(cols, axis=1)
    return jnp.pad(aux, ((0, 0), (0, 128 - aux.shape[1]))), by_chunk[:, None, :]


BLOCK = 256
REACH = 512


def rope_tables(length):
    position = jnp.arange(length).astype(F32)
    freqs = jnp.exp(-(jnp.arange(0, HD, 2).astype(F32) / HD) * math.log(THETA))
    angle = position[:, None] * freqs[None, :]
    cosine, sine = jnp.cos(angle), jnp.sin(angle)
    return (
        jnp.concatenate([cosine] * 4, axis=1),
        jnp.concatenate([-sine, sine, -sine, sine], axis=1),
    )


def turn(values, cosine, sine):
    lane = lax.broadcasted_iota(jnp.int32, values.shape, 1)
    swapped = jnp.where(
        lane % HD < HD // 2, pltpu.roll(values, 128 - HD // 2, 1), pltpu.roll(values, HD // 2, 1)
    )
    return values * cosine + swapped * sine


def attention_forward_kernel(
    qkv_ref, cos_ref, sin_ref, segcol_ref, segrow_ref, out_ref, turned_ref, lse_ref
):
    length = qkv_ref.shape[0]
    groups = KVHEADS
    cosine, sine = cos_ref[...], sin_ref[...]
    for t in range(groups + 1):
        cols = slice(128 * t, 128 * t + 128)
        turned_ref[:, cols] = turn(qkv_ref[:, cols].astype(F32), cosine, sine).astype(BF)
    key_at, value_at = 128 * groups, 128 * (groups + 1)
    lane = lax.broadcasted_iota(jnp.int32, (BLOCK, 128), 1)
    for b in range(length // BLOCK):
        rows = slice(b * BLOCK, (b + 1) * BLOCK)
        first = max(0, b * BLOCK - REACH)
        keys = slice(first, (b + 1) * BLOCK)
        many = (b + 1) * BLOCK - first
        at_row = lax.broadcasted_iota(jnp.int32, (BLOCK, many), 0) + b * BLOCK
        at_col = lax.broadcasted_iota(jnp.int32, (BLOCK, many), 1) + first
        allowed = (at_row >= at_col) & (segcol_ref[rows, 0:1] == segrow_ref[:, keys])
        lse = jnp.zeros((BLOCK, 128), F32)
        for g in range(groups):
            key = turned_ref[keys, key_at + 64 * g : key_at + 64 * g + 64]
            value = qkv_ref[keys, value_at + 64 * g : value_at + 64 * g + 64]
            parts = []
            for s in range(2):
                query = turned_ref[rows, 128 * g + 64 * s : 128 * g + 64 * s + 64]
                scores = dot(query, key, ((1,), (1,))) * HD ** (-0.5)
                scores = jnp.where(allowed, scores, NEG)
                peak = jnp.max(scores, axis=1, keepdims=True)
                weights = jnp.exp(scores - peak)
                total = jnp.sum(weights, axis=1, keepdims=True)
                probs = (weights * (1.0 / total)).astype(BF)
                parts.append(dot(probs, value))
                lse = jnp.where(lane == 2 * g + s, peak + jnp.log(total), lse)
            out_ref[rows, 128 * g : 128 * g + 128] = jnp.concatenate(parts, axis=1).astype(BF)
        lse_ref[rows, :] = lse


def attention_forward(qkv, cosine, sine, aux, segrow):
    length = qkv.shape[0]
    return pl.pallas_call(
        attention_forward_kernel,
        out_shape=[
            jax.ShapeDtypeStruct((length, 128 * KVHEADS), BF),
            jax.ShapeDtypeStruct((length, 128 * (KVHEADS + 1)), BF),
            jax.ShapeDtypeStruct((length, 128), F32),
        ],
        compiler_params=pltpu.CompilerParams(vmem_limit_bytes=VMEM_LIMIT),
        name="attention_forward",
    )(qkv, cosine, sine, aux, segrow)


def attention_backward_kernel(
    qkv_ref, turned_ref, datt_ref, lse_ref, delta_ref, cos_ref, sin_ref, segcol_ref, segrow_ref,
    dqkv_ref, dkey, dvalue,
):
    length = qkv_ref.shape[0]
    groups = KVHEADS
    key_at, value_at = 128 * groups, 128 * (groups + 1)
    dkey[...] = jnp.zeros_like(dkey)
    dvalue[...] = jnp.zeros_like(dvalue)
    for b in range(length // BLOCK):
        rows = slice(b * BLOCK, (b + 1) * BLOCK)
        first = max(0, b * BLOCK - REACH)
        keys = slice(first, (b + 1) * BLOCK)
        many = (b + 1) * BLOCK - first
        at_key = lax.broadcasted_iota(jnp.int32, (many, BLOCK), 0) + first
        at_row = lax.broadcasted_iota(jnp.int32, (many, BLOCK), 1) + b * BLOCK
        allowed = (at_row >= at_key) & (segcol_ref[keys, 0:1] == segrow_ref[:, rows])
        dquery = []
        for g in range(groups):
            key = turned_ref[keys, key_at + 64 * g : key_at + 64 * g + 64]
            value = qkv_ref[keys, value_at + 64 * g : value_at + 64 * g + 64]
            dk = jnp.zeros((many, HD), F32)
            dv = jnp.zeros((many, HD), F32)
            for s in range(2):
                head = 2 * g + s
                half = slice(128 * g + 64 * s, 128 * g + 64 * s + 64)
                query = turned_ref[rows, half]
                datt = datt_ref[rows, half]
                scores = dot(key, query, ((1,), (1,))) * HD ** (-0.5)
                probs = jnp.exp(jnp.where(allowed, scores, NEG) - lse_ref[head : head + 1, rows])
                dprobs = dot(value, datt, ((1,), (1,)))
                dscores = (probs * (dprobs - delta_ref[head : head + 1, rows])).astype(BF)
                dk = dk + dot(dscores, query)
                dv = dv + dot(probs.astype(BF), datt)
                dquery.append(dot(dscores, key, ((0,), (0,))) * HD ** (-0.5))
            dkey[keys, 64 * g : 64 * g + 64] += dk * HD ** (-0.5)
            dvalue[keys, 64 * g : 64 * g + 64] += dv
        for g in range(groups):
            tile = jnp.concatenate([dquery[2 * g], dquery[2 * g + 1]], axis=1)
            dqkv_ref[rows, 128 * g : 128 * g + 128] = turn(
                tile, cos_ref[rows, :], -sin_ref[rows, :]
            ).astype(BF)
    dqkv_ref[:, key_at : key_at + 128] = turn(dkey[...], cos_ref[...], -sin_ref[...]).astype(BF)
    dqkv_ref[:, value_at : value_at + 128] = dvalue[...].astype(BF)


def attention_backward(qkv, turned, datt, lse, delta, cosine, sine, aux, segrow):
    length = qkv.shape[0]
    return pl.pallas_call(
        attention_backward_kernel,
        out_shape=jax.ShapeDtypeStruct(qkv.shape, BF),
        scratch_shapes=[pltpu.VMEM((length, 128), F32), pltpu.VMEM((length, 128), F32)],
        compiler_params=pltpu.CompilerParams(vmem_limit_bytes=VMEM_LIMIT),
        name="attention_backward",
    )(qkv, turned, datt, lse, delta, cosine, sine, aux, segrow)


def core_swap(value):
    return lax.ppermute(value, "head", [(0, 1), (1, 0), (2, 3), (3, 2)])


def half_swap(value):
    return lax.ppermute(value, "head", [(0, 2), (2, 0), (1, 3), (3, 1)])


def half_groups(dp):
    return [[d * 4 + 2 * half + core for d in range(dp) for half in range(2)] for core in range(2)]


def ordered(is_first, mine, other, axis):
    return jnp.where(
        is_first,
        jnp.concatenate([mine, other], axis=axis),
        jnp.concatenate([other, mine], axis=axis),
    )


BITS = (2, 4, 1)


def pair_list(dp, low_heads, bit):
    pairs = []
    for d in range(dp):
        for slot in range(4):
            flip = low_heads[slot % 2]
            target = (d ^ bit) * 4 + slot if flip else d * 4 + (slot ^ 2)
            pairs.append((d * 4 + slot, target))
    return pairs


def dp_swap(value, bit):
    return lax.ppermute(value, "dp", [(d, d ^ bit) for d in range(8)])


def near_swap(value, step):
    return lax.ppermute(value, ("dp", "head"), pair_list(8, (step == 1, step == 0), 1))


def append(value, arrived):
    return jnp.concatenate([value, arrived], axis=0)


class Order:
    def __init__(self):
        self.last = None

    def __call__(self, *values):
        held = values if self.last is None else values + (self.last,)
        held = lax.optimization_barrier(held)
        self.last = held[0]
        return held[0] if len(values) == 1 else held[: len(values)]


class Gather:
    def along(self, piece):
        self.piece = piece
        self.first = dp_swap(piece, BITS[0])

    def join(self, first):
        return append(self.piece, first)

    def across(self, pair):
        self.pair = pair
        self.second = dp_swap(pair, BITS[1])

    def join2(self, second):
        return append(self.pair, second)

    def near_step(self, quad):
        self.quad = quad
        self.third = near_swap(quad, 0)

    def join3(self, third):
        return append(self.quad, third)

    def far_step(self, near):
        self.near = near
        self.far = near_swap(near, 1)


def gather_whole(piece, dp, is_first):
    rows, cols = piece.shape
    both = lax.all_gather(
        piece, ("dp", "head"), axis=0, tiled=False, axis_index_groups=half_groups(dp)
    ).reshape(dp, 2, rows, cols)
    mine = jnp.where(is_first, both[:, 0], both[:, 1]).reshape(dp * rows, cols)
    other = jnp.where(is_first, both[:, 1], both[:, 0]).reshape(dp * rows, cols)
    lines = lambda value, side: value.reshape(4, 2, -1, cols)[:, side].reshape(-1, cols)
    return append(lines(mine, 0), lines(other, 0)), append(lines(mine, 1), lines(other, 1))


def unpack_kernel(groups, place, near_a, near_b, far_a, far_b, *outs):
    first = place[0] == 0
    step = near_a.shape[0]
    own = pl.ds(pl.multiple_of(place[1] * step, step), step)
    neighbour = pl.ds(pl.multiple_of((1 - place[1]) * step, step), step)
    for out, (at, size) in zip(outs, groups):
        cols = slice(at, at + size)
        one, two = near_b[:, cols], far_a[:, cols]
        out[own, :size] = near_a[:, cols]
        out[neighbour, size:] = far_b[:, cols]
        out[neighbour, :size] = jnp.where(first, two, one)
        out[own, size:] = jnp.where(first, one, two)


def unpack(near, far, place, groups):
    total, cols = near.shape
    step = total // 8
    view = lambda shift: pl.BlockSpec((step, cols), lambda i, _: (i + shift, 0))
    return pl.pallas_call(
        functools.partial(unpack_kernel, groups),
        grid_spec=pltpu.PrefetchScalarGridSpec(
            num_scalar_prefetch=1,
            grid=(4,),
            in_specs=[view(0), view(4), view(0), view(4)],
            out_specs=[
                pl.BlockSpec((2 * step, 2 * size), lambda i, place: (place[2 + i], 0)) for _, size in groups
            ],
        ),
        out_shape=[jax.ShapeDtypeStruct((total, 2 * size), BF) for _, size in groups],
        compiler_params=pltpu.CompilerParams(vmem_limit_bytes=VMEM_LIMIT),
        name="unpack",
    )(place, near, near, far, far)


def pack_kernel(count, place, *refs):
    ins, (send, two, keep) = refs[:count], refs[count:]
    first = place[0] == 0
    step = keep.shape[0]
    own = pl.ds(pl.multiple_of(place[1] * step, step), step)
    neighbour = pl.ds(pl.multiple_of((1 - place[1]) * step, step), step)
    at = 0
    for ref in ins:
        size = ref.shape[1] // 2
        cols = slice(at, at + size)
        mixed = (ref[neighbour, :size], ref[own, size:])
        keep[:, cols] = ref[own, :size]
        send[1, :, cols] = ref[neighbour, size:]
        send[0, :, cols] = jnp.where(first, mixed[0], mixed[1])
        two[:, cols] = jnp.where(first, mixed[1], mixed[0])
        at += size


def pack(grads, place):
    total = grads[0].shape[0]
    step = total // 8
    cols = sum(grad.shape[1] for grad in grads) // 2
    return pl.pallas_call(
        functools.partial(pack_kernel, len(grads)),
        grid_spec=pltpu.PrefetchScalarGridSpec(
            num_scalar_prefetch=1,
            grid=(4,),
            in_specs=[
                pl.BlockSpec((2 * step, grad.shape[1]), lambda i, place: (place[2 + i], 0)) for grad in grads
            ],
            out_specs=[
                pl.BlockSpec((2, step, cols), lambda i, _: (0, i, 0)),
                pl.BlockSpec((step, cols), lambda i, _: (i, 0)),
                pl.BlockSpec((step, cols), lambda i, _: (i, 0)),
            ],
        ),
        out_shape=[
            jax.ShapeDtypeStruct((2, total // 2, cols), BF),
            jax.ShapeDtypeStruct((total // 2, cols), BF),
            jax.ShapeDtypeStruct((total // 2, cols), BF),
        ],
        compiler_params=pltpu.CompilerParams(vmem_limit_bytes=VMEM_LIMIT),
        name="pack",
    )(place, *grads)


def long(value):
    return value.astype(F32)


class Scatter:
    def __init__(self, grads, place):
        self.rows = grads[0].shape[0] // 8
        self.send, self.two, self.keep = pack(grads, place)

    def far_step(self, send):
        self.got = near_swap(send, 1)

    def sum2(self, got):
        self.got = got
        return (long(self.two) + long(got[1])).astype(BF)

    def near_step(self, part):
        self.got2 = near_swap(part, 0)

    def kept(self, part):
        return long(self.keep[part]) + long(self.got[0, part]) + long(self.got2[part])

    def sum3(self, got2):
        self.got2 = got2
        return self.kept(slice(2 * self.rows, 4 * self.rows)).astype(BF)

    def across(self, part):
        self.got3 = dp_swap(part, BITS[1])

    def lower(self, part):
        return self.kept(part) + long(self.got3[part])

    def sum4(self, got3):
        self.got3 = got3
        return self.lower(slice(self.rows, 2 * self.rows)).astype(BF)

    def along(self, part):
        self.got4 = dp_swap(part, BITS[0])

    def result(self, got4):
        return self.lower(slice(0, self.rows)) + long(got4)


def scatter_whole(grads, dp, is_first):
    rows = grads[0].shape[0] // dp
    half_of = lambda grad, side: grad[:, side * (grad.shape[1] // 2) : (side + 1) * (grad.shape[1] // 2)]
    mine, other = [
        jnp.concatenate([half_of(grad, side) for grad in grads], axis=1).reshape(dp, 1, rows, -1)
        for side in range(2)
    ]
    both = ordered(is_first, mine, other, 1).reshape(dp * 2 * rows, -1)
    return lax.psum_scatter(
        both, ("dp", "head"), scatter_dimension=0, tiled=True, axis_index_groups=half_groups(dp)
    ).astype(F32)


def load_kernel(place, tok_ref, cot_ref, gain_ref, rows_ref, cot_out, normed_ref, scale_ref):
    rows = tok_ref[...]
    rows_ref[...] = rows
    cot_out[...] = cot_ref[...]
    rows = rows.astype(F32)
    scale = lax.rsqrt(jnp.mean(rows * rows, axis=1, keepdims=True) + EPSILON)
    scale_ref[...] = scale
    normed_ref[...] = (rows * scale * gain_ref[...]).astype(BF)


def load(tokens, cotangent, gain, half, length):
    width = tokens.shape[1]
    step = 256
    steps = length // step
    picked = pl.BlockSpec((step, width), lambda i, place: (place[0] * steps + i, 0))
    plain = pl.BlockSpec((step, width), lambda i, place: (i, 0))
    return pl.pallas_call(
        load_kernel,
        grid_spec=pltpu.PrefetchScalarGridSpec(
            num_scalar_prefetch=1,
            grid=(steps,),
            in_specs=[picked, picked, pl.BlockSpec((1, width), lambda i, place: (0, 0))],
            out_specs=[plain, plain, plain, pl.BlockSpec((step, 1), lambda i, place: (i, 0))],
        ),
        out_shape=[jax.ShapeDtypeStruct((length, width), BF)] * 3
        + [jax.ShapeDtypeStruct((length, 1), F32)],
        compiler_params=pltpu.CompilerParams(vmem_limit_bytes=VMEM_LIMIT),
        name="load",
    )(half, tokens, cotangent, gain)


def store_kernel(place, mine_ref, got_ref, got2_ref, out_ref):
    step = pl.program_id(0)
    for index, ref in enumerate((mine_ref, got_ref, got2_ref)):

        @pl.when((step >= place[2 * index]) & (step < place[2 * index + 1]))
        def _():
            out_ref[...] = ref[...]


def part_of(mine, core):
    return lax.dynamic_slice_in_dim(mine, core * (mine.shape[0] // 2), mine.shape[0] // 2, 0)


def store(mine, got, got2, half, core):
    length, width = mine.shape
    step = 256
    per = length // step
    begin = jnp.stack(
        [half * per, (1 - half) * per + core * (per // 2), (1 - half) * per + (1 - core) * (per // 2)])
    many = jnp.array([per, per // 2, per // 2])
    place = jnp.stack([begin, begin + many], axis=1).reshape(-1).astype(jnp.int32)
    part = lambda index, size: pl.BlockSpec(
        (step, width), lambda i, place: (jnp.clip(i - place[2 * index], 0, size - 1), 0))
    return pl.pallas_call(
        store_kernel,
        grid_spec=pltpu.PrefetchScalarGridSpec(
            num_scalar_prefetch=1,
            grid=(2 * per,),
            in_specs=[part(0, per), part(1, per // 2), part(2, per // 2)],
            out_specs=pl.BlockSpec((step, width), lambda i, place: (i, 0)),
        ),
        out_shape=jax.ShapeDtypeStruct((2 * length, width), BF),
        compiler_params=pltpu.CompilerParams(vmem_limit_bytes=VMEM_LIMIT),
        name="store",
    )(place, mine, got, got2)


def first_piece_kernel(slot, x_ref, dt_ref, bc_ref, key_ref, value_ref, out_ref):
    inner = x_ref.shape[1]
    heads = dt_ref.shape[1]
    rows = x_ref.shape[0]
    out_ref[:, :inner] = x_ref[...].astype(BF)
    steps = dt_ref[...]
    out_ref[:, inner : inner + 128] = jnp.concatenate(
        [steps, steps, jnp.zeros((rows, 128 - 2 * heads), F32)], axis=1).astype(BF)
    sources = (bc_ref.at[:, :128], bc_ref.at[:, 128:], key_ref, value_ref)
    for index, ref in enumerate(sources):

        @pl.when(slot[0] == index)
        def _():
            out_ref[:, inner + 128 :] = ref[...].astype(BF)


def first_piece(slot, x, dt, bc, key, value):
    vmem = pl.BlockSpec(memory_space=pltpu.VMEM)
    return pl.pallas_call(
        first_piece_kernel,
        in_specs=[pl.BlockSpec(memory_space=pltpu.SMEM)] + [vmem] * 5,
        out_specs=vmem,
        out_shape=jax.ShapeDtypeStruct((x.shape[0], x.shape[1] + 256), BF),
        compiler_params=pltpu.CompilerParams(vmem_limit_bytes=VMEM_LIMIT),
        name="first_piece",
    )(slot[None].astype(jnp.int32), x, dt, bc, key, value)


def other_pieces_kernel(z_ref, q_ref, out_w, o_ref, gate_ref, up_ref, down_ref, p2, p3, p4, p5):
    join = lambda *parts: jnp.concatenate(parts, axis=1).astype(BF)
    p2[...] = join(z_ref[...], q_ref[...])
    p3[...] = join(out_w[...].T, o_ref[...].T)
    p4[...] = join(gate_ref[...], up_ref[...])
    p5[...] = down_ref[...].T.astype(BF)


def other_pieces(z, q, out_w, o, gate, up, down):
    rows = z.shape[0]
    vmem = pl.BlockSpec(memory_space=pltpu.VMEM)
    shape = lambda cols: jax.ShapeDtypeStruct((rows, cols), BF)
    return pl.pallas_call(
        other_pieces_kernel,
        in_specs=[vmem] * 7,
        out_specs=[vmem] * 4,
        out_shape=[
            shape(z.shape[1] + q.shape[1]), shape(out_w.shape[0] + o.shape[0]),
            shape(gate.shape[1] + up.shape[1]), shape(down.shape[0]),
        ],
        compiler_params=pltpu.CompilerParams(vmem_limit_bytes=VMEM_LIMIT),
        name="other_pieces",
    )(z, q, out_w, o, gate, up, down)


def shared_kernel(place, bc_ref, kv_ref, keep, send):
    half, core = place[0], place[1]
    step = bc_ref.shape[0] // 4
    for out, which in ((keep, core), (send, 1 - core)):
        for side in range(2):
            slot = 2 * (half if side == 0 else 1 - half) + which
            rows = pl.ds(pl.multiple_of(slot * step, step), step)
            for col in range(4):
                ref = bc_ref if col < 2 else kv_ref
                out[col * step : (col + 1) * step, 128 * side : 128 * side + 128] = ref[
                    rows, 128 * (col % 2) : 128 * (col % 2) + 128]


def shared_rows(grad_bc, grad_kv, half, core):
    total = grad_bc.shape[0]
    step = 128
    spec = pl.BlockSpec((step, 256), lambda i, _: (i, 0))
    return pl.pallas_call(
        shared_kernel,
        grid_spec=pltpu.PrefetchScalarGridSpec(
            num_scalar_prefetch=1,
            grid=(total // step,),
            in_specs=[spec, spec],
            out_specs=[spec, spec],
        ),
        out_shape=[jax.ShapeDtypeStruct((total, 256), BF)] * 2,
        compiler_params=pltpu.CompilerParams(vmem_limit_bytes=VMEM_LIMIT),
        name="shared_rows",
    )(jnp.stack([half, core]).astype(jnp.int32), grad_bc, grad_kv)


def products_kernel(count, *refs):
    out = refs[-1]
    total = dot(refs[0][...], refs[count][...], ((1,), (1,)))
    for i in range(1, count):
        total = total + dot(refs[i][...], refs[count + i][...], ((1,), (1,)))
    out[...] = total.astype(out.dtype)


def products(lefts, rights, dtype):
    length = lefts[0].shape[0]
    width = rights[0].shape[0]
    step = 256
    return pl.pallas_call(
        functools.partial(products_kernel, len(lefts)),
        grid=(length // step,),
        in_specs=[pl.BlockSpec((step, left.shape[1]), lambda i: (i, 0)) for left in lefts]
        + [pl.BlockSpec(right.shape, lambda i: (0, 0)) for right in rights],
        out_specs=pl.BlockSpec((step, width), lambda i: (i, 0)),
        out_shape=jax.ShapeDtypeStruct((length, width), dtype),
        compiler_params=pltpu.CompilerParams(vmem_limit_bytes=VMEM_LIMIT),
        name="products",
    )(*lefts, *rights)


def core_sum(part):
    part = part.astype(BF)
    return part.astype(F32) + core_swap(part).astype(F32)


def wide(mine, other, width):
    return jnp.concatenate([mine[:, :width], other[:, :width]], axis=1)


def norm_back(grad, values, scale, gain):
    weighted = grad * gain
    inner = jnp.mean(weighted * values, axis=-1, keepdims=True)
    return scale * weighted - values * (scale * scale * scale * inner), jnp.sum(
        grad * (values * scale), axis=0
    )


def body(
    tokens, segments, cotangent, gain_in, mamba_gate_weight, mamba_input_weight, w_dt, w_bc,
    convolution_input_taps, convolution_input_bias, conv_bc, conv_bc_bias, dt_bias, a_log, d_skip,
    w_q, w_k, w_v, w_o, mamba_output_weight, gain_ffn, w_gate, w_up, w_down,
):
    length = segments.shape[1]
    width = tokens.shape[1]
    rows_here = mamba_gate_weight.shape[0]
    dp = width // rows_here
    inner = mamba_gate_weight.shape[1]
    heads = w_dt.shape[1]
    qcols = w_q.shape[1]
    hidden_cols = w_gate.shape[1]
    slot = lax.axis_index("head")
    half = slot // 2
    core = slot % 2
    is_first = half == 0
    place_dp = lax.axis_index("dp")
    if dp == 8:
        route = jnp.stack([core, place_dp % 2] + [(place_dp // 2) ^ i for i in range(4)])
    else:
        route = jnp.concatenate([jnp.zeros((2,), jnp.int32), jnp.arange(4)])
    route = route.astype(jnp.int32)
    gain_in, gain_ffn = gain_in[None], gain_ffn[None]

    short = lambda value: value.astype(BF)
    first_core = core == 0
    flip = lambda tile: jnp.where(is_first, tile, jnp.concatenate([tile[:, HD:], tile[:, :HD]], axis=1))
    flips = lambda tile: jnp.concatenate([flip(tile[:, :128]), flip(tile[:, 128:])], axis=1)
    cols = ((0,), (0,))
    own = half[None].astype(jnp.int32)
    ringed = dp == 8
    order = Order()

    def tables(segments):
        seg = lax.dynamic_index_in_dim(segments, half, 0, keepdims=False)
        return segment_tables(seg) + rope_tables(length)

    piece1 = first_piece(slot, mamba_input_weight, w_dt, w_bc, w_k, w_v)
    rest = (mamba_gate_weight, w_q, mamba_output_weight, w_o, w_gate, w_up, w_down)
    shapes1 = ((0, inner + 128), (inner + 128, 128))
    shapes2 = shapes3 = ((0, inner), (inner, qcols))
    shapes4 = ((0, hidden_cols), (hidden_cols, hidden_cols))
    shapes5 = ((0, hidden_cols),)
    g1, g2, g3, g4, g5 = [Gather() for _ in range(5)]
    if ringed:
        g1.along(piece1)
        held = order(g1.first, tokens, cotangent, segments, *rest)
        first1, tokens, cotangent, segments = held[:4]
        pieces = other_pieces(*held[4:])
        pair1, *pieces = order(g1.join(first1), *pieces)
        g1.across(pair1)
        for g, piece in zip((g2, g3, g4, g5), pieces):
            g.along(piece)
    else:
        pieces = (
            jnp.concatenate([short(mamba_gate_weight), short(w_q)], axis=1),
            jnp.concatenate([short(mamba_output_weight).T, short(w_o).T], axis=1),
            jnp.concatenate([short(w_gate), short(w_up)], axis=1), short(w_down).T)
        ways = [gather_whole(piece, dp, is_first) for piece in (piece1,) + pieces]
    rows_b, upstream, normed, scale = load(tokens, cotangent, gain_in, own, length)
    aux, segrow, cosine, sine = tables(segments)
    seg_line = aux[:, 0][None]
    per_head = jnp.pad(jnp.stack([dt_bias, a_log, d_skip]), ((0, 5), (0, 128 - heads)))
    small = jnp.concatenate(
        [jnp.concatenate([convolution_input_taps, convolution_input_bias[None],
                          jnp.repeat(d_skip, HD)[None], jnp.zeros((2, inner), F32)], axis=0), per_head],
        axis=1)
    small_other = half_swap(small)
    xpar = jnp.concatenate([small[:, :inner], small_other[:, :inner]], axis=1)
    head_par = jnp.concatenate(
        [small[:2, inner : inner + heads], small_other[:2, inner : inner + heads],
         jnp.zeros((2, 128 - 2 * heads), F32)], axis=1)
    lane = jnp.arange(128) < 2 * heads
    hpar = jnp.concatenate(
        [head_par[:1], jnp.where(lane, -jnp.exp(head_par[1:]), 0.0), jnp.zeros((6, 128), F32)], axis=0)
    bcpar = jnp.concatenate([conv_bc, conv_bc_bias[None], jnp.zeros((3, conv_bc.shape[1]), F32)], axis=0)
    rows = rows_b.astype(F32)

    if ringed:
        second1, normed, aux, cosine, sine, xpar, hpar = order(
            g1.second, normed, aux, cosine, sine, xpar, hpar)
        quad1, first2 = order(g1.join2(second1), g2.first)
        g1.near_step(quad1)
        pair2, third1 = order(g2.join(first2), g1.third)
        g2.across(pair2)
        near1, second2 = order(g1.join3(third1), g2.second)
        g1.far_step(near1)
        quad2, first3 = order(g2.join2(second2), g3.first)
        g2.near_step(quad2)
        pair3, third2 = order(g3.join(first3), g2.third)
        g3.across(pair3)
        near2, far1 = order(g2.join3(third2), g1.far)
        g2.far_step(near2)
        ways1 = (g1.near, far1)
    else:
        ways1 = ways[0]
    weight1, quarters = unpack(*ways1, route, shapes1)
    swap_halves = lambda tile: jnp.concatenate([tile[:, 128:], tile[:, :128]], axis=1)
    quarters = jnp.where(is_first, quarters, swap_halves(quarters))
    others = core_swap(quarters)
    h1 = dot(normed, weight1)
    if ringed:
        h1, second3, first4 = order(h1, g3.second, g4.first)
        quad3, pair4 = g3.join2(second3), g4.join(first4)
        quad3, pair4, others = order(quad3, pair4, others)
        g3.near_step(quad3)
        g4.across(pair4)
    c0 = jnp.where(first_core, quarters, others)
    c1 = jnp.where(first_core, others, quarters)
    weight_bc = jnp.concatenate([c0[:, :128], c1[:, :128]], axis=1)
    weight_kv = flips(jnp.concatenate([c0[:, 128:], c1[:, 128:]], axis=1))
    pair = dot(normed, weight_bc)
    keyvalue = short(dot(normed, weight_kv))
    if ringed:
        third3, pair, keyvalue = order(g3.third, pair, keyvalue)
        near3, far2 = order(g3.join3(third3), g2.far)
        g3.far_step(near3)
        ways2 = (g2.near, far2)
    else:
        ways2 = ways[1]
    weight_z, weight_q = unpack(*ways2, route, shapes2)
    z = short(dot(normed, weight_z))
    qkv = jnp.concatenate([short(dot(normed, weight_q)), keyvalue], axis=1)
    if ringed:
        second4, first5, z, qkv = order(g4.second, g5.first, z, qkv)
        quad4, pair5, qkv = order(g4.join2(second4), g5.join(first5), qkv)
        g4.near_step(quad4)
        g5.across(pair5)

    attended, turned, lse = attention_forward(qkv, cosine, sine, aux, seg_line)
    if ringed:
        third4, far3, attended = order(g4.third, g3.far, attended)
        near4, second5 = order(g4.join3(third4), g5.second)
        g4.far_step(near4)
        quad5, z = order(g5.join2(second5), z)
        g5.near_step(quad5)
        ways3 = (g3.near, far3)
    else:
        ways3 = ways[2]
    gated, scan, start = ssd_forward(h1, pair, z, aux, segrow, xpar, bcpar, hpar)
    weight_out, weight_o = unpack(*ways3, route, shapes3)
    if ringed:
        third5, gated, weight_out = order(g5.third, gated, weight_out)
        near5, gated = order(g5.join3(third5), gated)
        g5.far_step(near5)
    mixed = dot(gated, weight_out, ((1,), (1,))) + dot(attended, weight_o, ((1,), (1,)))
    state = rows + core_sum(mixed)

    scale_ffn = lax.rsqrt(jnp.mean(state * state, axis=-1, keepdims=True) + EPSILON)
    normed_ffn = short(state * scale_ffn * gain_ffn)
    if ringed:
        normed_ffn, far4 = order(normed_ffn, g4.far)
        ways4 = (g4.near, far4)
    else:
        ways4 = ways[3]
    weight_gate, weight_up = unpack(*ways4, route, shapes4)
    gate = dot(normed_ffn, weight_gate)
    up = dot(normed_ffn, weight_up)
    sig = jax.nn.sigmoid(gate)
    hidden = short(gate * sig * up)
    grad_down = short(dot(upstream, hidden, cols))
    if ringed:
        s5 = Scatter([grad_down], route)
        send5, hidden, far5 = order(s5.send, hidden, g5.far)
        s5.far_step(send5)
        ways5 = (g5.near, far5)
    else:
        ways5 = ways[4]
    (weight_down,) = unpack(*ways5, route, shapes5)
    whole = short(dot(hidden, weight_down, ((1,), (1,))))
    if ringed:
        whole, upstream = order(whole, upstream)
    whole_got = core_swap(whole)

    dhidden = dot(upstream, weight_down)
    dgate = short(dhidden * up * (sig * (1.0 + gate * (1.0 - sig))))
    dup = short(dhidden * (gate * sig))
    grad_gate = short(dot(normed_ffn, dgate, cols))
    grad_up = short(dot(normed_ffn, dup, cols))
    if ringed:
        s4 = Scatter([grad_gate, grad_up], route)
        send4, whole_got, dgate, dup = order(s4.send, whole_got, dgate, dup)
        s4.far_step(send4)
    out_mine = short(state + (long(whole) + long(whole_got)))
    dnormed_part = short(dot(dgate, weight_gate, ((1,), (1,))) + dot(dup, weight_up, ((1,), (1,))))
    if ringed:
        dnormed_part, out_mine, got5 = order(dnormed_part, out_mine, s5.got)
    dnormed_got = core_swap(dnormed_part)
    if ringed:
        part5, dnormed_got = order(s5.sum2(got5), dnormed_got)
        s5.near_step(part5)
    out_got = half_swap(part_of(out_mine, core))
    dstate_norm, grad_gain_ffn = norm_back(
        long(dnormed_part) + long(dnormed_got), state, scale_ffn, gain_ffn)
    dstate = long(upstream) + dstate_norm
    dmixed = short(dstate)

    dgated = dot(dmixed, weight_out)
    gate_z = long(z)
    sig_z = jax.nn.sigmoid(gate_z)
    dz = short(dgated * long(scan) * (sig_z * (1.0 + gate_z * (1.0 - sig_z))))
    dgated = short(dgated)
    datt = short(dot(dmixed, weight_o))
    if ringed:
        dgated, dz, datt, got2_5 = order(dgated, dz, datt, s5.got2)
        third_5, datt, dz = order(s5.sum3(got2_5), datt, dz)
        s5.across(third_5)
    delta = jnp.sum((long(datt) * long(attended)).reshape(length, -1, HD), axis=-1).T
    delta = jnp.pad(delta, ((0, 8 - delta.shape[0]), (0, 0)))
    dqkv = attention_backward(
        qkv, turned, datt, lse[:, :8].T, delta, cosine, sine, aux, seg_line)
    if ringed:
        dqkv, got4 = order(dqkv, s4.got)
        part4, dqkv = order(s4.sum2(got4), dqkv)
        s4.near_step(part4)
    dqry, dkv = dqkv[:, : 2 * qcols], dqkv[:, 2 * qcols :]
    second_grads = [
        short(dot(dmixed, gated, cols)), short(dot(dmixed, attended, cols)),
        short(dot(normed, dz, cols)), short(dot(normed, dqry, cols))]
    if ringed:
        s2 = Scatter(second_grads, route)
        send2, got3_5, out_got = order(s2.send, s5.got3, out_got)
        s2.far_step(send2)
        fourth_5, got2_4 = order(s5.sum4(got3_5), s4.got2)
        s5.along(fourth_5)
        third_4, dgated = order(s4.sum3(got2_4), dgated)
        s4.across(third_4)
    dh1, dpair, xacc, bcacc, hacc = ssd_backward(
        h1, pair, z, dgated, start, aux, segrow, xpar, bcpar, hpar)
    if ringed:
        dh1, dpair, got_2, got3_4, got4_5 = order(dh1, dpair, s2.got, s4.got3, s5.got4)
        part2, fourth_4, dh1, dpair = order(s2.sum2(got_2), s4.sum4(got3_4), dh1, dpair)
        s2.near_step(part2)
        s4.along(fourth_4)

    grad1 = short(dot(normed, dh1, cols))
    grad_bc = short(dot(normed, dpair, cols))
    grad_kv = flips(short(dot(normed, dkv, cols)))
    keep_shared, send_shared = shared_rows(grad_bc, grad_kv, half, core)
    if ringed:
        send_shared, dh1, grad1 = order(send_shared, dh1, grad1)
    shared_got = core_swap(send_shared)
    out_got2 = core_swap(out_got)
    bc_got = core_swap(bcacc)
    dnormed_part = products(
        [dh1, dpair, dz, dqry, dkv], [weight1, weight_bc, weight_z, weight_q, weight_kv], BF)
    if ringed:
        dnormed_part, shared_got, got2_2 = order(dnormed_part, shared_got, s2.got2)
    dnormed_got = core_swap(dnormed_part)
    grad_shared = short(long(keep_shared) + long(shared_got))
    last_grads = [grad1, grad_shared]
    if ringed:
        s1 = Scatter(last_grads, route)
        send1, third_2 = order(s1.send, s2.sum3(got2_2))
        s1.far_step(send1)
        s2.across(third_2)
        dnormed_got, third_2, out_got2 = order(dnormed_got, third_2, out_got2)
    drows, grad_gain_in = norm_back(long(dnormed_part) + long(dnormed_got), rows, scale, gain_in)
    grad_mine = short(dstate + drows)
    output = store(out_mine, out_got, out_got2, half, core)
    if ringed:
        grad_mine, got_1 = order(grad_mine, s1.got)
        part1 = order(s1.sum2(got_1))
        s1.near_step(part1)
    grad_got = half_swap(part_of(grad_mine, core))

    skip = xacc[5].reshape(2, heads, HD).sum(axis=-1)
    stretches = []
    for side in range(2):
        stretches.append(jnp.concatenate([
            xacc[:5, side * inner : (side + 1) * inner].reshape(-1),
            hacc[0, side * heads : (side + 1) * heads], hacc[1, side * heads : (side + 1) * heads],
            skip[side]]))
    stretch = stretches[0].shape[0]
    bc_sum = (bcacc + bc_got)[:5]
    vector = jnp.concatenate([
        jnp.where(is_first, stretches[0], stretches[1]), jnp.where(is_first, stretches[1], stretches[0]),
        bc_sum.reshape(-1), grad_gain_in, grad_gain_ffn])
    size = vector.shape[0]
    vector = jnp.pad(vector, (0, -size % 1024)).reshape(-1, 128)
    if ringed:
        vector = vector + half_swap(vector)
        vector, got2_1, got3_2 = order(vector + dp_swap(vector, 1), s1.got2, s2.got3)
        third_1, fourth_2, vector = order(s1.sum3(got2_1), s2.sum4(got3_2), vector)
        s1.across(third_1)
        s2.along(fourth_2)
        vector = vector + dp_swap(vector, 2)
        vector, got4_2, got4_4 = order(vector + dp_swap(vector, 4), s2.got4, s4.got4)
        sent5, sent4, sent2 = s5.result(got4_5), s4.result(got4_4), s2.result(got4_2)
        got3_1 = order(s1.got3)
        fourth_1 = order(s1.sum4(got3_1))
        s1.along(fourth_1)
        sent1 = s1.result(s1.got4)
    else:
        vector = lax.psum(vector, ("dp", "head"), axis_index_groups=half_groups(dp))
        sent5, sent4, sent2, sent1 = [
            scatter_whole(grads, dp, is_first)
            for grads in ([grad_down], [grad_gate, grad_up], second_grads, last_grads)]
    sent3, sent2 = sent2[:, : inner + qcols], sent2[:, inner + qcols :]
    grad_tokens = store(grad_mine, grad_got, core_swap(grad_got), half, core)
    vector = vector.reshape(-1)[:size]
    own = jnp.where(is_first, vector[:stretch], vector[stretch : 2 * stretch])
    taps = own[: 5 * inner].reshape(5, inner)
    per = own[5 * inner :].reshape(3, heads)
    rank = place_dp * 4 + slot
    bc_cols = conv_bc.shape[1] // (4 * dp)
    at = 2 * stretch
    bc_own = lax.dynamic_slice_in_dim(
        vector[at : at + bc_sum.size].reshape(5, -1), rank * bc_cols, bc_cols, 1)
    gain_grads = lax.dynamic_slice_in_dim(
        vector[at + bc_sum.size :].reshape(2, width), place_dp * rows_here, rows_here, 1)

    quarter_rows = rows_here // 4
    shared_own = sent1[:, inner + 128 :].reshape(4, quarter_rows, 128).swapaxes(0, 1).reshape(quarter_rows, -1)
    return (
        output,
        grad_tokens,
        gain_grads[0],
        sent2[:, :inner],
        sent1[:, :inner],
        sent1[:, inner : inner + heads] + sent1[:, inner + heads : inner + 2 * heads],
        shared_own[:, : 2 * STATE],
        taps[:4],
        taps[4],
        bc_own[:4],
        bc_own[4],
        per[0],
        per[1],
        per[2],
        sent2[:, inner:],
        shared_own[:, 2 * STATE : 2 * STATE + 128],
        shared_own[:, 2 * STATE + 128 :],
        sent3[:, inner:].T,
        sent3[:, :inner].T,
        gain_grads[1],
        sent4[:, :hidden_cols],
        sent4[:, hidden_cols:],
        sent5.T,
    )


def solution(mesh):
    in_specs = (
        P("dp", None),
        P("dp", None),
        P("dp", None),
        P(),
        P("dp", "head"),
        P("dp", "head"),
        P("dp", "head"),
        P("dp", None),
        P(None, "head"),
        P("head"),
        P(),
        P(),
        P("head"),
        P("head"),
        P("head"),
        P("dp", "head"),
        P("dp", None),
        P("dp", None),
        P("head", "dp"),
        P("head", "dp"),
        P(),
        P("dp", "head"),
        P("dp", "head"),
        P("head", "dp"),
    )
    out_specs = (
        P("dp", None),
        P("dp", None),
        P("dp"),
        P("dp", "head"),
        P("dp", "head"),
        P("dp", "head"),
        P(("dp", "head"), None),
        P(None, "head"),
        P("head"),
        P(None, ("dp", "head")),
        P(("dp", "head")),
        P("head"),
        P("head"),
        P("head"),
        P("dp", "head"),
        P(("dp", "head"), None),
        P(("dp", "head"), None),
        P("head", "dp"),
        P("head", "dp"),
        P("dp"),
        P("dp", "head"),
        P("dp", "head"),
        P("head", "dp"),
    )
    return jax.shard_map(body, mesh=mesh, in_specs=in_specs, out_specs=out_specs, check_vma=False)
```

```python
import functools
import math

import jax
import jax.numpy as jnp
from jax import lax
from jax.experimental import pallas as pl
from jax.experimental.pallas import tpu as pltpu
from jax.sharding import PartitionSpec as P

QHEADS = 8
KVHEADS = 2
HD = 64
STATE = 128
CHUNK = 128
TAPS = 4
EPSILON = 1e-05
THETA = 100000000000.0
NEG = -1e30
HIGHEST = lax.Precision.HIGHEST
BF = jnp.bfloat16
F32 = jnp.float32
MIB = 1024 * 1024


def cost(micros):
    return pl.CostEstimate(flops=0, transcendentals=0, bytes_accessed=int(micros * 1.107e6))


def dot(left, right, dims=((1,), (0,))):
    return lax.dot_general(left, right, (dims, ((), ())), preferred_element_type=F32)


def dot_exact(left, right):
    return lax.dot_general(
        left, right, (((1,), (0,)), ((), ())), precision=HIGHEST, preferred_element_type=F32
    )


def sigmoid(values):
    return 0.5 + 0.5 * jnp.tanh(0.5 * values)


def pick(low_half, table, first):
    return jnp.where(low_half, table[:, first : first + 1], table[:, first + 1 : first + 2])


def halves(low_half, tile):
    zero = jnp.zeros_like(tile)
    return jnp.concatenate(
        [jnp.where(low_half, tile, zero), jnp.where(low_half, zero, tile)], axis=0
    )


def ssd_tables(dt_raw, dt_bias, rate, emask, fmask, total, lower):
    step = jnp.log1p(jnp.exp(dt_raw + dt_bias))
    decay = dot_exact(lower, step * rate)
    last = decay[CHUNK - 1 : CHUNK, :]
    enter = jnp.exp(decay) * emask
    leave = jnp.exp(last - decay) * fmask
    whole = jnp.exp(last) * total
    return step, decay, enter, leave, whole


def shifted_rows(buf, cols, keeps):
    return [keep * buf[8 - k : 8 - k + CHUNK, cols] for k, keep in enumerate(keeps, 1)]


def conv_rows(now, shifted, taps, bias):
    result = bias + taps[0:1] * now
    for k, earlier in enumerate(shifted, 1):
        result = result + taps[k : k + 1] * earlier
    return result


def column(table, at):
    return jnp.broadcast_to(table[:, at : at + 1], (table.shape[0], 128))


def wide_column(tile):
    return jnp.concatenate([tile, tile], axis=1)


def head_lanes(inner):
    head = lax.broadcasted_iota(jnp.int32, (128, inner), 0)
    channel = lax.broadcasted_iota(jnp.int32, (128, inner), 1)
    return (head == channel // 64).astype(BF)


def spread(table, lanes2):
    high = table.astype(BF)
    rest = (table - high.astype(F32)).astype(BF)
    return dot(jnp.concatenate([high, rest], axis=1), lanes2)


def place_of(cols, inner):
    return slice(cols.start + 128 * (2 * cols.start // inner), cols.stop + 128 * (2 * cols.start // inner))


def steps_of(h_ref, inner, lane, heads):
    mid = inner // 2
    mine, other = h_ref[:, mid : mid + 128], h_ref[:, inner + 128 :]
    return jnp.where(lane < heads, mine, jnp.where(lane < 2 * heads, other, 0.0))


def ssd_forward_kernel(
    h_ref, pair_ref, z_ref, aux_ref, segrow_ref, xpar_ref, bcpar_ref, hpar_ref,
    gated_ref, scan_ref, start_ref, xbuf, pbuf, state, lanes2, step_s, enter_s, leave_s,
):
    inner = z_ref.shape[1]
    pairs = inner // 128
    lane = lax.broadcasted_iota(jnp.int32, (CHUNK, 128), 1)
    sub = lax.broadcasted_iota(jnp.int32, (CHUNK, 128), 0)
    low_half = lane < 64

    @pl.when(pl.program_id(0) == 0)
    def _():
        xbuf[0:8, :] = jnp.zeros((8, inner), F32)
        pbuf[0:8, :] = jnp.zeros((8, 2 * STATE), F32)
        state[...] = jnp.zeros_like(state)
        lanes2[0:128, :] = head_lanes(inner)
        lanes2[128:256, :] = head_lanes(inner)

    for first in (0, inner // 2):
        cols = slice(first, first + inner // 2)
        xbuf[8 : 8 + CHUNK, cols] = h_ref[:, place_of(cols, inner)]
    pbuf[8 : 8 + CHUNK, :] = pair_ref[...]
    aux = aux_ref[...]
    keeps = [column(aux, k) for k in range(1, TAPS)]
    pre_pair = conv_rows(
        pbuf[8 : 8 + CHUNK, :], shifted_rows(pbuf, slice(None), [wide_column(v) for v in keeps]),
        bcpar_ref[0:4, :], bcpar_ref[4:5, :])
    act_pair = pre_pair * sigmoid(pre_pair)
    in_b = act_pair[:, :STATE].astype(BF)
    out_c = act_pair[:, STATE:].astype(BF)
    inter = dot(out_c, in_b, ((1,), (1,)))
    allowed = (sub >= lane) & (column(aux, 0) == segrow_ref[0])
    hide = jnp.where(allowed, 0.0, NEG)
    lower = (sub >= lane).astype(F32)
    emask = aux[:, 7:8]
    step, decay, enter, leave, whole = ssd_tables(
        steps_of(h_ref, inner, lane, pairs), hpar_ref[0:1, :], hpar_ref[1:2, :],
        emask, aux[:, 8:9], emask[CHUNK - 1 : CHUNK, :], lower,
    )
    step_s[...] = spread(step, lanes2[...])
    enter_s[...] = spread(enter, lanes2[...])
    leave_s[...] = spread(leave, lanes2[...])
    decay_t = decay.T
    start = state[...].astype(BF)
    start_ref[...] = start
    enter_s[...] = dot(out_c, start) * enter_s[...]
    for p in range(pairs):
        cols = slice(128 * p, 128 * p + 128)
        pre = conv_rows(
            xbuf[8 : 8 + CHUNK, cols], shifted_rows(xbuf, cols, keeps),
            xpar_ref[0:4, cols], xpar_ref[4:5, cols])
        act = pre * sigmoid(pre)
        driven = (step_s[:, cols] * act).astype(BF)
        mixes = []
        for head in (2 * p, 2 * p + 1):
            gap = column(decay, head) - decay_t[head : head + 1, :]
            mixes.append((inter * jnp.exp(gap + hide)).astype(BF))
        scanned = dot(jnp.concatenate(mixes, axis=1), halves(low_half, driven))
        scanned = scanned + enter_s[:, cols] + xpar_ref[5:6, cols] * act
        scan_ref[:, cols] = scanned.astype(scan_ref.dtype)
        gate = z_ref[:, cols].astype(F32)
        gated_ref[:, cols] = (scanned * (gate * sigmoid(gate))).astype(BF)
        sent = (leave_s[:, cols] * driven.astype(F32)).astype(BF)
        state[:, cols] = pick(low_half[0:1], whole, 2 * p) * state[:, cols] + dot(
            in_b, sent, ((0,), (0,))
        )
    xbuf[0:8, :] = xbuf[CHUNK : CHUNK + 8, :]
    pbuf[0:8, :] = pbuf[CHUNK : CHUNK + 8, :]


def ssd_forward(h1, pair, z, aux, segrow, xpar, bcpar, hpar):
    length, inner = z.shape
    chunks = length // CHUNK
    width = h1.shape[1]
    whole = lambda arr: pl.BlockSpec(arr.shape, lambda c: (0,) * arr.ndim)
    rows = lambda cols: pl.BlockSpec((CHUNK, cols), lambda c: (c, 0))
    return pl.pallas_call(
        ssd_forward_kernel,
        grid=(chunks,),
        in_specs=[
            rows(width), rows(2 * STATE), rows(inner), rows(128),
            pl.BlockSpec((1, 1, CHUNK), lambda c: (c, 0, 0)),
            whole(xpar), whole(bcpar), whole(hpar),
        ],
        out_specs=[rows(inner), rows(inner), rows(inner)],
        out_shape=[
            jax.ShapeDtypeStruct((length, inner), BF),
            jax.ShapeDtypeStruct((length, inner), BF),
            jax.ShapeDtypeStruct((chunks * STATE, inner), BF),
        ],
        scratch_shapes=[
            pltpu.VMEM((CHUNK + 8, inner), F32),
            pltpu.VMEM((CHUNK + 8, 2 * STATE), F32),
            pltpu.VMEM((STATE, inner), F32),
            pltpu.VMEM((256, inner), BF),
            pltpu.VMEM((CHUNK, inner), F32),
            pltpu.VMEM((CHUNK, inner), F32),
            pltpu.VMEM((CHUNK, inner), F32),
        ],
        compiler_params=pltpu.CompilerParams(vmem_limit_bytes=20 * MIB),
        cost_estimate=cost(10),
        name="ssd_forward",
    )(h1, pair, z, aux, segrow, xpar, bcpar, hpar)


def ssd_backward_kernel(
    h_ref, prev_ref, pair_ref, pair_prev_ref, z_ref, dgated_ref, start_ref, aux_ref,
    segrow_ref, xpar_ref, bcpar_ref, hpar_ref,
    dh_ref, dpair_ref, acc_ref,
    xbuf, pbuf, dxbuf, dpbuf, dstate, lanes2, step_s, enter_s, leave_s, came_s, dcame_s, sent_s,
    direct_s, inter_s, row_s, across_s,
):
    inner = z_ref.shape[1]
    pairs = inner // 128
    lane = lax.broadcasted_iota(jnp.int32, (CHUNK, 128), 1)
    sub = lax.broadcasted_iota(jnp.int32, (CHUNK, 128), 0)
    low_half = lane < 64
    low_row = low_half[0:1]

    @pl.when(pl.program_id(0) == 0)
    def _():
        dxbuf[CHUNK : CHUNK + 8, :] = jnp.zeros((8, inner), F32)
        dpbuf[CHUNK : CHUNK + 8, :] = jnp.zeros((8, 2 * STATE), F32)
        dstate[...] = jnp.zeros_like(dstate)
        acc_ref[...] = jnp.zeros_like(acc_ref)
        across_s[...] = jnp.zeros_like(across_s)
        lanes2[0:128, :] = head_lanes(inner)
        lanes2[128:256, :] = head_lanes(inner)

    for first in (0, inner // 2):
        cols = slice(first, first + inner // 2)
        xbuf[0:8, cols] = prev_ref[:, place_of(cols, inner)]
        xbuf[8 : 8 + CHUNK, cols] = h_ref[:, place_of(cols, inner)]
    pbuf[0:8, :] = pair_prev_ref[...]
    pbuf[8 : 8 + CHUNK, :] = pair_ref[...]
    aux = aux_ref[...]
    keeps = [column(aux, k) for k in range(1, TAPS)]
    later = [column(aux, 3 + k) for k in range(1, TAPS)]
    shifted_pair = shifted_rows(pbuf, slice(None), [wide_column(v) for v in keeps])
    pre_pair = conv_rows(
        pbuf[8 : 8 + CHUNK, :], shifted_pair, bcpar_ref[0:4, :], bcpar_ref[4:5, :])
    sig_pair = sigmoid(pre_pair)
    act_pair = pre_pair * sig_pair
    in_b = act_pair[:, :STATE].astype(BF)
    out_c = act_pair[:, STATE:].astype(BF)
    inter_t = dot(in_b, out_c, ((1,), (1,)))
    allowed_t = (lane >= sub) & (column(aux, 0) == segrow_ref[0])
    hide_t = jnp.where(allowed_t, 0.0, NEG)
    lower = sub >= lane
    emask = aux[:, 7:8]
    rate = hpar_ref[1:2, :]
    dt_raw = steps_of(h_ref, inner, lane, pairs)
    step, decay, enter, leave, whole = ssd_tables(
        dt_raw, hpar_ref[0:1, :], rate,
        emask, aux[:, 8:9], emask[CHUNK - 1 : CHUNK, :], lower.astype(F32),
    )
    step_s[...] = spread(step, lanes2[...])
    enter_s[...] = spread(enter, lanes2[...])
    leave_s[...] = spread(leave, lanes2[...])
    came_s[...] = dot(out_c, start_ref[...]) * enter_s[...]
    leave_b = leave_s[...]
    row_s[...] = (dot(in_b, dstate[...].astype(BF)) * leave_b).astype(BF)
    decay_t = decay.T
    lower_b = lower.astype(BF)
    grad_inter_t = jnp.zeros((CHUNK, 128), F32)
    row_list = []
    for p in range(pairs):
        cols = slice(128 * p, 128 * p + 128)
        shifted = shifted_rows(xbuf, cols, keeps)
        now = xbuf[8 : 8 + CHUNK, cols]
        pre = conv_rows(now, shifted, xpar_ref[0:4, cols], xpar_ref[4:5, cols])
        sig = sigmoid(pre)
        act = pre * sig
        gate = z_ref[:, cols].astype(F32)
        dscan = (dgated_ref[:, cols].astype(F32) * (gate * sigmoid(gate))).astype(BF)
        dscan_f = dscan.astype(F32)
        step_p = step_s[:, cols]
        driven = (step_p * act).astype(BF)
        zero_b = jnp.zeros_like(driven)
        mixes = []
        for head in (2 * p, 2 * p + 1):
            gap = decay_t[head : head + 1, :] - column(decay, head)
            damp = jnp.exp(gap + hide_t)
            mixed = inter_t * damp
            mixes.append(mixed.astype(BF))
            own = jnp.where(low_half == (head % 2 == 0), driven, zero_b)
            grad_mix = dot(own, dscan, ((1,), (1,)))
            grad_inter_t = grad_inter_t + grad_mix * damp
            flow = dot((grad_mix * mixed).astype(BF), lower_b)
            row_list.append(jnp.sum(jnp.where(lane > sub, flow, 0.0), axis=0, keepdims=True))
        from_inter = row_s[:, cols].astype(F32)
        ddriven = dot(jnp.concatenate(mixes, axis=1), halves(low_half, dscan)) + from_inter
        dact = xpar_ref[5:6, cols] * dscan_f + step_p * ddriven
        direct_s[:, cols] = (act * ddriven).astype(BF)
        inter_s[:, cols] = (act * from_inter).astype(BF)
        row_s[:, cols] = (dscan_f * came_s[:, cols]).astype(BF)
        dst = dstate[:, cols]
        whole_p = pick(low_row, whole, 2 * p)
        across_s[0:1, cols] = whole_p * jnp.sum(
            dst * start_ref[:, cols].astype(F32), axis=0, keepdims=True)
        dcame_s[:, cols] = (enter_s[:, cols] * dscan_f).astype(BF)
        sent_s[:, cols] = (leave_s[:, cols] * driven.astype(F32)).astype(BF)
        dpre = dact * (sig * (1.0 + pre * (1.0 - sig)))
        dxbuf[0:CHUNK, cols] = dpre
        dval = xpar_ref[0:1, cols] * dpre
        sums = [jnp.sum(dpre * now, axis=0, keepdims=True)]
        for k in range(1, TAPS):
            dval = dval + xpar_ref[k : k + 1, cols] * (later[k - 1] * dxbuf[k : k + CHUNK, cols])
            sums.append(jnp.sum(dpre * shifted[k - 1], axis=0, keepdims=True))
        sums.append(jnp.sum(dpre, axis=0, keepdims=True))
        sums.append(jnp.sum(dscan_f * act, axis=0, keepdims=True))
        sums.append(jnp.zeros((2, 128), F32))
        acc_ref[:, cols] += jnp.concatenate(sums, axis=0)
        dh_ref[:, place_of(cols, inner)] = dval.astype(BF)
    dxbuf[CHUNK : CHUNK + 8, :] = dxbuf[0:8, :]
    grad_inter_b = grad_inter_t.astype(BF)
    dstate_b = dstate[...].astype(BF)
    grad_b = dot(grad_inter_b, out_c) + dot(sent_s[...], dstate_b, ((1,), (1,)))
    grad_c = dot(grad_inter_b, in_b, ((0,), (0,))) + dot(dcame_s[...], start_ref[...], ((1,), (1,)))
    for p in range(pairs):
        cols = slice(128 * p, 128 * p + 128)
        dstate[:, cols] = pick(low_row, whole, 2 * p) * dstate[:, cols] + dot(
            out_c, dcame_s[:, cols], ((0,), (0,)))
    grad_act = jnp.concatenate([grad_b, grad_c], axis=1)
    dpre = grad_act * (sig_pair * (1.0 + pre_pair * (1.0 - sig_pair)))
    dpbuf[0:CHUNK, :] = dpre
    dval = bcpar_ref[0:1, :] * dpre
    sums = [jnp.sum(dpre * pbuf[8 : 8 + CHUNK, :], axis=0, keepdims=True)]
    for k in range(1, TAPS):
        dval = dval + bcpar_ref[k : k + 1, :] * (wide_column(later[k - 1]) * dpbuf[k : k + CHUNK, :])
        sums.append(jnp.sum(dpre * shifted_pair[k - 1], axis=0, keepdims=True))
    sums.append(jnp.sum(dpre, axis=0, keepdims=True))
    sums.append(jnp.zeros((3, 2 * STATE), F32))
    acc_ref[:, inner : inner + 2 * STATE] += jnp.concatenate(sums, axis=0)
    dpair_ref[...] = dval.astype(BF)
    dpbuf[CHUNK : CHUNK + 8, :] = dpbuf[0:8, :]
    lanes = lanes2[0:128, :]
    by_head = lambda value: dot(value, lanes, ((1,), (1,)))
    direct = by_head(direct_s[...])
    direct_inter = by_head(inter_s[...])
    row_inter = by_head(row_s[...])
    across = lax.dot_general(
        across_s[...], lanes.astype(F32), (((1,), (1,)), ((), ())), precision=HIGHEST,
        preferred_element_type=F32)[0:1]
    rows = jnp.concatenate(row_list + [jnp.zeros((CHUNK - 2 * pairs, 128), F32)], axis=0).T
    upper_b = (sub <= lane).astype(BF)
    strict_b = (sub > lane).astype(BF)
    grad_decay = rows + across + dot(upper_b, row_inter.astype(BF))
    grad_decay = grad_decay + dot(strict_b, (step * direct_inter).astype(BF))
    dstep = direct + grad_decay * rate
    draw = dstep * sigmoid(dt_raw + hpar_ref[0:1, :])
    acc_ref[:, inner + 2 * STATE :] += jnp.concatenate([
        jnp.sum(draw, axis=0, keepdims=True),
        jnp.sum(grad_decay * step, axis=0, keepdims=True) * rate,
        jnp.zeros((6, 128), F32)], axis=0)
    mid = inner // 2
    dh_ref[:, mid : mid + 128] = jnp.where(lane < pairs, draw, 0.0).astype(BF)
    dh_ref[:, inner + 128 :] = jnp.where(lane >= pairs, draw, 0.0).astype(BF)


def ssd_backward(h1, pair, z, dgated, start, aux, segrow, xpar, bcpar, hpar):
    length, inner = z.shape
    chunks = length // CHUNK
    width = h1.shape[1]
    whole = lambda arr: pl.BlockSpec(arr.shape, lambda c: (0,) * arr.ndim)
    rows = lambda cols: pl.BlockSpec((CHUNK, cols), lambda c: (chunks - 1 - c, 0))
    before = lambda cols: pl.BlockSpec(
        (8, cols), lambda c: (jnp.maximum((chunks - 1 - c) * (CHUNK // 8) - 1, 0), 0))
    fixed = lambda r, cols: pl.BlockSpec((r, cols), lambda c: (0, 0))
    return pl.pallas_call(
        ssd_backward_kernel,
        grid=(chunks,),
        in_specs=[
            rows(width), before(width), rows(2 * STATE), before(2 * STATE),
            rows(inner), rows(inner), rows(inner), rows(128),
            pl.BlockSpec((1, 1, CHUNK), lambda c: (chunks - 1 - c, 0, 0)),
            whole(xpar), whole(bcpar), whole(hpar),
        ],
        out_specs=[
            rows(width), rows(2 * STATE),
            fixed(8, inner + 2 * STATE + 128),
        ],
        out_shape=[
            jax.ShapeDtypeStruct((length, width), BF),
            jax.ShapeDtypeStruct((length, 2 * STATE), BF),
            jax.ShapeDtypeStruct((8, inner + 2 * STATE + 128), F32),
        ],
        scratch_shapes=[
            pltpu.VMEM((CHUNK + 8, inner), F32),
            pltpu.VMEM((CHUNK + 8, 2 * STATE), F32),
            pltpu.VMEM((CHUNK + 8, inner), F32),
            pltpu.VMEM((CHUNK + 8, 2 * STATE), F32),
            pltpu.VMEM((STATE, inner), F32),
            pltpu.VMEM((256, inner), BF),
            pltpu.VMEM((CHUNK, inner), F32),
            pltpu.VMEM((CHUNK, inner), F32),
            pltpu.VMEM((CHUNK, inner), F32),
            pltpu.VMEM((CHUNK, inner), F32),
            pltpu.VMEM((CHUNK, inner), BF),
            pltpu.VMEM((CHUNK, inner), BF),
            pltpu.VMEM((CHUNK, inner), BF),
            pltpu.VMEM((CHUNK, inner), BF),
            pltpu.VMEM((CHUNK, inner), BF),
            pltpu.VMEM((8, inner), F32),
        ],
        compiler_params=pltpu.CompilerParams(vmem_limit_bytes=20 * MIB),
        cost_estimate=cost(28),
        name="ssd_backward",
    )(h1, h1, pair, pair, z, dgated, start, aux, segrow, xpar, bcpar, hpar)


def segment_tables(seg):
    length = seg.shape[0]
    chunks = length // CHUNK
    value = seg.astype(F32)
    far = jnp.full((TAPS,), -1.0, F32)
    cols = [value]
    for k in range(1, TAPS):
        cols.append((value == jnp.concatenate([far[:k], value[:-k]])).astype(F32))
    for k in range(1, TAPS):
        cols.append((value == jnp.concatenate([value[k:], far[:k]])).astype(F32))
    by_chunk = value.reshape(chunks, CHUNK)
    ends = by_chunk[:, -1:]
    before = jnp.concatenate([far[:1, None], ends[:-1]], axis=0)
    cols.append((by_chunk == before).astype(F32).reshape(-1))
    cols.append((by_chunk == ends).astype(F32).reshape(-1))
    aux = jnp.stack(cols, axis=1)
    return jnp.pad(aux, ((0, 0), (0, 128 - aux.shape[1]))), by_chunk[:, None, :]


BLOCK = 256
REACH = 512


def rope_tables(length):
    position = jnp.arange(length).astype(F32)
    freqs = jnp.exp(-(jnp.arange(0, HD, 2).astype(F32) / HD) * math.log(THETA))
    angle = position[:, None] * freqs[None, :]
    cosine, sine = jnp.cos(angle), jnp.sin(angle)
    return (
        jnp.concatenate([cosine] * 4, axis=1),
        jnp.concatenate([-sine, sine, -sine, sine], axis=1),
    )


def turn(values, cosine, sine):
    lane = lax.broadcasted_iota(jnp.int32, values.shape, 1)
    swapped = jnp.where(
        lane % HD < HD // 2, pltpu.roll(values, 128 - HD // 2, 1), pltpu.roll(values, HD // 2, 1)
    )
    return values * cosine + swapped * sine


def attention_forward_kernel(
    qkv_ref, cos_ref, sin_ref, segcol_ref, segrow_ref, out_ref, turned_ref, lse_ref
):
    length = qkv_ref.shape[0]
    groups = KVHEADS
    cosine, sine = cos_ref[...], sin_ref[...]
    for t in range(groups + 1):
        cols = slice(128 * t, 128 * t + 128)
        turned_ref[:, cols] = turn(qkv_ref[:, cols].astype(F32), cosine, sine).astype(BF)
    key_at, value_at = 128 * groups, 128 * (groups + 1)
    lane = lax.broadcasted_iota(jnp.int32, (BLOCK, 128), 1)
    for b in range(length // BLOCK):
        rows = slice(b * BLOCK, (b + 1) * BLOCK)
        first = max(0, b * BLOCK - REACH)
        keys = slice(first, (b + 1) * BLOCK)
        many = (b + 1) * BLOCK - first
        at_row = lax.broadcasted_iota(jnp.int32, (BLOCK, many), 0) + b * BLOCK
        at_col = lax.broadcasted_iota(jnp.int32, (BLOCK, many), 1) + first
        allowed = (at_row >= at_col) & (segcol_ref[rows, 0:1] == segrow_ref[:, keys])
        lse = jnp.zeros((BLOCK, 128), F32)
        for g in range(groups):
            key = turned_ref[keys, key_at + 64 * g : key_at + 64 * g + 64]
            value = qkv_ref[keys, value_at + 64 * g : value_at + 64 * g + 64]
            parts = []
            for s in range(2):
                query = turned_ref[rows, 128 * g + 64 * s : 128 * g + 64 * s + 64]
                scores = dot(query, key, ((1,), (1,))) * HD ** (-0.5)
                scores = jnp.where(allowed, scores, NEG)
                peak = jnp.max(scores, axis=1, keepdims=True)
                weights = jnp.exp(scores - peak)
                total = jnp.sum(weights, axis=1, keepdims=True)
                probs = (weights * (1.0 / total)).astype(BF)
                parts.append(dot(probs, value))
                lse = jnp.where(lane == 2 * g + s, peak + jnp.log(total), lse)
            out_ref[rows, 128 * g : 128 * g + 128] = jnp.concatenate(parts, axis=1).astype(BF)
        lse_ref[:, rows] = lse.T[0:8, :]


def attention_forward(qkv, cosine, sine, aux, segrow):
    length = qkv.shape[0]
    return pl.pallas_call(
        attention_forward_kernel,
        out_shape=[
            jax.ShapeDtypeStruct((length, 128 * KVHEADS), BF),
            jax.ShapeDtypeStruct((length, 128 * (KVHEADS + 1)), BF),
            jax.ShapeDtypeStruct((8, length), F32),
        ],
        compiler_params=pltpu.CompilerParams(vmem_limit_bytes=20 * MIB),
        cost_estimate=cost(8),
        name="attention_forward",
    )(qkv, cosine, sine, aux, segrow)


def attention_backward_kernel(
    qkv_ref, turned_ref, datt_ref, lse_ref, delta_ref, cos_ref, sin_ref, segcol_ref, segrow_ref,
    dqkv_ref, dkey, dvalue,
):
    length = qkv_ref.shape[0]
    groups = KVHEADS
    key_at, value_at = 128 * groups, 128 * (groups + 1)
    dkey[...] = jnp.zeros_like(dkey)
    dvalue[...] = jnp.zeros_like(dvalue)
    for b in range(length // BLOCK):
        rows = slice(b * BLOCK, (b + 1) * BLOCK)
        first = max(0, b * BLOCK - REACH)
        keys = slice(first, (b + 1) * BLOCK)
        many = (b + 1) * BLOCK - first
        at_key = lax.broadcasted_iota(jnp.int32, (many, BLOCK), 0) + first
        at_row = lax.broadcasted_iota(jnp.int32, (many, BLOCK), 1) + b * BLOCK
        allowed = (at_row >= at_key) & (segcol_ref[keys, 0:1] == segrow_ref[:, rows])
        dquery = []
        for g in range(groups):
            key = turned_ref[keys, key_at + 64 * g : key_at + 64 * g + 64]
            value = qkv_ref[keys, value_at + 64 * g : value_at + 64 * g + 64]
            dk = jnp.zeros((many, HD), F32)
            dv = jnp.zeros((many, HD), F32)
            for s in range(2):
                head = 2 * g + s
                half = slice(128 * g + 64 * s, 128 * g + 64 * s + 64)
                query = turned_ref[rows, half]
                datt = datt_ref[rows, half]
                scores = dot(key, query, ((1,), (1,))) * HD ** (-0.5)
                probs = jnp.exp(jnp.where(allowed, scores, NEG) - lse_ref[head : head + 1, rows])
                dprobs = dot(value, datt, ((1,), (1,)))
                dscores = (probs * (dprobs - delta_ref[head : head + 1, rows])).astype(BF)
                dk = dk + dot(dscores, query)
                dv = dv + dot(probs.astype(BF), datt)
                dquery.append(dot(dscores, key, ((0,), (0,))) * HD ** (-0.5))
            dkey[keys, 64 * g : 64 * g + 64] += dk * HD ** (-0.5)
            dvalue[keys, 64 * g : 64 * g + 64] += dv
        for g in range(groups):
            tile = jnp.concatenate([dquery[2 * g], dquery[2 * g + 1]], axis=1)
            dqkv_ref[rows, 128 * g : 128 * g + 128] = turn(
                tile, cos_ref[rows, :], -sin_ref[rows, :]
            ).astype(BF)
    dqkv_ref[:, key_at : key_at + 128] = turn(dkey[...], cos_ref[...], -sin_ref[...]).astype(BF)
    dqkv_ref[:, value_at : value_at + 128] = dvalue[...].astype(BF)


def attention_backward(qkv, turned, datt, lse, delta, cosine, sine, aux, segrow):
    length = qkv.shape[0]
    return pl.pallas_call(
        attention_backward_kernel,
        out_shape=jax.ShapeDtypeStruct(qkv.shape, BF),
        scratch_shapes=[pltpu.VMEM((length, 128), F32), pltpu.VMEM((length, 128), F32)],
        compiler_params=pltpu.CompilerParams(vmem_limit_bytes=20 * MIB),
        cost_estimate=cost(9),
        name="attention_backward",
    )(qkv, turned, datt, lse, delta, cosine, sine, aux, segrow)


def feed_forward_kernel(
    rows_ref, part_ref, got_ref, up_ref, gain_ref, gate_w, up_w, down_w,
    state_ref, normed_ref, hidden_ref, dgate_ref, dup_ref, whole_ref, dnormed_ref,
):
    state = rows_ref[...].astype(F32) + (part_ref[...].astype(F32) + got_ref[...].astype(F32))
    state_ref[...] = state
    scale = lax.rsqrt(jnp.mean(state * state, axis=1, keepdims=True) + EPSILON)
    normed = (state * scale * gain_ref[...]).astype(BF)
    normed_ref[...] = normed.T
    gate = dot(normed, gate_w[...])
    up = dot(normed, up_w[...])
    sig = sigmoid(gate)
    act = gate * sig
    hidden = (act * up).astype(BF)
    hidden_ref[...] = hidden
    whole_ref[...] = dot(hidden, down_w[...], ((1,), (1,))).astype(BF)
    dhidden = dot(up_ref[...], down_w[...])
    dup = (dhidden * act).astype(BF)
    dup_ref[...] = dup
    dgate = (dhidden * up * (sig * (1.0 + gate * (1.0 - sig)))).astype(BF)
    dgate_ref[...] = dgate
    dnormed_ref[...] = (
        dot(dgate, gate_w[...], ((1,), (1,))) + dot(dup, up_w[...], ((1,), (1,)))).astype(BF)


def feed_forward(rows, part, got, upstream, gain, gate_w, up_w, down_w):
    length, width = rows.shape
    units = gate_w.shape[1]
    step = 256
    block = lambda cols: pl.BlockSpec((step, cols), lambda i: (i, 0))
    whole = lambda arr: pl.BlockSpec(arr.shape, lambda i: (0, 0))
    shape = lambda cols, kind=BF: jax.ShapeDtypeStruct((length, cols), kind)
    return pl.pallas_call(
        feed_forward_kernel,
        grid=(length // step,),
        in_specs=[block(width)] * 4 + [whole(gain), whole(gate_w), whole(up_w), whole(down_w)],
        out_specs=[block(width), pl.BlockSpec((width, step), lambda i: (0, i))]
        + [block(units)] * 3 + [block(width)] * 2,
        out_shape=[shape(width, F32), jax.ShapeDtypeStruct((width, length), BF)]
        + [shape(units)] * 3 + [shape(width)] * 2,
        compiler_params=pltpu.CompilerParams(vmem_limit_bytes=44 * MIB),
        cost_estimate=cost(18),
        name="feed_forward",
    )(rows, part, got, upstream, gain, gate_w, up_w, down_w)


def norm_gradient(grad, values, scale, gain):
    weighted = grad * gain
    inner = jnp.mean(weighted * values, axis=1, keepdims=True)
    return scale * weighted - values * (scale * scale * scale * inner), jnp.sum(
        grad * (values * scale), axis=0, keepdims=True)


def middle_kernel(
    state_ref, up_ref, dpart_ref, dgot_ref, gain_ref, scan_ref, z_ref, att_ref,
    out_w, o_w, dmixed_ref, dgated_ref, dz_ref, datt_ref, delta_ref, gacc_ref, dmixed_t,
):
    @pl.when(pl.program_id(0) == 0)
    def _():
        gacc_ref[...] = jnp.zeros_like(gacc_ref)

    state = state_ref[...]
    scale = lax.rsqrt(jnp.mean(state * state, axis=1, keepdims=True) + EPSILON)
    grad, gain_grad = norm_gradient(
        dpart_ref[...].astype(F32) + dgot_ref[...].astype(F32), state, scale, gain_ref[...])
    gacc_ref[0:1, :] += gain_grad
    dmixed = (up_ref[...].astype(F32) + grad).astype(BF)
    dmixed_ref[...] = dmixed
    dmixed_t[...] = dmixed.T
    dgated = dot(dmixed, out_w[...])
    dgated_ref[...] = dgated.astype(BF)
    gate = z_ref[...].astype(F32)
    sig = sigmoid(gate)
    dz_ref[...] = (dgated * scan_ref[...].astype(F32) * (sig * (1.0 + gate * (1.0 - sig)))).astype(BF)
    datt = dot(dmixed, o_w[...]).astype(BF)
    datt_ref[...] = datt
    product = datt.astype(F32) * att_ref[...].astype(F32)
    channel = lax.broadcasted_iota(jnp.int32, (product.shape[1], 128), 0)
    head = lax.broadcasted_iota(jnp.int32, (product.shape[1], 128), 1)
    delta = dot_exact(product, (channel // HD == head).astype(F32))
    delta_ref[...] = delta.T[0:8, :]


def middle(state, upstream, dpart, dgot, gain, scan, z, att, out_w, o_w):
    length, width = state.shape
    step = 256
    block = lambda arr: pl.BlockSpec((step, arr.shape[1]), lambda i: (i, 0))
    whole = lambda arr: pl.BlockSpec(arr.shape, lambda i: (0, 0))
    like = lambda arr: jax.ShapeDtypeStruct(arr.shape, BF)
    return pl.pallas_call(
        middle_kernel,
        grid=(length // step,),
        in_specs=[block(arr) for arr in (state, upstream, dpart, dgot)]
        + [whole(gain), block(scan), block(z), block(att), whole(out_w), whole(o_w)],
        out_specs=[block(upstream)] + [block(scan)] * 2
        + [block(att), pl.BlockSpec((8, step), lambda i: (0, i)), pl.BlockSpec((8, width), lambda i: (0, 0)),
           pl.BlockSpec((width, step), lambda i: (0, i))],
        out_shape=[like(upstream)] + [like(scan)] * 2 + [like(att)]
        + [jax.ShapeDtypeStruct((8, length), F32), jax.ShapeDtypeStruct((8, width), F32),
           jax.ShapeDtypeStruct((width, length), BF)],
        compiler_params=pltpu.CompilerParams(vmem_limit_bytes=36 * MIB),
        cost_estimate=cost(11),
        name="middle",
    )(state, upstream, dpart, dgot, gain, scan, z, att, out_w, o_w)


def last_norm_kernel(dpart_ref, dgot_ref, rows_ref, dmixed_ref, scale_ref, gain_ref, out_ref, gacc_ref):
    @pl.when(pl.program_id(0) == 0)
    def _():
        gacc_ref[...] = jnp.zeros_like(gacc_ref)

    grad, gain_grad = norm_gradient(
        dpart_ref[...].astype(F32) + dgot_ref[...].astype(F32), rows_ref[...].astype(F32),
        scale_ref[...], gain_ref[...])
    gacc_ref[0:1, :] += gain_grad
    out_ref[...] = (dmixed_ref[...].astype(F32) + grad).astype(BF)


def last_norm(dpart, dgot, rows, dmixed, scale, gain):
    length, width = rows.shape
    step = 256
    block = pl.BlockSpec((step, width), lambda i: (i, 0))
    return pl.pallas_call(
        last_norm_kernel,
        grid=(length // step,),
        in_specs=[block] * 4 + [pl.BlockSpec((step, 1), lambda i: (i, 0)), pl.BlockSpec((1, width), lambda i: (0, 0))],
        out_specs=[block, pl.BlockSpec((8, width), lambda i: (0, 0))],
        out_shape=[jax.ShapeDtypeStruct((length, width), BF), jax.ShapeDtypeStruct((8, width), F32)],
        compiler_params=pltpu.CompilerParams(vmem_limit_bytes=20 * MIB),
        cost_estimate=cost(4.5),
        name="last_norm",
    )(dpart, dgot, rows, dmixed, scale, gain)


def core_swap(value):
    return lax.ppermute(value, "head", [(0, 1), (1, 0), (2, 3), (3, 2)])


def half_swap(value):
    return lax.ppermute(value, "head", [(0, 2), (2, 0), (1, 3), (3, 1)])


def half_groups(dp):
    return [[d * 4 + 2 * half + core for d in range(dp) for half in range(2)] for core in range(2)]


def ordered(is_first, mine, other, axis):
    return jnp.where(
        is_first,
        jnp.concatenate([mine, other], axis=axis),
        jnp.concatenate([other, mine], axis=axis),
    )


BITS = (2, 4, 1)


def pair_list(dp, low_heads, bit):
    pairs = []
    for d in range(dp):
        for slot in range(4):
            flip = low_heads[slot % 2]
            target = (d ^ bit) * 4 + slot if flip else d * 4 + (slot ^ 2)
            pairs.append((d * 4 + slot, target))
    return pairs


def dp_swap(value, bit):
    return lax.ppermute(value, "dp", [(d, d ^ bit) for d in range(8)])


def near_swap(value, step):
    return lax.ppermute(value, ("dp", "head"), pair_list(8, (step == 1, step == 0), 1))


def append(value, arrived):
    return jnp.concatenate([value, arrived], axis=0)


class Order:
    def __init__(self):
        self.last = None

    def __call__(self, *values):
        held = values if self.last is None else values + (self.last,)
        held = lax.optimization_barrier(held)
        self.last = held[0]
        return held[0] if len(values) == 1 else held[: len(values)]


class Gather:
    def along(self, piece):
        self.piece = piece
        self.first = dp_swap(piece, BITS[0])

    def join(self, first):
        return append(self.piece, first)

    def across(self, pair):
        self.pair = pair
        self.second = dp_swap(pair, BITS[1])

    def join2(self, second):
        return append(self.pair, second)

    def near_step(self, quad):
        self.quad = quad
        self.third = near_swap(quad, 0)

    def join3(self, third):
        return append(self.quad, third)

    def far_step(self, near):
        self.near = near
        self.far = near_swap(near, 1)


def gather_whole(piece, dp, is_first):
    rows, cols = piece.shape
    both = lax.all_gather(
        piece, ("dp", "head"), axis=0, tiled=False, axis_index_groups=half_groups(dp)
    ).reshape(dp, 2, rows, cols)
    mine = jnp.where(is_first, both[:, 0], both[:, 1]).reshape(dp * rows, cols)
    other = jnp.where(is_first, both[:, 1], both[:, 0]).reshape(dp * rows, cols)
    lines = lambda value, side: value.reshape(4, 2, -1, cols)[:, side].reshape(-1, cols)
    return append(lines(mine, 0), lines(other, 0)), append(lines(mine, 1), lines(other, 1))


def unpack_kernel(groups, place, near_a, near_b, far_a, far_b, *outs):
    first = place[0] == 0
    step = near_a.shape[0]
    own = pl.ds(pl.multiple_of(place[1] * step, step), step)
    neighbour = pl.ds(pl.multiple_of((1 - place[1]) * step, step), step)
    for out, (at, size) in zip(outs, groups):
        cols = slice(at, at + size)
        one, two = near_b[:, cols], far_a[:, cols]
        out[own, :size] = near_a[:, cols]
        out[neighbour, size:] = far_b[:, cols]
        out[neighbour, :size] = jnp.where(first, two, one)
        out[own, size:] = jnp.where(first, one, two)


def unpack(near, far, place, groups):
    total, cols = near.shape
    step = total // 8
    view = lambda shift: pl.BlockSpec((step, cols), lambda i, _: (i + shift, 0))
    return pl.pallas_call(
        functools.partial(unpack_kernel, groups),
        grid_spec=pltpu.PrefetchScalarGridSpec(
            num_scalar_prefetch=1,
            grid=(4,),
            in_specs=[view(0), view(4), view(0), view(4)],
            out_specs=[
                pl.BlockSpec((2 * step, 2 * size), lambda i, place: (place[2 + i], 0)) for _, size in groups
            ],
        ),
        out_shape=[jax.ShapeDtypeStruct((total, 2 * size), BF) for _, size in groups],
        compiler_params=pltpu.CompilerParams(vmem_limit_bytes=20 * MIB),
        cost_estimate=cost(3),
        name="unpack",
    )(place, near, near, far, far)


def grads_kernel(spans, place, *refs):
    count = len(spans)
    lefts = refs[:count]
    mines, others = refs[count : 2 * count], refs[2 * count : 3 * count]
    send, two, keep, whole = refs[3 * count :]
    step = pl.program_id(0)
    for left, mine, other, (begin, end) in zip(lefts, mines, others, spans):

        @pl.when((step >= begin) & (step < end))
        def _():
            both = jnp.concatenate([mine[...], other[...]], axis=1)
            whole[...] = both if left is None else dot(left[...], both).astype(BF)

    first = place[0] == 0
    rows = keep.shape[0] // 4
    for line in range(4):
        at = pl.multiple_of(place[2 + line] * (2 * rows), 2 * rows)
        own = pl.ds(at + pl.multiple_of(place[1] * rows, rows), rows)
        neighbour = pl.ds(at + pl.multiple_of((1 - place[1]) * rows, rows), rows)
        here = slice(line * rows, (line + 1) * rows)
        one, other = whole[neighbour, :128], whole[own, 128:]
        keep[here, :] = whole[own, :128]
        send[1, here, :] = whole[neighbour, 128:]
        send[0, here, :] = jnp.where(first, one, other)
        two[here, :] = jnp.where(first, other, one)


def grads(pairs, place):
    total = pairs[0][1].shape[0]
    spans, at = [], 0
    for _, right in pairs:
        tiles = right.shape[1] // 256
        spans.append((at, at + tiles))
        at += tiles
    cols = 128 * at
    lefts = [left for left, _ in pairs if left is not None]
    keys = []
    for left in lefts:
        if not any(left is key for key in keys):
            keys.append(left)
    index_of = [None if left is None else [left is key for key in keys].index(True) for left, _ in pairs]

    def kernel(place, *refs):
        arrays, rest = refs[: len(keys)], refs[len(keys) :]
        chosen = tuple(None if index is None else arrays[index] for index in index_of)
        grads_kernel(spans, place, *chosen, *rest)

    def view(right, span, side):
        tiles = span[1] - span[0]
        return pl.BlockSpec(
            (right.shape[0], 128),
            lambda i, place: (0, side * tiles + jnp.clip(i - span[0], 0, tiles - 1)))

    views = [view(right, span, side) for side in range(2) for (_, right), span in zip(pairs, spans)]
    rights = [right for _, right in pairs]
    return pl.pallas_call(
        kernel,
        grid_spec=pltpu.PrefetchScalarGridSpec(
            num_scalar_prefetch=1,
            grid=(at,),
            in_specs=[pl.BlockSpec(key.shape, lambda i, place: (0, 0)) for key in keys] + views,
            out_specs=[
                pl.BlockSpec((2, total // 2, 128), lambda i, _: (0, 0, i)),
                pl.BlockSpec((total // 2, 128), lambda i, _: (0, i)),
                pl.BlockSpec((total // 2, 128), lambda i, _: (0, i)),
            ],
            scratch_shapes=[pltpu.VMEM((total, 256), BF)],
        ),
        out_shape=[
            jax.ShapeDtypeStruct((2, total // 2, cols), BF),
            jax.ShapeDtypeStruct((total // 2, cols), BF),
            jax.ShapeDtypeStruct((total // 2, cols), BF),
        ],
        compiler_params=pltpu.CompilerParams(vmem_limit_bytes=28 * MIB),
        cost_estimate=cost(6),
        name="grads",
    )(place, *keys, *rights, *rights)


def long(value):
    return value.astype(F32)


def beside(*parts):
    return jnp.concatenate(parts, axis=1)


class Scatter:
    def __init__(self, pairs, place):
        self.rows = pairs[0][1].shape[0] // 8
        self.send, self.two, self.keep = grads(pairs, place)
        self.extra = None

    def far_step(self, send):
        self.got = near_swap(send, 1)

    def sum2(self, got):
        self.got = got
        return (long(self.two) + long(got[1])).astype(BF)

    def near_step(self, part):
        self.got2 = near_swap(part, 0)

    def kept(self, part):
        total = long(self.keep[part]) + long(self.got[0, part]) + long(self.got2[part])
        return total if self.extra is None else total + self.extra[part]

    def sum3(self, got2):
        self.got2 = got2
        return self.kept(slice(2 * self.rows, 4 * self.rows)).astype(BF)

    def across(self, part):
        self.got3 = dp_swap(part, BITS[1])

    def lower(self, part):
        return self.kept(part) + long(self.got3[part])

    def sum4(self, got3):
        self.got3 = got3
        return self.lower(slice(self.rows, 2 * self.rows)).astype(BF)

    def along(self, part):
        self.got4 = dp_swap(part, BITS[0])

    def result(self, got4):
        return self.lower(slice(0, self.rows)) + long(got4)


def scatter_whole(pairs, dp, is_first):
    grads = [right if left is None else dot(left, right).astype(BF) for left, right in pairs]
    rows = grads[0].shape[0] // dp
    half_of = lambda grad, side: grad[:, side * (grad.shape[1] // 2) : (side + 1) * (grad.shape[1] // 2)]
    mine, other = [
        jnp.concatenate([half_of(grad, side) for grad in grads], axis=1).reshape(dp, 1, rows, -1)
        for side in range(2)
    ]
    both = ordered(is_first, mine, other, 1).reshape(dp * 2 * rows, -1)
    return lax.psum_scatter(
        both, ("dp", "head"), scatter_dimension=0, tiled=True, axis_index_groups=half_groups(dp)
    ).astype(F32)


def load_kernel(place, tok_ref, cot_ref, gain_ref, rows_ref, cot_out, normed_ref, scale_ref, normed_t, cot_t):
    rows = tok_ref[...]
    rows_ref[...] = rows
    cot_out[...] = cot_ref[...]
    cot_t[...] = cot_ref[...].T
    rows = rows.astype(F32)
    scale = lax.rsqrt(jnp.mean(rows * rows, axis=1, keepdims=True) + EPSILON)
    scale_ref[...] = scale
    normed = (rows * scale * gain_ref[...]).astype(BF)
    normed_ref[...] = normed
    normed_t[...] = normed.T


def load(tokens, cotangent, gain, half, length):
    width = tokens.shape[1]
    step = 256
    steps = length // step
    picked = pl.BlockSpec((step, width), lambda i, place: (place[0] * steps + i, 0))
    plain = pl.BlockSpec((step, width), lambda i, place: (i, 0))
    return pl.pallas_call(
        load_kernel,
        grid_spec=pltpu.PrefetchScalarGridSpec(
            num_scalar_prefetch=1,
            grid=(steps,),
            in_specs=[picked, picked, pl.BlockSpec((1, width), lambda i, place: (0, 0))],
            out_specs=[plain, plain, plain, pl.BlockSpec((step, 1), lambda i, place: (i, 0))]
            + [pl.BlockSpec((width, step), lambda i, place: (0, i))] * 2,
        ),
        out_shape=[jax.ShapeDtypeStruct((length, width), BF)] * 3
        + [jax.ShapeDtypeStruct((length, 1), F32)]
        + [jax.ShapeDtypeStruct((width, length), BF)] * 2,
        compiler_params=pltpu.CompilerParams(vmem_limit_bytes=20 * MIB),
        cost_estimate=cost(4.5),
        name="load",
    )(half, tokens, cotangent, gain)


def store_kernel(place, *refs):
    step = pl.program_id(0)
    for index, ref in enumerate(refs[:-1]):

        @pl.when((step >= place[2 * index]) & (step < place[2 * index + 1]))
        def _():
            refs[-1][...] = ref[...]


def part_of(mine, core):
    return lax.dynamic_slice_in_dim(mine, core * (mine.shape[0] // 2), mine.shape[0] // 2, 0)


def store(parts, half, core):
    width = parts[0].shape[1]
    length = sum(part.shape[0] for part in parts) // 2
    step = 256
    per = length // step
    begin = [half * per, (1 - half) * per + core * (per // 2), (1 - half) * per + (1 - core) * (per // 2)]
    if len(parts) == 4:
        begin = [half * per + core * (per // 2), half * per + (1 - core) * (per // 2)] + begin[1:]
    many = [part.shape[0] // step for part in parts]
    place = jnp.stack([value for at, size in zip(begin, many) for value in (at, at + size)]).astype(jnp.int32)
    view = lambda index, size: pl.BlockSpec(
        (step, width), lambda i, place: (jnp.clip(i - place[2 * index], 0, size - 1), 0))
    return pl.pallas_call(
        store_kernel,
        grid_spec=pltpu.PrefetchScalarGridSpec(
            num_scalar_prefetch=1,
            grid=(2 * per,),
            in_specs=[view(index, size) for index, size in enumerate(many)],
            out_specs=pl.BlockSpec((step, width), lambda i, place: (i, 0)),
        ),
        out_shape=jax.ShapeDtypeStruct((2 * length, width), BF),
        compiler_params=pltpu.CompilerParams(vmem_limit_bytes=20 * MIB),
        cost_estimate=cost(5),
        name="store",
    )(place, *parts)


def first_piece_kernel(slot, x_ref, dt_ref, bc_ref, key_ref, value_ref, out_ref):
    inner = x_ref.shape[1]
    heads = dt_ref.shape[1]
    rows = x_ref.shape[0]
    out_ref[:, :inner] = x_ref[...].astype(BF)
    steps = dt_ref[...]
    out_ref[:, inner : inner + 128] = jnp.concatenate(
        [steps, steps, jnp.zeros((rows, 128 - 2 * heads), F32)], axis=1).astype(BF)
    sources = (bc_ref.at[:, :128], bc_ref.at[:, 128:], key_ref, value_ref)
    for index, ref in enumerate(sources):

        @pl.when(slot[0] == index)
        def _():
            out_ref[:, inner + 128 :] = ref[...].astype(BF)


def first_piece(slot, x, dt, bc, key, value):
    vmem = pl.BlockSpec(memory_space=pltpu.VMEM)
    return pl.pallas_call(
        first_piece_kernel,
        in_specs=[pl.BlockSpec(memory_space=pltpu.SMEM)] + [vmem] * 5,
        out_specs=vmem,
        out_shape=jax.ShapeDtypeStruct((x.shape[0], x.shape[1] + 256), BF),
        compiler_params=pltpu.CompilerParams(vmem_limit_bytes=20 * MIB),
        cost_estimate=cost(1),
        name="first_piece",
    )(slot[None].astype(jnp.int32), x, dt, bc, key, value)


def other_pieces_kernel(z_ref, q_ref, out_w, o_ref, gate_ref, up_ref, down_ref, p2, p3, p4, p5):
    join = lambda *parts: jnp.concatenate(parts, axis=1).astype(BF)
    p2[...] = join(z_ref[...], q_ref[...])
    p3[...] = join(out_w[...].T, o_ref[...].T)
    p4[...] = join(gate_ref[...], up_ref[...])
    p5[...] = down_ref[...].T.astype(BF)


def other_pieces(z, q, out_w, o, gate, up, down):
    rows = z.shape[0]
    vmem = pl.BlockSpec(memory_space=pltpu.VMEM)
    shape = lambda cols: jax.ShapeDtypeStruct((rows, cols), BF)
    return pl.pallas_call(
        other_pieces_kernel,
        in_specs=[vmem] * 7,
        out_specs=[vmem] * 4,
        out_shape=[
            shape(z.shape[1] + q.shape[1]), shape(out_w.shape[0] + o.shape[0]),
            shape(gate.shape[1] + up.shape[1]), shape(down.shape[0]),
        ],
        compiler_params=pltpu.CompilerParams(vmem_limit_bytes=20 * MIB),
        cost_estimate=cost(1),
        name="other_pieces",
    )(z, q, out_w, o, gate, up, down)


def shared_kernel(place, bc_ref, kv_ref, keep, send):
    half, core = place[0], place[1]
    step = bc_ref.shape[0] // 4
    for out, which in ((keep, core), (send, 1 - core)):
        for side in range(2):
            slot = 2 * (half if side == 0 else 1 - half) + which
            rows = pl.ds(pl.multiple_of(slot * step, step), step)
            for col in range(4):
                ref = bc_ref if col < 2 else kv_ref
                out[col * step : (col + 1) * step, 128 * side : 128 * side + 128] = ref[
                    rows, 128 * (col % 2) : 128 * (col % 2) + 128]


def shared_rows(grad_bc, grad_kv, half, core):
    total = grad_bc.shape[0]
    step = 128
    spec = pl.BlockSpec((step, 256), lambda i, _: (i, 0))
    return pl.pallas_call(
        shared_kernel,
        grid_spec=pltpu.PrefetchScalarGridSpec(
            num_scalar_prefetch=1,
            grid=(total // step,),
            in_specs=[spec, spec],
            out_specs=[spec, spec],
        ),
        out_shape=[jax.ShapeDtypeStruct((total, 256), BF)] * 2,
        compiler_params=pltpu.CompilerParams(vmem_limit_bytes=20 * MIB),
        cost_estimate=cost(2),
        name="shared_rows",
    )(jnp.stack([half, core]).astype(jnp.int32), grad_bc, grad_kv)


def products_kernel(count, *refs):
    out = refs[-1]
    total = dot(refs[0][...], refs[count][...], ((1,), (1,)))
    for i in range(1, count):
        total = total + dot(refs[i][...], refs[count + i][...], ((1,), (1,)))
    out[...] = total.astype(out.dtype)


def products(lefts, rights, dtype):
    length = lefts[0].shape[0]
    width = rights[0].shape[0]
    step = 256
    return pl.pallas_call(
        functools.partial(products_kernel, len(lefts)),
        grid=(length // step,),
        in_specs=[pl.BlockSpec((step, left.shape[1]), lambda i: (i, 0)) for left in lefts]
        + [pl.BlockSpec(right.shape, lambda i: (0, 0)) for right in rights],
        out_specs=pl.BlockSpec((step, width), lambda i: (i, 0)),
        out_shape=jax.ShapeDtypeStruct((length, width), dtype),
        compiler_params=pltpu.CompilerParams(vmem_limit_bytes=28 * MIB),
        cost_estimate=cost(6),
        name="products",
    )(*lefts, *rights)


def wide(mine, other, width):
    return jnp.concatenate([mine[:, :width], other[:, :width]], axis=1)


def body(
    tokens, segments, cotangent, gain_in, mamba_gate_weight, mamba_input_weight, w_dt, w_bc,
    convolution_input_taps, convolution_input_bias, conv_bc, conv_bc_bias, dt_bias, a_log, d_skip,
    w_q, w_k, w_v, w_o, mamba_output_weight, gain_ffn, w_gate, w_up, w_down,
):
    length = segments.shape[1]
    width = tokens.shape[1]
    rows_here = mamba_gate_weight.shape[0]
    dp = width // rows_here
    inner = mamba_gate_weight.shape[1]
    heads = w_dt.shape[1]
    qcols = w_q.shape[1]
    hidden_cols = w_gate.shape[1]
    slot = lax.axis_index("head")
    half = slot // 2
    core = slot % 2
    is_first = half == 0
    place_dp = lax.axis_index("dp")
    if dp == 8:
        route = jnp.stack([core, place_dp % 2] + [(place_dp // 2) ^ i for i in range(4)])
    else:
        route = jnp.concatenate([jnp.zeros((2,), jnp.int32), jnp.arange(4)])
    route = route.astype(jnp.int32)
    gain_in, gain_ffn = gain_in[None], gain_ffn[None]

    short = lambda value: value.astype(BF)
    first_core = core == 0
    flip = lambda tile: jnp.where(is_first, tile, jnp.concatenate([tile[:, HD:], tile[:, :HD]], axis=1))
    flips = lambda tile: jnp.concatenate([flip(tile[:, :128]), flip(tile[:, 128:])], axis=1)
    cols = ((0,), (0,))
    own = half[None].astype(jnp.int32)
    ringed = dp == 8
    order = Order()

    def tables(segments):
        seg = lax.dynamic_index_in_dim(segments, half, 0, keepdims=False)
        return segment_tables(seg) + rope_tables(length)

    def own_sums(mine, other):
        low, at = 2 * inner, 2 * inner + 2 * STATE
        return jnp.concatenate([
            mine[:, :inner] + other[:, inner:low], mine[:, low:at] + other[:, low:at],
            mine[:, at : at + heads] + other[:, at + heads : at + 2 * heads],
            jnp.zeros((8, 128 - heads), F32), mine[:, at + 128 :] + other[:, at + 128 :]], axis=1)

    piece1 = first_piece(slot, mamba_input_weight, w_dt, w_bc, w_k, w_v)
    rest = (mamba_gate_weight, w_q, mamba_output_weight, w_o, w_gate, w_up, w_down)
    shapes1 = ((0, inner + 128), (inner + 128, 128))
    shapes2 = shapes3 = ((0, inner), (inner, qcols))
    shapes4 = ((0, hidden_cols), (hidden_cols, hidden_cols))
    shapes5 = ((0, hidden_cols),)
    g1, g2, g3, g4, g5 = [Gather() for _ in range(5)]
    scan_params = (convolution_input_taps, convolution_input_bias, dt_bias, a_log, d_skip)
    if ringed:
        g1.along(piece1)
        held = order(g1.first, tokens, cotangent, segments, *rest, *scan_params)
        first1, tokens, cotangent, segments = held[:4]
        convolution_input_taps, convolution_input_bias, dt_bias, a_log, d_skip = held[11:]
        pieces = other_pieces(*held[4:11])
        pair1, *pieces = order(g1.join(first1), *pieces)
        g1.across(pair1)
        piece2, piece3, piece4, piece5 = pieces
        g2.along(piece2)
    else:
        pieces = (
            jnp.concatenate([short(mamba_gate_weight), short(w_q)], axis=1),
            jnp.concatenate([short(mamba_output_weight).T, short(w_o).T], axis=1),
            jnp.concatenate([short(w_gate), short(w_up)], axis=1), short(w_down).T)
        ways = [gather_whole(piece, dp, is_first) for piece in (piece1,) + pieces]
    rows_b, upstream, normed, scale, normed_t, upstream_t = load(tokens, cotangent, gain_in, own, length)
    aux, segrow, cosine, sine = tables(segments)
    seg_line = aux[:, 0][None]
    per_head = jnp.pad(jnp.stack([dt_bias, a_log, d_skip]), ((0, 5), (0, 128 - heads)))
    small = jnp.concatenate(
        [jnp.concatenate([convolution_input_taps, convolution_input_bias[None],
                          jnp.repeat(d_skip, HD)[None], jnp.zeros((2, inner), F32)], axis=0), per_head],
        axis=1)
    small_other = half_swap(small)
    xpar = jnp.concatenate([small[:, :inner], small_other[:, :inner]], axis=1)
    head_par = jnp.concatenate(
        [small[:2, inner : inner + heads], small_other[:2, inner : inner + heads],
         jnp.zeros((2, 128 - 2 * heads), F32)], axis=1)
    lane = jnp.arange(128) < 2 * heads
    hpar = jnp.concatenate(
        [head_par[:1], jnp.where(lane, -jnp.exp(head_par[1:]), 0.0), jnp.zeros((6, 128), F32)], axis=0)
    bcpar = jnp.concatenate([conv_bc, conv_bc_bias[None], jnp.zeros((3, conv_bc.shape[1]), F32)], axis=0)

    if ringed:
        second1, first2, normed, aux, cosine, sine, xpar, hpar = order(
            g1.second, g2.first, normed, aux, cosine, sine, xpar, hpar)
        quad1, pair2, piece3 = order(g1.join2(second1), g2.join(first2), piece3)
        g1.near_step(quad1)
        g2.across(pair2)
        g3.along(piece3)
        third1, second2, first3 = order(g1.third, g2.second, g3.first)
        near1, quad2, pair3, piece4 = order(g1.join3(third1), g2.join2(second2), g3.join(first3), piece4)
        g1.far_step(near1)
        g2.near_step(quad2)
        g3.across(pair3)
        g4.along(piece4)
        far1, third2, second3, first4 = order(g1.far, g2.third, g3.second, g4.first)
        near2, quad3, pair4, piece5 = order(g2.join3(third2), g3.join2(second3), g4.join(first4), piece5)
        g2.far_step(near2)
        g3.near_step(quad3)
        g4.across(pair4)
        g5.along(piece5)
        ways1 = (near1, far1)
    else:
        ways1 = ways[0]
    weight1, quarters = unpack(*ways1, route, shapes1)
    swap_halves = lambda tile: jnp.concatenate([tile[:, 128:], tile[:, :128]], axis=1)
    quarters = jnp.where(is_first, quarters, swap_halves(quarters))
    others = core_swap(quarters)
    h1 = dot(normed, weight1)
    c0 = jnp.where(first_core, quarters, others)
    c1 = jnp.where(first_core, others, quarters)
    weight_bc = jnp.concatenate([c0[:, :128], c1[:, :128]], axis=1)
    weight_kv = flips(jnp.concatenate([c0[:, 128:], c1[:, 128:]], axis=1))
    pair = dot(normed, weight_bc)
    keyvalue = short(dot(normed, weight_kv))
    if ringed:
        far2, third3, second4, first5, h1, pair, keyvalue = order(
            g2.far, g3.third, g4.second, g5.first, h1, pair, keyvalue)
        near3, quad4, pair5 = order(g3.join3(third3), g4.join2(second4), g5.join(first5))
        g3.far_step(near3)
        g4.near_step(quad4)
        g5.across(pair5)
        ways2 = (near2, far2)
    else:
        ways2 = ways[1]
    weight_z, weight_q = unpack(*ways2, route, shapes2)
    z = short(dot(normed, weight_z))
    qkv = jnp.concatenate([short(dot(normed, weight_q)), keyvalue], axis=1)

    attended, turned, lse = attention_forward(qkv, cosine, sine, aux, seg_line)
    if ringed:
        far3, third4, second5, attended, z = order(g3.far, g4.third, g5.second, attended, z)
        near4, quad5, z = order(g4.join3(third4), g5.join2(second5), z)
        g4.far_step(near4)
        g5.near_step(quad5)
        ways3 = (near3, far3)
    else:
        ways3 = ways[2]
    gated, scan, start = ssd_forward(h1, pair, z, aux, segrow, xpar, bcpar, hpar)
    weight_out, weight_o = unpack(*ways3, route, shapes3)
    mixed = products([gated, attended], [weight_out, weight_o], BF)
    mixed_got = core_swap(mixed)

    if ringed:
        third5, mixed = order(g5.third, mixed)
        near5 = order(g5.join3(third5))
        g5.far_step(near5)
        far4 = order(g4.far)
        ways4 = (near4, far4)
    else:
        ways4 = ways[3]
    weight_gate, weight_up = unpack(*ways4, route, shapes4)
    if ringed:
        weight_gate, weight_up, far5, mixed_got = order(weight_gate, weight_up, g5.far, mixed_got)
        ways5 = (near5, far5)
    else:
        ways5 = ways[4]
    (weight_down,) = unpack(*ways5, route, shapes5)
    state, normed_ffn_t, hidden, dgate, dup, whole, dnormed_part = feed_forward(
        rows_b, mixed, mixed_got, upstream, gain_ffn, weight_gate, weight_up, weight_down)
    whole_got = core_swap(whole)
    dnormed_got = core_swap(dnormed_part)
    down_pairs = [(upstream_t, hidden)]
    ffn_pairs = [(normed_ffn_t, dgate), (normed_ffn_t, dup)]
    if ringed:
        s5 = Scatter(down_pairs, route)
        send5, normed_ffn_t, whole_got = order(s5.send, normed_ffn_t, whole_got)
        s5.far_step(send5)
        ffn_pairs = [(normed_ffn_t, dgate), (normed_ffn_t, dup)]
        s4 = Scatter(ffn_pairs, route)
    out_mine = short(state + (long(whole) + long(whole_got)))
    if ringed:
        send4, got5, dnormed_got = order(s4.send, s5.got, dnormed_got)
        part5, send4, dnormed_got = order(s5.sum2(got5), send4, dnormed_got)
        s4.far_step(send4)
        s5.near_step(part5)
    dmixed, dgated, dz, datt, delta, gacc_ffn, dmixed_t = middle(
        state, upstream, dnormed_part, dnormed_got, gain_ffn, scan, z, attended, weight_out, weight_o)
    dqkv = attention_backward(qkv, turned, datt, lse, delta, cosine, sine, aux, seg_line)
    if ringed:
        dqkv, got4, got2_5, out_mine = order(dqkv, s4.got, s5.got2, out_mine)
        part4, dqkv, dz = order(s4.sum2(got4), dqkv, dz)
        s4.near_step(part4)
    dqry, dkv = dqkv[:, : 2 * qcols], dqkv[:, 2 * qcols :]
    second_pairs = [(dmixed_t, gated), (dmixed_t, attended), (normed_t, dz), (normed_t, dqry)]
    grad_kv = short(dot(normed_t, dkv))
    if ringed:
        s2 = Scatter(second_pairs, route)
        send2, got2_4, grad_kv = order(s2.send, s4.got2, grad_kv)
        third_4, send2, dgated = order(beside(s4.sum3(got2_4), s5.sum3(got2_5)), send2, dgated)
        s2.far_step(send2)
        got3_4 = dp_swap(third_4, BITS[1])
    dh1, dpair, acc = ssd_backward(
        h1, pair, z, dgated, start, aux, segrow, xpar, bcpar, hpar)
    if ringed:
        dh1, dpair, acc, got_2, got3_4 = order(dh1, dpair, acc, s2.got, got3_4)
        part2, fourth_4, dh1, dpair, out_part, acc = order(
            s2.sum2(got_2),
            beside(s4.sum4(got3_4[:, : 2 * hidden_cols]), s5.sum4(got3_4[:, 2 * hidden_cols :])),
            dh1, dpair, part_of(out_mine, core), jnp.concatenate([acc, gacc_ffn], axis=1))
        s2.near_step(part2)
        got4_4 = dp_swap(fourth_4, BITS[0])
        acc_got = dp_swap(acc, BITS[1])
    else:
        acc = jnp.concatenate([acc, gacc_ffn], axis=1)
        out_part = part_of(out_mine, core)
    out_got = half_swap(out_part)

    grad_bc = short(dot(normed_t, dpair))
    keep_shared, send_shared = shared_rows(grad_bc, flips(grad_kv), half, core)
    shared_got = core_swap(send_shared)
    dnormed_part = products(
        [dh1, dpair, dz, dqry, dkv], [weight1, weight_bc, weight_z, weight_q, weight_kv], BF)
    dnormed_send = part_of(dnormed_part, 1 - core)
    dnormed_own = part_of(dnormed_part, core)
    if ringed:
        dnormed_send, dnormed_own, got2_2, got4_4, shared_got, acc = order(
            dnormed_send, dnormed_own, s2.got2, got4_4, shared_got, acc + acc_got)
        third_2, acc, dnormed_send = order(s2.sum3(got2_2), acc, dnormed_send)
        acc_got = dp_swap(acc, BITS[0])
        s2.across(third_2)
    dnormed_got = core_swap(dnormed_send)
    grad_shared = short(long(keep_shared) + long(shared_got))
    last_pairs = [(normed_t, dh1), (None, grad_shared)]
    if ringed:
        s1 = Scatter(last_pairs, route)
        send1, acc, out_got = order(s1.send, acc + acc_got, out_got)
        s1.far_step(send1)
        acc_got = half_swap(acc)
        sent4 = s4.result(got4_4[:, : 2 * hidden_cols])
        sent5 = s5.result(got4_4[:, 2 * hidden_cols :]).T
    grad_mine, gacc_in = last_norm(
        dnormed_own, dnormed_got, part_of(rows_b, core), part_of(dmixed, core), part_of(scale, core), gain_in)
    if ringed:
        grad_mine, gacc_in, sent4, sent5 = order(grad_mine, gacc_in, sent4, sent5)
        gacc_in, got3_2 = order(gacc_in + core_swap(gacc_in), s2.got3)
        fourth_2, gacc_in = order(s2.sum4(got3_2), gacc_in)
        s2.along(fourth_2)
        gains_got = half_swap(gacc_in)
        out_got2 = core_swap(out_got)
        output = store([out_mine, out_got, out_got2], half, core)
        got_1, output, acc, gacc_in = order(s1.got, output, own_sums(acc, acc_got), gacc_in + gains_got)
        part1, gacc_in, acc = order(s1.sum2(got_1), gacc_in, acc)
        gains_got = dp_swap(gacc_in, BITS[2])
        acc_got = dp_swap(acc, BITS[2])
        s1.near_step(part1)
        grad_got = half_swap(grad_mine)
        got2_1, gacc_in, acc = order(s1.got2, gacc_in + gains_got, acc + acc_got)
        bc_got = core_swap(acc[:, inner : inner + 2 * STATE])
        blocks = gacc_in[0].reshape(4, 2 * rows_here)
        gain_rows = jnp.concatenate([
            lax.dynamic_slice(blocks, ((place_dp // 2) ^ i, (place_dp % 2) * rows_here), (1, rows_here))
            for i in range(4)], axis=1).reshape(-1, 1)
        s1.extra = jnp.pad(gain_rows, ((0, 0), (inner + 2 * heads, 256 - 2 * heads - 1)))
        third_1 = order(s1.sum3(got2_1))
        s1.across(third_1)
        sent2 = s2.result(s2.got4)
        got3_1, sent2, grad_got, bc_got = order(s1.got3, sent2, grad_got, bc_got)
        fourth_1, grad_got = order(s1.sum4(got3_1), grad_got)
        s1.along(fourth_1)
        grad_near, grad_got2 = core_swap(grad_mine), core_swap(grad_got)
        grad_near, grad_got2 = order(grad_near, grad_got2)
        grad_tokens = store([grad_mine, grad_near, grad_got, grad_got2], half, core)
        sent1 = s1.result(s1.got4)
        gain_grads_in = sent1[:, inner + 2 * heads]
    else:
        acc = lax.psum(acc, "dp")
        acc = own_sums(acc, half_swap(acc))
        bc_got = core_swap(acc[:, inner : inner + 2 * STATE])
        gain_sums = lax.psum(gacc_in[0], ("dp", "head"))
        gain_grads_in = lax.dynamic_slice_in_dim(gain_sums, place_dp * rows_here, rows_here, 0)
        sent5, sent4, sent2, sent1 = [
            scatter_whole(pairs, dp, is_first)
            for pairs in (down_pairs, ffn_pairs, second_pairs, last_pairs)]
        sent5 = sent5.T
        grad_got = half_swap(grad_mine)
        output = store([out_mine, out_got, core_swap(out_got)], half, core)
        grad_tokens = store([grad_mine, core_swap(grad_mine), grad_got, core_swap(grad_got)], half, core)
    sent3, sent2 = sent2[:, : inner + qcols], sent2[:, inner + qcols :]
    steps_at = inner + 2 * STATE
    own = acc[:, :inner]
    skip = own[5].reshape(heads, HD).sum(axis=-1)
    rank = place_dp * 4 + slot
    many = conv_bc.shape[1] // (4 * dp)
    bc_own = lax.dynamic_slice_in_dim(acc[:, inner:steps_at] + bc_got, rank * many, many, 1)
    per = acc[:2, steps_at : steps_at + heads]
    gain_grads_ffn = lax.dynamic_slice_in_dim(acc[0, steps_at + 128 :], place_dp * rows_here, rows_here, 0)
    quarter_rows = rows_here // 4
    shared_own = sent1[:, inner + 128 :].reshape(4, quarter_rows, 128).swapaxes(0, 1).reshape(quarter_rows, -1)
    return (
        output,
        grad_tokens,
        gain_grads_in,
        sent2[:, :inner],
        sent1[:, :inner],
        sent1[:, inner : inner + heads] + sent1[:, inner + heads : inner + 2 * heads],
        shared_own[:, : 2 * STATE],
        own[:4],
        own[4],
        bc_own[:4],
        bc_own[4],
        per[0],
        per[1],
        skip,
        sent2[:, inner:],
        shared_own[:, 2 * STATE : 2 * STATE + 128],
        shared_own[:, 2 * STATE + 128 :],
        sent3[:, inner:].T,
        sent3[:, :inner].T,
        gain_grads_ffn,
        sent4[:, :hidden_cols],
        sent4[:, hidden_cols:],
        sent5,
    )


def solution(mesh):
    in_specs = (
        P("dp", None),
        P("dp", None),
        P("dp", None),
        P(),
        P("dp", "head"),
        P("dp", "head"),
        P("dp", "head"),
        P("dp", None),
        P(None, "head"),
        P("head"),
        P(),
        P(),
        P("head"),
        P("head"),
        P("head"),
        P("dp", "head"),
        P("dp", None),
        P("dp", None),
        P("head", "dp"),
        P("head", "dp"),
        P(),
        P("dp", "head"),
        P("dp", "head"),
        P("head", "dp"),
    )
    out_specs = (
        P("dp", None),
        P("dp", None),
        P("dp"),
        P("dp", "head"),
        P("dp", "head"),
        P("dp", "head"),
        P(("dp", "head"), None),
        P(None, "head"),
        P("head"),
        P(None, ("dp", "head")),
        P(("dp", "head")),
        P("head"),
        P("head"),
        P("head"),
        P("dp", "head"),
        P(("dp", "head"), None),
        P(("dp", "head"), None),
        P("head", "dp"),
        P("head", "dp"),
        P("dp"),
        P("dp", "head"),
        P("dp", "head"),
        P("head", "dp"),
    )
    return jax.shard_map(body, mesh=mesh, in_specs=in_specs, out_specs=out_specs, check_vma=False)
```

```python
import functools
import math

import jax
import jax.numpy as jnp
from jax import lax
from jax.experimental import pallas as pl
from jax.experimental.pallas import tpu as pltpu
from jax.sharding import PartitionSpec as P

QHEADS = 8
KVHEADS = 2
HD = 64
STATE = 128
CHUNK = 128
TAPS = 4
EPSILON = 1e-05
THETA = 100000000000.0
NEG = -1e30
HIGHEST = lax.Precision.HIGHEST
BF = jnp.bfloat16
F32 = jnp.float32
MIB = 1024 * 1024


def cost(micros):
    return pl.CostEstimate(flops=0, transcendentals=0, bytes_accessed=int(micros * 1.107e6))


def dot(left, right, dims=((1,), (0,))):
    return lax.dot_general(left, right, (dims, ((), ())), preferred_element_type=F32)


def dot_exact(left, right):
    return lax.dot_general(
        left, right, (((1,), (0,)), ((), ())), precision=HIGHEST, preferred_element_type=F32
    )


def sigmoid(values):
    return 0.5 + 0.5 * jnp.tanh(0.5 * values)


def pick(low_half, table, first):
    return jnp.where(low_half, table[:, first : first + 1], table[:, first + 1 : first + 2])


def halves(low_half, tile):
    zero = jnp.zeros_like(tile)
    return jnp.concatenate(
        [jnp.where(low_half, tile, zero), jnp.where(low_half, zero, tile)], axis=0
    )


def ssd_tables(dt_raw, dt_bias, rate, emask, fmask, total, lower):
    step = jnp.log1p(jnp.exp(dt_raw + dt_bias))
    decay = dot_exact(lower, step * rate)
    last = decay[CHUNK - 1 : CHUNK, :]
    enter = jnp.exp(decay) * emask
    leave = jnp.exp(last - decay) * fmask
    whole = jnp.exp(last) * total
    return step, decay, enter, leave, whole


def shifted_rows(buf, cols, keeps):
    return [keep * buf[8 - k : 8 - k + CHUNK, cols] for k, keep in enumerate(keeps, 1)]


def conv_rows(now, shifted, taps, bias):
    result = bias + taps[0:1] * now
    for k, earlier in enumerate(shifted, 1):
        result = result + taps[k : k + 1] * earlier
    return result


def column(table, at):
    return jnp.broadcast_to(table[:, at : at + 1], (table.shape[0], 128))


def wide_column(tile):
    return jnp.concatenate([tile, tile], axis=1)


def head_lanes(inner):
    head = lax.broadcasted_iota(jnp.int32, (128, inner), 0)
    channel = lax.broadcasted_iota(jnp.int32, (128, inner), 1)
    return (head == channel // 64).astype(BF)


def spread(table, lanes2):
    high = table.astype(BF)
    rest = (table - high.astype(F32)).astype(BF)
    return dot(jnp.concatenate([high, rest], axis=1), lanes2)


def place_of(cols, inner):
    return slice(cols.start + 128 * (2 * cols.start // inner), cols.stop + 128 * (2 * cols.start // inner))


def steps_of(h_ref, inner, lane, heads):
    mid = inner // 2
    mine, other = h_ref[:, mid : mid + 128], h_ref[:, inner + 128 :]
    return jnp.where(lane < heads, mine, jnp.where(lane < 2 * heads, other, 0.0))


def ssd_forward_kernel(
    h_ref, pair_ref, z_ref, aux_ref, segrow_ref, xpar_ref, bcpar_ref, hpar_ref,
    gated_ref, scan_ref, start_ref, xbuf, pbuf, state, lanes2, step_s, enter_s, leave_s,
):
    inner = z_ref.shape[1]
    pairs = inner // 128
    lane = lax.broadcasted_iota(jnp.int32, (CHUNK, 128), 1)
    sub = lax.broadcasted_iota(jnp.int32, (CHUNK, 128), 0)
    low_half = lane < 64

    @pl.when(pl.program_id(0) == 0)
    def _():
        xbuf[0:8, :] = jnp.zeros((8, inner), F32)
        pbuf[0:8, :] = jnp.zeros((8, 2 * STATE), F32)
        state[...] = jnp.zeros_like(state)
        lanes2[0:128, :] = head_lanes(inner)
        lanes2[128:256, :] = head_lanes(inner)

    for first in (0, inner // 2):
        cols = slice(first, first + inner // 2)
        xbuf[8 : 8 + CHUNK, cols] = h_ref[:, place_of(cols, inner)]
    pbuf[8 : 8 + CHUNK, :] = pair_ref[...]
    aux = aux_ref[...]
    keeps = [column(aux, k) for k in range(1, TAPS)]
    pre_pair = conv_rows(
        pbuf[8 : 8 + CHUNK, :], shifted_rows(pbuf, slice(None), [wide_column(v) for v in keeps]),
        bcpar_ref[0:4, :], bcpar_ref[4:5, :])
    act_pair = pre_pair * sigmoid(pre_pair)
    in_b = act_pair[:, :STATE].astype(BF)
    out_c = act_pair[:, STATE:].astype(BF)
    inter = dot(out_c, in_b, ((1,), (1,)))
    allowed = (sub >= lane) & (column(aux, 0) == segrow_ref[0])
    hide = jnp.where(allowed, 0.0, NEG)
    lower = (sub >= lane).astype(F32)
    emask = aux[:, 7:8]
    step, decay, enter, leave, whole = ssd_tables(
        steps_of(h_ref, inner, lane, pairs), hpar_ref[0:1, :], hpar_ref[1:2, :],
        emask, aux[:, 8:9], emask[CHUNK - 1 : CHUNK, :], lower,
    )
    step_s[...] = spread(step, lanes2[...])
    enter_s[...] = spread(enter, lanes2[...])
    leave_s[...] = spread(leave, lanes2[...])
    decay_t = decay.T
    start = state[...].astype(BF)
    start_ref[...] = start
    enter_s[...] = dot(out_c, start) * enter_s[...]
    for p in range(pairs):
        cols = slice(128 * p, 128 * p + 128)
        pre = conv_rows(
            xbuf[8 : 8 + CHUNK, cols], shifted_rows(xbuf, cols, keeps),
            xpar_ref[0:4, cols], xpar_ref[4:5, cols])
        act = pre * sigmoid(pre)
        driven = (step_s[:, cols] * act).astype(BF)
        mixes = []
        for head in (2 * p, 2 * p + 1):
            gap = column(decay, head) - decay_t[head : head + 1, :]
            mixes.append((inter * jnp.exp(gap + hide)).astype(BF))
        scanned = dot(jnp.concatenate(mixes, axis=1), halves(low_half, driven))
        scanned = scanned + enter_s[:, cols] + xpar_ref[5:6, cols] * act
        scan_ref[:, cols] = scanned.astype(scan_ref.dtype)
        gate = z_ref[:, cols].astype(F32)
        gated_ref[:, cols] = (scanned * (gate * sigmoid(gate))).astype(BF)
        sent = (leave_s[:, cols] * driven.astype(F32)).astype(BF)
        state[:, cols] = pick(low_half[0:1], whole, 2 * p) * state[:, cols] + dot(
            in_b, sent, ((0,), (0,))
        )
    xbuf[0:8, :] = xbuf[CHUNK : CHUNK + 8, :]
    pbuf[0:8, :] = pbuf[CHUNK : CHUNK + 8, :]


def ssd_forward(h1, pair, z, aux, segrow, xpar, bcpar, hpar):
    length, inner = z.shape
    chunks = length // CHUNK
    width = h1.shape[1]
    whole = lambda arr: pl.BlockSpec(arr.shape, lambda c: (0,) * arr.ndim)
    rows = lambda cols: pl.BlockSpec((CHUNK, cols), lambda c: (c, 0))
    return pl.pallas_call(
        ssd_forward_kernel,
        grid=(chunks,),
        in_specs=[
            rows(width), rows(2 * STATE), rows(inner), rows(128),
            pl.BlockSpec((1, 1, CHUNK), lambda c: (c, 0, 0)),
            whole(xpar), whole(bcpar), whole(hpar),
        ],
        out_specs=[rows(inner), rows(inner), rows(inner)],
        out_shape=[
            jax.ShapeDtypeStruct((length, inner), BF),
            jax.ShapeDtypeStruct((length, inner), BF),
            jax.ShapeDtypeStruct((chunks * STATE, inner), BF),
        ],
        scratch_shapes=[
            pltpu.VMEM((CHUNK + 8, inner), F32),
            pltpu.VMEM((CHUNK + 8, 2 * STATE), F32),
            pltpu.VMEM((STATE, inner), F32),
            pltpu.VMEM((256, inner), BF),
            pltpu.VMEM((CHUNK, inner), F32),
            pltpu.VMEM((CHUNK, inner), F32),
            pltpu.VMEM((CHUNK, inner), F32),
        ],
        compiler_params=pltpu.CompilerParams(vmem_limit_bytes=20 * MIB),
        cost_estimate=cost(10),
        name="ssd_forward",
    )(h1, pair, z, aux, segrow, xpar, bcpar, hpar)


def ssd_backward_kernel(
    h_ref, prev_ref, pair_ref, pair_prev_ref, z_ref, dgated_ref, start_ref, aux_ref,
    segrow_ref, xpar_ref, bcpar_ref, hpar_ref,
    dh_ref, dpair_ref, acc_ref,
    xbuf, pbuf, dxbuf, dpbuf, dstate, lanes2, step_s, enter_s, leave_s, came_s, dcame_s, sent_s,
    direct_s, inter_s, row_s, across_s,
):
    inner = z_ref.shape[1]
    pairs = inner // 128
    lane = lax.broadcasted_iota(jnp.int32, (CHUNK, 128), 1)
    sub = lax.broadcasted_iota(jnp.int32, (CHUNK, 128), 0)
    low_half = lane < 64
    low_row = low_half[0:1]

    @pl.when(pl.program_id(0) == 0)
    def _():
        dxbuf[CHUNK : CHUNK + 8, :] = jnp.zeros((8, inner), F32)
        dpbuf[CHUNK : CHUNK + 8, :] = jnp.zeros((8, 2 * STATE), F32)
        dstate[...] = jnp.zeros_like(dstate)
        acc_ref[...] = jnp.zeros_like(acc_ref)
        across_s[...] = jnp.zeros_like(across_s)
        lanes2[0:128, :] = head_lanes(inner)
        lanes2[128:256, :] = head_lanes(inner)

    for first in (0, inner // 2):
        cols = slice(first, first + inner // 2)
        xbuf[0:8, cols] = prev_ref[:, place_of(cols, inner)]
        xbuf[8 : 8 + CHUNK, cols] = h_ref[:, place_of(cols, inner)]
    pbuf[0:8, :] = pair_prev_ref[...]
    pbuf[8 : 8 + CHUNK, :] = pair_ref[...]
    aux = aux_ref[...]
    keeps = [column(aux, k) for k in range(1, TAPS)]
    later = [column(aux, 3 + k) for k in range(1, TAPS)]
    shifted_pair = shifted_rows(pbuf, slice(None), [wide_column(v) for v in keeps])
    pre_pair = conv_rows(
        pbuf[8 : 8 + CHUNK, :], shifted_pair, bcpar_ref[0:4, :], bcpar_ref[4:5, :])
    sig_pair = sigmoid(pre_pair)
    act_pair = pre_pair * sig_pair
    in_b = act_pair[:, :STATE].astype(BF)
    out_c = act_pair[:, STATE:].astype(BF)
    inter_t = dot(in_b, out_c, ((1,), (1,)))
    allowed_t = (lane >= sub) & (column(aux, 0) == segrow_ref[0])
    hide_t = jnp.where(allowed_t, 0.0, NEG)
    lower = sub >= lane
    emask = aux[:, 7:8]
    rate = hpar_ref[1:2, :]
    dt_raw = steps_of(h_ref, inner, lane, pairs)
    step, decay, enter, leave, whole = ssd_tables(
        dt_raw, hpar_ref[0:1, :], rate,
        emask, aux[:, 8:9], emask[CHUNK - 1 : CHUNK, :], lower.astype(F32),
    )
    step_s[...] = spread(step, lanes2[...])
    enter_s[...] = spread(enter, lanes2[...])
    leave_s[...] = spread(leave, lanes2[...])
    came_s[...] = dot(out_c, start_ref[...]) * enter_s[...]
    leave_b = leave_s[...]
    row_s[...] = (dot(in_b, dstate[...].astype(BF)) * leave_b).astype(BF)
    decay_t = decay.T
    lower_b = lower.astype(BF)
    grad_inter_t = jnp.zeros((CHUNK, 128), F32)
    row_list = []
    for p in range(pairs):
        cols = slice(128 * p, 128 * p + 128)
        shifted = shifted_rows(xbuf, cols, keeps)
        now = xbuf[8 : 8 + CHUNK, cols]
        pre = conv_rows(now, shifted, xpar_ref[0:4, cols], xpar_ref[4:5, cols])
        sig = sigmoid(pre)
        act = pre * sig
        gate = z_ref[:, cols].astype(F32)
        dscan = (dgated_ref[:, cols].astype(F32) * (gate * sigmoid(gate))).astype(BF)
        dscan_f = dscan.astype(F32)
        step_p = step_s[:, cols]
        driven = (step_p * act).astype(BF)
        zero_b = jnp.zeros_like(driven)
        mixes = []
        for head in (2 * p, 2 * p + 1):
            gap = decay_t[head : head + 1, :] - column(decay, head)
            damp = jnp.exp(gap + hide_t)
            mixed = inter_t * damp
            mixes.append(mixed.astype(BF))
            own = jnp.where(low_half == (head % 2 == 0), driven, zero_b)
            grad_mix = dot(own, dscan, ((1,), (1,)))
            grad_inter_t = grad_inter_t + grad_mix * damp
            flow = dot((grad_mix * mixed).astype(BF), lower_b)
            row_list.append(jnp.sum(jnp.where(lane > sub, flow, 0.0), axis=0, keepdims=True))
        from_inter = row_s[:, cols].astype(F32)
        ddriven = dot(jnp.concatenate(mixes, axis=1), halves(low_half, dscan)) + from_inter
        dact = xpar_ref[5:6, cols] * dscan_f + step_p * ddriven
        direct_s[:, cols] = (act * ddriven).astype(BF)
        inter_s[:, cols] = (act * from_inter).astype(BF)
        row_s[:, cols] = (dscan_f * came_s[:, cols]).astype(BF)
        dst = dstate[:, cols]
        whole_p = pick(low_row, whole, 2 * p)
        across_s[0:1, cols] = whole_p * jnp.sum(
            dst * start_ref[:, cols].astype(F32), axis=0, keepdims=True)
        dcame_s[:, cols] = (enter_s[:, cols] * dscan_f).astype(BF)
        sent_s[:, cols] = (leave_s[:, cols] * driven.astype(F32)).astype(BF)
        dpre = dact * (sig * (1.0 + pre * (1.0 - sig)))
        dxbuf[0:CHUNK, cols] = dpre
        dval = xpar_ref[0:1, cols] * dpre
        sums = [jnp.sum(dpre * now, axis=0, keepdims=True)]
        for k in range(1, TAPS):
            dval = dval + xpar_ref[k : k + 1, cols] * (later[k - 1] * dxbuf[k : k + CHUNK, cols])
            sums.append(jnp.sum(dpre * shifted[k - 1], axis=0, keepdims=True))
        sums.append(jnp.sum(dpre, axis=0, keepdims=True))
        sums.append(jnp.sum(dscan_f * act, axis=0, keepdims=True))
        sums.append(jnp.zeros((2, 128), F32))
        acc_ref[:, cols] += jnp.concatenate(sums, axis=0)
        dh_ref[:, place_of(cols, inner)] = dval.astype(BF)
    dxbuf[CHUNK : CHUNK + 8, :] = dxbuf[0:8, :]
    grad_inter_b = grad_inter_t.astype(BF)
    dstate_b = dstate[...].astype(BF)
    grad_b = dot(grad_inter_b, out_c) + dot(sent_s[...], dstate_b, ((1,), (1,)))
    grad_c = dot(grad_inter_b, in_b, ((0,), (0,))) + dot(dcame_s[...], start_ref[...], ((1,), (1,)))
    for p in range(pairs):
        cols = slice(128 * p, 128 * p + 128)
        dstate[:, cols] = pick(low_row, whole, 2 * p) * dstate[:, cols] + dot(
            out_c, dcame_s[:, cols], ((0,), (0,)))
    grad_act = jnp.concatenate([grad_b, grad_c], axis=1)
    dpre = grad_act * (sig_pair * (1.0 + pre_pair * (1.0 - sig_pair)))
    dpbuf[0:CHUNK, :] = dpre
    dval = bcpar_ref[0:1, :] * dpre
    sums = [jnp.sum(dpre * pbuf[8 : 8 + CHUNK, :], axis=0, keepdims=True)]
    for k in range(1, TAPS):
        dval = dval + bcpar_ref[k : k + 1, :] * (wide_column(later[k - 1]) * dpbuf[k : k + CHUNK, :])
        sums.append(jnp.sum(dpre * shifted_pair[k - 1], axis=0, keepdims=True))
    sums.append(jnp.sum(dpre, axis=0, keepdims=True))
    sums.append(jnp.zeros((3, 2 * STATE), F32))
    acc_ref[:, inner : inner + 2 * STATE] += jnp.concatenate(sums, axis=0)
    dpair_ref[...] = dval.astype(BF)
    dpbuf[CHUNK : CHUNK + 8, :] = dpbuf[0:8, :]
    lanes = lanes2[0:128, :]
    by_head = lambda value: dot(value, lanes, ((1,), (1,)))
    direct = by_head(direct_s[...])
    direct_inter = by_head(inter_s[...])
    row_inter = by_head(row_s[...])
    across = lax.dot_general(
        across_s[...], lanes.astype(F32), (((1,), (1,)), ((), ())), precision=HIGHEST,
        preferred_element_type=F32)[0:1]
    rows = jnp.concatenate(row_list + [jnp.zeros((CHUNK - 2 * pairs, 128), F32)], axis=0).T
    upper_b = (sub <= lane).astype(BF)
    strict_b = (sub > lane).astype(BF)
    grad_decay = rows + across + dot(upper_b, row_inter.astype(BF))
    grad_decay = grad_decay + dot(strict_b, (step * direct_inter).astype(BF))
    dstep = direct + grad_decay * rate
    draw = dstep * sigmoid(dt_raw + hpar_ref[0:1, :])
    acc_ref[:, inner + 2 * STATE :] += jnp.concatenate([
        jnp.sum(draw, axis=0, keepdims=True),
        jnp.sum(grad_decay * step, axis=0, keepdims=True) * rate,
        jnp.zeros((6, 128), F32)], axis=0)
    mid = inner // 2
    dh_ref[:, mid : mid + 128] = jnp.where(lane < pairs, draw, 0.0).astype(BF)
    dh_ref[:, inner + 128 :] = jnp.where(lane >= pairs, draw, 0.0).astype(BF)


def ssd_backward(h1, pair, z, dgated, start, aux, segrow, xpar, bcpar, hpar):
    length, inner = z.shape
    chunks = length // CHUNK
    width = h1.shape[1]
    whole = lambda arr: pl.BlockSpec(arr.shape, lambda c: (0,) * arr.ndim)
    rows = lambda cols: pl.BlockSpec((CHUNK, cols), lambda c: (chunks - 1 - c, 0))
    before = lambda cols: pl.BlockSpec(
        (8, cols), lambda c: (jnp.maximum((chunks - 1 - c) * (CHUNK // 8) - 1, 0), 0))
    fixed = lambda r, cols: pl.BlockSpec((r, cols), lambda c: (0, 0))
    return pl.pallas_call(
        ssd_backward_kernel,
        grid=(chunks,),
        in_specs=[
            rows(width), before(width), rows(2 * STATE), before(2 * STATE),
            rows(inner), rows(inner), rows(inner), rows(128),
            pl.BlockSpec((1, 1, CHUNK), lambda c: (chunks - 1 - c, 0, 0)),
            whole(xpar), whole(bcpar), whole(hpar),
        ],
        out_specs=[
            rows(width), rows(2 * STATE),
            fixed(8, inner + 2 * STATE + 128),
        ],
        out_shape=[
            jax.ShapeDtypeStruct((length, width), BF),
            jax.ShapeDtypeStruct((length, 2 * STATE), BF),
            jax.ShapeDtypeStruct((8, inner + 2 * STATE + 128), F32),
        ],
        scratch_shapes=[
            pltpu.VMEM((CHUNK + 8, inner), F32),
            pltpu.VMEM((CHUNK + 8, 2 * STATE), F32),
            pltpu.VMEM((CHUNK + 8, inner), F32),
            pltpu.VMEM((CHUNK + 8, 2 * STATE), F32),
            pltpu.VMEM((STATE, inner), F32),
            pltpu.VMEM((256, inner), BF),
            pltpu.VMEM((CHUNK, inner), F32),
            pltpu.VMEM((CHUNK, inner), F32),
            pltpu.VMEM((CHUNK, inner), F32),
            pltpu.VMEM((CHUNK, inner), F32),
            pltpu.VMEM((CHUNK, inner), BF),
            pltpu.VMEM((CHUNK, inner), BF),
            pltpu.VMEM((CHUNK, inner), BF),
            pltpu.VMEM((CHUNK, inner), BF),
            pltpu.VMEM((CHUNK, inner), BF),
            pltpu.VMEM((8, inner), F32),
        ],
        compiler_params=pltpu.CompilerParams(vmem_limit_bytes=20 * MIB),
        cost_estimate=cost(28),
        name="ssd_backward",
    )(h1, h1, pair, pair, z, dgated, start, aux, segrow, xpar, bcpar, hpar)


def segment_tables(seg):
    length = seg.shape[0]
    chunks = length // CHUNK
    value = seg.astype(F32)
    far = jnp.full((TAPS,), -1.0, F32)
    cols = [value]
    for k in range(1, TAPS):
        cols.append((value == jnp.concatenate([far[:k], value[:-k]])).astype(F32))
    for k in range(1, TAPS):
        cols.append((value == jnp.concatenate([value[k:], far[:k]])).astype(F32))
    by_chunk = value.reshape(chunks, CHUNK)
    ends = by_chunk[:, -1:]
    before = jnp.concatenate([far[:1, None], ends[:-1]], axis=0)
    cols.append((by_chunk == before).astype(F32).reshape(-1))
    cols.append((by_chunk == ends).astype(F32).reshape(-1))
    aux = jnp.stack(cols, axis=1)
    return jnp.pad(aux, ((0, 0), (0, 128 - aux.shape[1]))), by_chunk[:, None, :]


BLOCK = 256
REACH = 512


def rope_tables(length):
    position = jnp.arange(length).astype(F32)
    freqs = jnp.exp(-(jnp.arange(0, HD, 2).astype(F32) / HD) * math.log(THETA))
    angle = position[:, None] * freqs[None, :]
    cosine, sine = jnp.cos(angle), jnp.sin(angle)
    return (
        jnp.concatenate([cosine] * 4, axis=1),
        jnp.concatenate([-sine, sine, -sine, sine], axis=1),
    )


def turn(values, cosine, sine):
    lane = lax.broadcasted_iota(jnp.int32, values.shape, 1)
    swapped = jnp.where(
        lane % HD < HD // 2, pltpu.roll(values, 128 - HD // 2, 1), pltpu.roll(values, HD // 2, 1)
    )
    return values * cosine + swapped * sine


def attention_forward_kernel(
    qkv_ref, cos_ref, sin_ref, segcol_ref, segrow_ref, out_ref, turned_ref, lse_ref
):
    length = qkv_ref.shape[0]
    groups = KVHEADS
    cosine, sine = cos_ref[...], sin_ref[...]
    for t in range(groups + 1):
        cols = slice(128 * t, 128 * t + 128)
        turned_ref[:, cols] = turn(qkv_ref[:, cols].astype(F32), cosine, sine).astype(BF)
    key_at, value_at = 128 * groups, 128 * (groups + 1)
    lane = lax.broadcasted_iota(jnp.int32, (BLOCK, 128), 1)
    for b in range(length // BLOCK):
        rows = slice(b * BLOCK, (b + 1) * BLOCK)
        first = max(0, b * BLOCK - REACH)
        keys = slice(first, (b + 1) * BLOCK)
        many = (b + 1) * BLOCK - first
        at_row = lax.broadcasted_iota(jnp.int32, (BLOCK, many), 0) + b * BLOCK
        at_col = lax.broadcasted_iota(jnp.int32, (BLOCK, many), 1) + first
        allowed = (at_row >= at_col) & (segcol_ref[rows, 0:1] == segrow_ref[:, keys])
        lse = jnp.zeros((BLOCK, 128), F32)
        for g in range(groups):
            key = turned_ref[keys, key_at + 64 * g : key_at + 64 * g + 64]
            value = qkv_ref[keys, value_at + 64 * g : value_at + 64 * g + 64]
            parts = []
            for s in range(2):
                query = turned_ref[rows, 128 * g + 64 * s : 128 * g + 64 * s + 64]
                scores = dot(query, key, ((1,), (1,))) * HD ** (-0.5)
                scores = jnp.where(allowed, scores, NEG)
                peak = jnp.max(scores, axis=1, keepdims=True)
                weights = jnp.exp(scores - peak)
                total = jnp.sum(weights, axis=1, keepdims=True)
                probs = (weights * (1.0 / total)).astype(BF)
                parts.append(dot(probs, value))
                lse = jnp.where(lane == 2 * g + s, peak + jnp.log(total), lse)
            out_ref[rows, 128 * g : 128 * g + 128] = jnp.concatenate(parts, axis=1).astype(BF)
        lse_ref[:, rows] = lse.T[0:8, :]


def attention_forward(qkv, cosine, sine, aux, segrow):
    length = qkv.shape[0]
    return pl.pallas_call(
        attention_forward_kernel,
        out_shape=[
            jax.ShapeDtypeStruct((length, 128 * KVHEADS), BF),
            jax.ShapeDtypeStruct((length, 128 * (KVHEADS + 1)), BF),
            jax.ShapeDtypeStruct((8, length), F32),
        ],
        compiler_params=pltpu.CompilerParams(vmem_limit_bytes=20 * MIB),
        cost_estimate=cost(8),
        name="attention_forward",
    )(qkv, cosine, sine, aux, segrow)


def attention_backward_kernel(
    qkv_ref, turned_ref, datt_ref, lse_ref, delta_ref, cos_ref, sin_ref, segcol_ref, segrow_ref,
    dqkv_ref, dkey, dvalue,
):
    length = qkv_ref.shape[0]
    groups = KVHEADS
    key_at, value_at = 128 * groups, 128 * (groups + 1)
    dkey[...] = jnp.zeros_like(dkey)
    dvalue[...] = jnp.zeros_like(dvalue)
    for b in range(length // BLOCK):
        rows = slice(b * BLOCK, (b + 1) * BLOCK)
        first = max(0, b * BLOCK - REACH)
        keys = slice(first, (b + 1) * BLOCK)
        many = (b + 1) * BLOCK - first
        at_key = lax.broadcasted_iota(jnp.int32, (many, BLOCK), 0) + first
        at_row = lax.broadcasted_iota(jnp.int32, (many, BLOCK), 1) + b * BLOCK
        allowed = (at_row >= at_key) & (segcol_ref[keys, 0:1] == segrow_ref[:, rows])
        dquery = []
        for g in range(groups):
            key = turned_ref[keys, key_at + 64 * g : key_at + 64 * g + 64]
            value = qkv_ref[keys, value_at + 64 * g : value_at + 64 * g + 64]
            dk = jnp.zeros((many, HD), F32)
            dv = jnp.zeros((many, HD), F32)
            for s in range(2):
                head = 2 * g + s
                half = slice(128 * g + 64 * s, 128 * g + 64 * s + 64)
                query = turned_ref[rows, half]
                datt = datt_ref[rows, half]
                scores = dot(key, query, ((1,), (1,))) * HD ** (-0.5)
                probs = jnp.exp(jnp.where(allowed, scores, NEG) - lse_ref[head : head + 1, rows])
                dprobs = dot(value, datt, ((1,), (1,)))
                dscores = (probs * (dprobs - delta_ref[head : head + 1, rows])).astype(BF)
                dk = dk + dot(dscores, query)
                dv = dv + dot(probs.astype(BF), datt)
                dquery.append(dot(dscores, key, ((0,), (0,))) * HD ** (-0.5))
            dkey[keys, 64 * g : 64 * g + 64] += dk * HD ** (-0.5)
            dvalue[keys, 64 * g : 64 * g + 64] += dv
        for g in range(groups):
            tile = jnp.concatenate([dquery[2 * g], dquery[2 * g + 1]], axis=1)
            dqkv_ref[rows, 128 * g : 128 * g + 128] = turn(
                tile, cos_ref[rows, :], -sin_ref[rows, :]
            ).astype(BF)
    dqkv_ref[:, key_at : key_at + 128] = turn(dkey[...], cos_ref[...], -sin_ref[...]).astype(BF)
    dqkv_ref[:, value_at : value_at + 128] = dvalue[...].astype(BF)


def attention_backward(qkv, turned, datt, lse, delta, cosine, sine, aux, segrow):
    length = qkv.shape[0]
    return pl.pallas_call(
        attention_backward_kernel,
        out_shape=jax.ShapeDtypeStruct(qkv.shape, BF),
        scratch_shapes=[pltpu.VMEM((length, 128), F32), pltpu.VMEM((length, 128), F32)],
        compiler_params=pltpu.CompilerParams(vmem_limit_bytes=20 * MIB),
        cost_estimate=cost(9),
        name="attention_backward",
    )(qkv, turned, datt, lse, delta, cosine, sine, aux, segrow)


def feed_forward_kernel(
    rows_ref, part_ref, got_ref, up_ref, gain_ref, gate_w, up_w, down_w,
    state_ref, normed_ref, hidden_ref, dgate_ref, dup_ref, whole_ref, dnormed_ref,
):
    state = rows_ref[...].astype(F32) + (part_ref[...].astype(F32) + got_ref[...].astype(F32))
    state_ref[...] = state
    scale = lax.rsqrt(jnp.mean(state * state, axis=1, keepdims=True) + EPSILON)
    normed = (state * scale * gain_ref[...]).astype(BF)
    normed_ref[...] = normed.T
    gate = dot(normed, gate_w[...])
    up = dot(normed, up_w[...])
    sig = sigmoid(gate)
    act = gate * sig
    hidden = (act * up).astype(BF)
    hidden_ref[...] = hidden
    whole_ref[...] = dot(hidden, down_w[...], ((1,), (1,))).astype(BF)
    dhidden = dot(up_ref[...], down_w[...])
    dup = (dhidden * act).astype(BF)
    dup_ref[...] = dup
    dgate = (dhidden * up * (sig * (1.0 + gate * (1.0 - sig)))).astype(BF)
    dgate_ref[...] = dgate
    dnormed_ref[...] = (
        dot(dgate, gate_w[...], ((1,), (1,))) + dot(dup, up_w[...], ((1,), (1,)))).astype(BF)


def feed_forward(rows, part, got, upstream, gain, gate_w, up_w, down_w):
    length, width = rows.shape
    units = gate_w.shape[1]
    step = 256
    block = lambda cols: pl.BlockSpec((step, cols), lambda i: (i, 0))
    whole = lambda arr: pl.BlockSpec(arr.shape, lambda i: (0, 0))
    shape = lambda cols, kind=BF: jax.ShapeDtypeStruct((length, cols), kind)
    return pl.pallas_call(
        feed_forward_kernel,
        grid=(length // step,),
        in_specs=[block(width)] * 4 + [whole(gain), whole(gate_w), whole(up_w), whole(down_w)],
        out_specs=[block(width), pl.BlockSpec((width, step), lambda i: (0, i))]
        + [block(units)] * 3 + [block(width)] * 2,
        out_shape=[shape(width, F32), jax.ShapeDtypeStruct((width, length), BF)]
        + [shape(units)] * 3 + [shape(width)] * 2,
        compiler_params=pltpu.CompilerParams(vmem_limit_bytes=44 * MIB),
        cost_estimate=cost(18),
        name="feed_forward",
    )(rows, part, got, upstream, gain, gate_w, up_w, down_w)


def norm_gradient(grad, values, scale, gain):
    weighted = grad * gain
    inner = jnp.mean(weighted * values, axis=1, keepdims=True)
    return scale * weighted - values * (scale * scale * scale * inner), jnp.sum(
        grad * (values * scale), axis=0, keepdims=True)


def middle_kernel(
    state_ref, up_ref, dpart_ref, dgot_ref, gain_ref, scan_ref, z_ref, att_ref,
    out_w, o_w, dmixed_ref, dgated_ref, dz_ref, datt_ref, delta_ref, gacc_ref, dmixed_t,
):
    @pl.when(pl.program_id(0) == 0)
    def _():
        gacc_ref[...] = jnp.zeros_like(gacc_ref)

    state = state_ref[...]
    scale = lax.rsqrt(jnp.mean(state * state, axis=1, keepdims=True) + EPSILON)
    grad, gain_grad = norm_gradient(
        dpart_ref[...].astype(F32) + dgot_ref[...].astype(F32), state, scale, gain_ref[...])
    gacc_ref[0:1, :] += gain_grad
    dmixed = (up_ref[...].astype(F32) + grad).astype(BF)
    dmixed_ref[...] = dmixed
    dmixed_t[...] = dmixed.T
    dgated = dot(dmixed, out_w[...])
    dgated_ref[...] = dgated.astype(BF)
    gate = z_ref[...].astype(F32)
    sig = sigmoid(gate)
    dz_ref[...] = (dgated * scan_ref[...].astype(F32) * (sig * (1.0 + gate * (1.0 - sig)))).astype(BF)
    datt = dot(dmixed, o_w[...]).astype(BF)
    datt_ref[...] = datt
    product = datt.astype(F32) * att_ref[...].astype(F32)
    channel = lax.broadcasted_iota(jnp.int32, (product.shape[1], 128), 0)
    head = lax.broadcasted_iota(jnp.int32, (product.shape[1], 128), 1)
    delta = dot_exact(product, (channel // HD == head).astype(F32))
    delta_ref[...] = delta.T[0:8, :]


def middle(state, upstream, dpart, dgot, gain, scan, z, att, out_w, o_w):
    length, width = state.shape
    step = 256
    block = lambda arr: pl.BlockSpec((step, arr.shape[1]), lambda i: (i, 0))
    whole = lambda arr: pl.BlockSpec(arr.shape, lambda i: (0, 0))
    like = lambda arr: jax.ShapeDtypeStruct(arr.shape, BF)
    return pl.pallas_call(
        middle_kernel,
        grid=(length // step,),
        in_specs=[block(arr) for arr in (state, upstream, dpart, dgot)]
        + [whole(gain), block(scan), block(z), block(att), whole(out_w), whole(o_w)],
        out_specs=[block(upstream)] + [block(scan)] * 2
        + [block(att), pl.BlockSpec((8, step), lambda i: (0, i)), pl.BlockSpec((8, width), lambda i: (0, 0)),
           pl.BlockSpec((width, step), lambda i: (0, i))],
        out_shape=[like(upstream)] + [like(scan)] * 2 + [like(att)]
        + [jax.ShapeDtypeStruct((8, length), F32), jax.ShapeDtypeStruct((8, width), F32),
           jax.ShapeDtypeStruct((width, length), BF)],
        compiler_params=pltpu.CompilerParams(vmem_limit_bytes=36 * MIB),
        cost_estimate=cost(11),
        name="middle",
    )(state, upstream, dpart, dgot, gain, scan, z, att, out_w, o_w)


def last_norm_kernel(dpart_ref, dgot_ref, rows_ref, dmixed_ref, scale_ref, gain_ref, out_ref, gacc_ref):
    @pl.when(pl.program_id(0) == 0)
    def _():
        gacc_ref[...] = jnp.zeros_like(gacc_ref)

    grad, gain_grad = norm_gradient(
        dpart_ref[...].astype(F32) + dgot_ref[...].astype(F32), rows_ref[...].astype(F32),
        scale_ref[...], gain_ref[...])
    gacc_ref[0:1, :] += gain_grad
    out_ref[...] = (dmixed_ref[...].astype(F32) + grad).astype(BF)


def last_norm(dpart, dgot, rows, dmixed, scale, gain):
    length, width = rows.shape
    step = 256
    block = pl.BlockSpec((step, width), lambda i: (i, 0))
    return pl.pallas_call(
        last_norm_kernel,
        grid=(length // step,),
        in_specs=[block] * 4 + [pl.BlockSpec((step, 1), lambda i: (i, 0)), pl.BlockSpec((1, width), lambda i: (0, 0))],
        out_specs=[block, pl.BlockSpec((8, width), lambda i: (0, 0))],
        out_shape=[jax.ShapeDtypeStruct((length, width), BF), jax.ShapeDtypeStruct((8, width), F32)],
        compiler_params=pltpu.CompilerParams(vmem_limit_bytes=20 * MIB),
        cost_estimate=cost(4.5),
        name="last_norm",
    )(dpart, dgot, rows, dmixed, scale, gain)


def core_swap(value):
    return lax.ppermute(value, "head", [(0, 1), (1, 0), (2, 3), (3, 2)])


def half_swap(value):
    return lax.ppermute(value, "head", [(0, 2), (2, 0), (1, 3), (3, 1)])


def half_groups(dp):
    return [[d * 4 + 2 * half + core for d in range(dp) for half in range(2)] for core in range(2)]


def ordered(is_first, mine, other, axis):
    return jnp.where(
        is_first,
        jnp.concatenate([mine, other], axis=axis),
        jnp.concatenate([other, mine], axis=axis),
    )


BITS = (2, 4, 1)


def pair_list(dp, low_heads, bit):
    pairs = []
    for d in range(dp):
        for slot in range(4):
            flip = low_heads[slot % 2]
            target = (d ^ bit) * 4 + slot if flip else d * 4 + (slot ^ 2)
            pairs.append((d * 4 + slot, target))
    return pairs


def dp_swap(value, bit):
    return lax.ppermute(value, "dp", [(d, d ^ bit) for d in range(8)])


def near_swap(value, step):
    return lax.ppermute(value, ("dp", "head"), pair_list(8, (step == 1, step == 0), 1))


def append(value, arrived):
    return jnp.concatenate([value, arrived], axis=0)


class Order:
    def __init__(self):
        self.last = None

    def __call__(self, *values):
        held = values if self.last is None else values + (self.last,)
        held = lax.optimization_barrier(held)
        self.last = held[0]
        return held[0] if len(values) == 1 else held[: len(values)]


class Gather:
    def along(self, piece):
        self.piece = piece
        self.first = dp_swap(piece, BITS[0])

    def join(self, first):
        return append(self.piece, first)

    def across(self, pair):
        self.pair = pair
        self.second = dp_swap(pair, BITS[1])

    def join2(self, second):
        return append(self.pair, second)

    def near_step(self, quad):
        self.quad = quad
        self.third = near_swap(quad, 0)

    def join3(self, third):
        return append(self.quad, third)

    def far_step(self, near):
        self.near = near
        self.far = near_swap(near, 1)


def gather_whole(piece, dp, is_first):
    rows, cols = piece.shape
    both = lax.all_gather(
        piece, ("dp", "head"), axis=0, tiled=False, axis_index_groups=half_groups(dp)
    ).reshape(dp, 2, rows, cols)
    mine = jnp.where(is_first, both[:, 0], both[:, 1]).reshape(dp * rows, cols)
    other = jnp.where(is_first, both[:, 1], both[:, 0]).reshape(dp * rows, cols)
    lines = lambda value, side: value.reshape(4, 2, -1, cols)[:, side].reshape(-1, cols)
    return append(lines(mine, 0), lines(other, 0)), append(lines(mine, 1), lines(other, 1))


def unpack_kernel(groups, place, near_a, near_b, far_a, far_b, *outs):
    first = place[0] == 0
    step = near_a.shape[0]
    own = pl.ds(pl.multiple_of(place[1] * step, step), step)
    neighbour = pl.ds(pl.multiple_of((1 - place[1]) * step, step), step)
    for out, (at, size) in zip(outs, groups):
        cols = slice(at, at + size)
        one, two = near_b[:, cols], far_a[:, cols]
        out[own, :size] = near_a[:, cols]
        out[neighbour, size:] = far_b[:, cols]
        out[neighbour, :size] = jnp.where(first, two, one)
        out[own, size:] = jnp.where(first, one, two)


def unpack(near, far, place, groups):
    total, cols = near.shape
    step = total // 8
    view = lambda shift: pl.BlockSpec((step, cols), lambda i, _: (i + shift, 0))
    return pl.pallas_call(
        functools.partial(unpack_kernel, groups),
        grid_spec=pltpu.PrefetchScalarGridSpec(
            num_scalar_prefetch=1,
            grid=(4,),
            in_specs=[view(0), view(4), view(0), view(4)],
            out_specs=[
                pl.BlockSpec((2 * step, 2 * size), lambda i, place: (place[2 + i], 0)) for _, size in groups
            ],
        ),
        out_shape=[jax.ShapeDtypeStruct((total, 2 * size), BF) for _, size in groups],
        compiler_params=pltpu.CompilerParams(vmem_limit_bytes=20 * MIB),
        cost_estimate=cost(3),
        name="unpack",
    )(place, near, near, far, far)


def grads_kernel(spans, place, *refs):
    count = len(spans)
    lefts = refs[:count]
    mines, others = refs[count : 2 * count], refs[2 * count : 3 * count]
    send, two, keep, whole = refs[3 * count :]
    step = pl.program_id(0)
    for left, mine, other, (begin, end) in zip(lefts, mines, others, spans):

        @pl.when((step >= begin) & (step < end))
        def _():
            both = jnp.concatenate([mine[...], other[...]], axis=1)
            whole[...] = both if left is None else dot(left[...], both).astype(BF)

    first = place[0] == 0
    rows = keep.shape[0] // 4
    for line in range(4):
        at = pl.multiple_of(place[2 + line] * (2 * rows), 2 * rows)
        own = pl.ds(at + pl.multiple_of(place[1] * rows, rows), rows)
        neighbour = pl.ds(at + pl.multiple_of((1 - place[1]) * rows, rows), rows)
        here = slice(line * rows, (line + 1) * rows)
        one, other = whole[neighbour, :128], whole[own, 128:]
        keep[here, :] = whole[own, :128]
        send[1, here, :] = whole[neighbour, 128:]
        send[0, here, :] = jnp.where(first, one, other)
        two[here, :] = jnp.where(first, other, one)


def grads(pairs, place):
    total = pairs[0][1].shape[0]
    spans, at = [], 0
    for _, right in pairs:
        tiles = right.shape[1] // 256
        spans.append((at, at + tiles))
        at += tiles
    cols = 128 * at
    lefts = [left for left, _ in pairs if left is not None]
    keys = []
    for left in lefts:
        if not any(left is key for key in keys):
            keys.append(left)
    index_of = [None if left is None else [left is key for key in keys].index(True) for left, _ in pairs]

    def kernel(place, *refs):
        arrays, rest = refs[: len(keys)], refs[len(keys) :]
        chosen = tuple(None if index is None else arrays[index] for index in index_of)
        grads_kernel(spans, place, *chosen, *rest)

    def view(right, span, side):
        tiles = span[1] - span[0]
        return pl.BlockSpec(
            (right.shape[0], 128),
            lambda i, place: (0, side * tiles + jnp.clip(i - span[0], 0, tiles - 1)))

    views = [view(right, span, side) for side in range(2) for (_, right), span in zip(pairs, spans)]
    rights = [right for _, right in pairs]
    return pl.pallas_call(
        kernel,
        grid_spec=pltpu.PrefetchScalarGridSpec(
            num_scalar_prefetch=1,
            grid=(at,),
            in_specs=[pl.BlockSpec(key.shape, lambda i, place: (0, 0)) for key in keys] + views,
            out_specs=[
                pl.BlockSpec((2, total // 2, 128), lambda i, _: (0, 0, i)),
                pl.BlockSpec((total // 2, 128), lambda i, _: (0, i)),
                pl.BlockSpec((total // 2, 128), lambda i, _: (0, i)),
            ],
            scratch_shapes=[pltpu.VMEM((total, 256), BF)],
        ),
        out_shape=[
            jax.ShapeDtypeStruct((2, total // 2, cols), BF),
            jax.ShapeDtypeStruct((total // 2, cols), BF),
            jax.ShapeDtypeStruct((total // 2, cols), BF),
        ],
        compiler_params=pltpu.CompilerParams(vmem_limit_bytes=28 * MIB),
        cost_estimate=cost(6),
        name="grads",
    )(place, *keys, *rights, *rights)


def long(value):
    return value.astype(F32)


def beside(*parts):
    return jnp.concatenate(parts, axis=1)


class Scatter:
    def __init__(self, pairs, place):
        self.rows = pairs[0][1].shape[0] // 8
        self.send, self.two, self.keep = grads(pairs, place)
        self.extra = None

    def far_step(self, send):
        self.got = near_swap(send, 1)

    def sum2(self, got):
        self.got = got
        return (long(self.two) + long(got[1])).astype(BF)

    def near_step(self, part):
        self.got2 = near_swap(part, 0)

    def kept(self, part):
        total = long(self.keep[part]) + long(self.got[0, part]) + long(self.got2[part])
        return total if self.extra is None else total + self.extra[part]

    def sum3(self, got2):
        self.got2 = got2
        return self.kept(slice(2 * self.rows, 4 * self.rows)).astype(BF)

    def across(self, part):
        self.got3 = dp_swap(part, BITS[1])

    def lower(self, part):
        return self.kept(part) + long(self.got3[part])

    def sum4(self, got3):
        self.got3 = got3
        return self.lower(slice(self.rows, 2 * self.rows)).astype(BF)

    def along(self, part):
        self.got4 = dp_swap(part, BITS[0])

    def result(self, got4):
        return self.lower(slice(0, self.rows)) + long(got4)


def scatter_whole(pairs, dp, is_first):
    grads = [right if left is None else dot(left, right).astype(BF) for left, right in pairs]
    rows = grads[0].shape[0] // dp
    half_of = lambda grad, side: grad[:, side * (grad.shape[1] // 2) : (side + 1) * (grad.shape[1] // 2)]
    mine, other = [
        jnp.concatenate([half_of(grad, side) for grad in grads], axis=1).reshape(dp, 1, rows, -1)
        for side in range(2)
    ]
    both = ordered(is_first, mine, other, 1).reshape(dp * 2 * rows, -1)
    return lax.psum_scatter(
        both, ("dp", "head"), scatter_dimension=0, tiled=True, axis_index_groups=half_groups(dp)
    ).astype(F32)


def load_kernel(place, tok_ref, cot_ref, gain_ref, rows_ref, cot_out, normed_ref, scale_ref, normed_t, cot_t):
    rows = tok_ref[...]
    rows_ref[...] = rows
    cot_out[...] = cot_ref[...]
    cot_t[...] = cot_ref[...].T
    rows = rows.astype(F32)
    scale = lax.rsqrt(jnp.mean(rows * rows, axis=1, keepdims=True) + EPSILON)
    scale_ref[...] = scale
    normed = (rows * scale * gain_ref[...]).astype(BF)
    normed_ref[...] = normed
    normed_t[...] = normed.T


def load(tokens, cotangent, gain, half, length):
    width = tokens.shape[1]
    step = 256
    steps = length // step
    picked = pl.BlockSpec((step, width), lambda i, place: (place[0] * steps + i, 0))
    plain = pl.BlockSpec((step, width), lambda i, place: (i, 0))
    return pl.pallas_call(
        load_kernel,
        grid_spec=pltpu.PrefetchScalarGridSpec(
            num_scalar_prefetch=1,
            grid=(steps,),
            in_specs=[picked, picked, pl.BlockSpec((1, width), lambda i, place: (0, 0))],
            out_specs=[plain, plain, plain, pl.BlockSpec((step, 1), lambda i, place: (i, 0))]
            + [pl.BlockSpec((width, step), lambda i, place: (0, i))] * 2,
        ),
        out_shape=[jax.ShapeDtypeStruct((length, width), BF)] * 3
        + [jax.ShapeDtypeStruct((length, 1), F32)]
        + [jax.ShapeDtypeStruct((width, length), BF)] * 2,
        compiler_params=pltpu.CompilerParams(vmem_limit_bytes=20 * MIB),
        cost_estimate=cost(4.5),
        name="load",
    )(half, tokens, cotangent, gain)


def store_kernel(place, *refs):
    step = pl.program_id(0)
    for index, ref in enumerate(refs[:-1]):

        @pl.when((step >= place[2 * index]) & (step < place[2 * index + 1]))
        def _():
            refs[-1][...] = ref[...]


def part_of(mine, core):
    return lax.dynamic_slice_in_dim(mine, core * (mine.shape[0] // 2), mine.shape[0] // 2, 0)


def store(parts, half, core):
    width = parts[0].shape[1]
    length = sum(part.shape[0] for part in parts) // 2
    step = 256
    per = length // step
    begin = [half * per, (1 - half) * per + core * (per // 2), (1 - half) * per + (1 - core) * (per // 2)]
    if len(parts) == 4:
        begin = [half * per + core * (per // 2), half * per + (1 - core) * (per // 2)] + begin[1:]
    many = [part.shape[0] // step for part in parts]
    place = jnp.stack([value for at, size in zip(begin, many) for value in (at, at + size)]).astype(jnp.int32)
    view = lambda index, size: pl.BlockSpec(
        (step, width), lambda i, place: (jnp.clip(i - place[2 * index], 0, size - 1), 0))
    return pl.pallas_call(
        store_kernel,
        grid_spec=pltpu.PrefetchScalarGridSpec(
            num_scalar_prefetch=1,
            grid=(2 * per,),
            in_specs=[view(index, size) for index, size in enumerate(many)],
            out_specs=pl.BlockSpec((step, width), lambda i, place: (i, 0)),
        ),
        out_shape=jax.ShapeDtypeStruct((2 * length, width), BF),
        compiler_params=pltpu.CompilerParams(vmem_limit_bytes=20 * MIB),
        cost_estimate=cost(5),
        name="store",
    )(place, *parts)


def first_piece_kernel(slot, x_ref, dt_ref, bc_ref, key_ref, value_ref, out_ref):
    inner = x_ref.shape[1]
    heads = dt_ref.shape[1]
    rows = x_ref.shape[0]
    out_ref[:, :inner] = x_ref[...].astype(BF)
    steps = dt_ref[...]
    out_ref[:, inner : inner + 128] = jnp.concatenate(
        [steps, steps, jnp.zeros((rows, 128 - 2 * heads), F32)], axis=1).astype(BF)
    sources = (bc_ref.at[:, :128], bc_ref.at[:, 128:], key_ref, value_ref)
    for index, ref in enumerate(sources):

        @pl.when(slot[0] == index)
        def _():
            out_ref[:, inner + 128 :] = ref[...].astype(BF)


def first_piece(slot, x, dt, bc, key, value):
    vmem = pl.BlockSpec(memory_space=pltpu.VMEM)
    return pl.pallas_call(
        first_piece_kernel,
        in_specs=[pl.BlockSpec(memory_space=pltpu.SMEM)] + [vmem] * 5,
        out_specs=vmem,
        out_shape=jax.ShapeDtypeStruct((x.shape[0], x.shape[1] + 256), BF),
        compiler_params=pltpu.CompilerParams(vmem_limit_bytes=20 * MIB),
        cost_estimate=cost(1),
        name="first_piece",
    )(slot[None].astype(jnp.int32), x, dt, bc, key, value)


def other_pieces_kernel(z_ref, q_ref, out_w, o_ref, gate_ref, up_ref, down_ref, p2, p3, p4, p5):
    join = lambda *parts: jnp.concatenate(parts, axis=1).astype(BF)
    p2[...] = join(z_ref[...], q_ref[...])
    p3[...] = join(out_w[...].T, o_ref[...].T)
    p4[...] = join(gate_ref[...], up_ref[...])
    p5[...] = down_ref[...].T.astype(BF)


def other_pieces(z, q, out_w, o, gate, up, down):
    rows = z.shape[0]
    vmem = pl.BlockSpec(memory_space=pltpu.VMEM)
    shape = lambda cols: jax.ShapeDtypeStruct((rows, cols), BF)
    return pl.pallas_call(
        other_pieces_kernel,
        in_specs=[vmem] * 7,
        out_specs=[vmem] * 4,
        out_shape=[
            shape(z.shape[1] + q.shape[1]), shape(out_w.shape[0] + o.shape[0]),
            shape(gate.shape[1] + up.shape[1]), shape(down.shape[0]),
        ],
        compiler_params=pltpu.CompilerParams(vmem_limit_bytes=20 * MIB),
        cost_estimate=cost(1),
        name="other_pieces",
    )(z, q, out_w, o, gate, up, down)


def shared_kernel(place, bc_ref, kv_ref, keep, send):
    half, core = place[0], place[1]
    step = bc_ref.shape[0] // 4
    for out, which in ((keep, core), (send, 1 - core)):
        for side in range(2):
            slot = 2 * (half if side == 0 else 1 - half) + which
            rows = pl.ds(pl.multiple_of(slot * step, step), step)
            for col in range(4):
                ref = bc_ref if col < 2 else kv_ref
                out[col * step : (col + 1) * step, 128 * side : 128 * side + 128] = ref[
                    rows, 128 * (col % 2) : 128 * (col % 2) + 128]


def shared_rows(grad_bc, grad_kv, half, core, dp):
    total = grad_bc.shape[0]
    if total // dp != 128:
        tiles = jnp.concatenate([grad_bc, grad_kv], axis=1).reshape(dp, 4, -1, 4, 128).swapaxes(2, 3)
        tile = lambda slot: lax.dynamic_index_in_dim(tiles, slot, 1, keepdims=False).reshape(total, 128)
        both = lambda which: jnp.concatenate(
            [tile(2 * half + which), tile(2 * (1 - half) + which)], axis=1)
        return both(core), both(1 - core)
    step = 128
    spec = pl.BlockSpec((step, 256), lambda i, _: (i, 0))
    return pl.pallas_call(
        shared_kernel,
        grid_spec=pltpu.PrefetchScalarGridSpec(
            num_scalar_prefetch=1,
            grid=(total // step,),
            in_specs=[spec, spec],
            out_specs=[spec, spec],
        ),
        out_shape=[jax.ShapeDtypeStruct((total, 256), BF)] * 2,
        compiler_params=pltpu.CompilerParams(vmem_limit_bytes=20 * MIB),
        cost_estimate=cost(2),
        name="shared_rows",
    )(jnp.stack([half, core]).astype(jnp.int32), grad_bc, grad_kv)


def products_kernel(count, *refs):
    out = refs[-1]
    total = dot(refs[0][...], refs[count][...], ((1,), (1,)))
    for i in range(1, count):
        total = total + dot(refs[i][...], refs[count + i][...], ((1,), (1,)))
    out[...] = total.astype(out.dtype)


def products(lefts, rights, dtype):
    length = lefts[0].shape[0]
    width = rights[0].shape[0]
    step = 256
    return pl.pallas_call(
        functools.partial(products_kernel, len(lefts)),
        grid=(length // step,),
        in_specs=[pl.BlockSpec((step, left.shape[1]), lambda i: (i, 0)) for left in lefts]
        + [pl.BlockSpec(right.shape, lambda i: (0, 0)) for right in rights],
        out_specs=pl.BlockSpec((step, width), lambda i: (i, 0)),
        out_shape=jax.ShapeDtypeStruct((length, width), dtype),
        compiler_params=pltpu.CompilerParams(vmem_limit_bytes=28 * MIB),
        cost_estimate=cost(6),
        name="products",
    )(*lefts, *rights)


def wide(mine, other, width):
    return jnp.concatenate([mine[:, :width], other[:, :width]], axis=1)


def body(
    tokens, segments, cotangent, gain_in, mamba_gate_weight, mamba_input_weight, w_dt, w_bc,
    convolution_input_taps, convolution_input_bias, conv_bc, conv_bc_bias, dt_bias, a_log, d_skip,
    w_q, w_k, w_v, w_o, mamba_output_weight, gain_ffn, w_gate, w_up, w_down,
):
    length = segments.shape[1]
    width = tokens.shape[1]
    rows_here = mamba_gate_weight.shape[0]
    dp = width // rows_here
    inner = mamba_gate_weight.shape[1]
    heads = w_dt.shape[1]
    qcols = w_q.shape[1]
    hidden_cols = w_gate.shape[1]
    slot = lax.axis_index("head")
    half = slot // 2
    core = slot % 2
    is_first = half == 0
    place_dp = lax.axis_index("dp")
    if dp == 8:
        route = jnp.stack([core, place_dp % 2] + [(place_dp // 2) ^ i for i in range(4)])
    else:
        route = jnp.concatenate([jnp.zeros((2,), jnp.int32), jnp.arange(4)])
    route = route.astype(jnp.int32)
    gain_in, gain_ffn = gain_in[None], gain_ffn[None]

    short = lambda value: value.astype(BF)
    first_core = core == 0
    flip = lambda tile: jnp.where(is_first, tile, jnp.concatenate([tile[:, HD:], tile[:, :HD]], axis=1))
    flips = lambda tile: jnp.concatenate([flip(tile[:, :128]), flip(tile[:, 128:])], axis=1)
    cols = ((0,), (0,))
    own = half[None].astype(jnp.int32)
    ringed = dp == 8
    order = Order()

    def tables(segments):
        seg = lax.dynamic_index_in_dim(segments, half, 0, keepdims=False)
        return segment_tables(seg) + rope_tables(length)

    def own_sums(mine, other):
        low, at = 2 * inner, 2 * inner + 2 * STATE
        return jnp.concatenate([
            mine[:, :inner] + other[:, inner:low], mine[:, low:at] + other[:, low:at],
            mine[:, at : at + heads] + other[:, at + heads : at + 2 * heads],
            jnp.zeros((8, 128 - heads), F32), mine[:, at + 128 :] + other[:, at + 128 :]], axis=1)

    piece1 = first_piece(slot, mamba_input_weight, w_dt, w_bc, w_k, w_v)
    rest = (mamba_gate_weight, w_q, mamba_output_weight, w_o, w_gate, w_up, w_down)
    shapes1 = ((0, inner + 128), (inner + 128, 128))
    shapes2 = shapes3 = ((0, inner), (inner, qcols))
    shapes4 = ((0, hidden_cols), (hidden_cols, hidden_cols))
    shapes5 = ((0, hidden_cols),)
    g1, g2, g3, g4, g5 = [Gather() for _ in range(5)]
    scan_params = (convolution_input_taps, convolution_input_bias, dt_bias, a_log, d_skip)
    if ringed:
        g1.along(piece1)
        held = order(g1.first, tokens, cotangent, segments, *rest, *scan_params)
        first1, tokens, cotangent, segments = held[:4]
        convolution_input_taps, convolution_input_bias, dt_bias, a_log, d_skip = held[11:]
        pieces = other_pieces(*held[4:11])
        pair1, *pieces = order(g1.join(first1), *pieces)
        g1.across(pair1)
        piece2, piece3, piece4, piece5 = pieces
        g2.along(piece2)
    else:
        pieces = (
            jnp.concatenate([short(mamba_gate_weight), short(w_q)], axis=1),
            jnp.concatenate([short(mamba_output_weight).T, short(w_o).T], axis=1),
            jnp.concatenate([short(w_gate), short(w_up)], axis=1), short(w_down).T)
        ways = [gather_whole(piece, dp, is_first) for piece in (piece1,) + pieces]
    rows_b, upstream, normed, scale, normed_t, upstream_t = load(tokens, cotangent, gain_in, own, length)
    aux, segrow, cosine, sine = tables(segments)
    seg_line = aux[:, 0][None]
    per_head = jnp.pad(jnp.stack([dt_bias, a_log, d_skip]), ((0, 5), (0, 128 - heads)))
    small = jnp.concatenate(
        [jnp.concatenate([convolution_input_taps, convolution_input_bias[None],
                          jnp.repeat(d_skip, HD)[None], jnp.zeros((2, inner), F32)], axis=0), per_head],
        axis=1)
    small_other = half_swap(small)
    xpar = jnp.concatenate([small[:, :inner], small_other[:, :inner]], axis=1)
    head_par = jnp.concatenate(
        [small[:2, inner : inner + heads], small_other[:2, inner : inner + heads],
         jnp.zeros((2, 128 - 2 * heads), F32)], axis=1)
    lane = jnp.arange(128) < 2 * heads
    hpar = jnp.concatenate(
        [head_par[:1], jnp.where(lane, -jnp.exp(head_par[1:]), 0.0), jnp.zeros((6, 128), F32)], axis=0)
    bcpar = jnp.concatenate([conv_bc, conv_bc_bias[None], jnp.zeros((3, conv_bc.shape[1]), F32)], axis=0)

    if ringed:
        second1, first2, normed, aux, cosine, sine, xpar, hpar = order(
            g1.second, g2.first, normed, aux, cosine, sine, xpar, hpar)
        quad1, pair2, piece3 = order(g1.join2(second1), g2.join(first2), piece3)
        g1.near_step(quad1)
        g2.across(pair2)
        g3.along(piece3)
        third1, second2, first3 = order(g1.third, g2.second, g3.first)
        near1, quad2, pair3, piece4 = order(g1.join3(third1), g2.join2(second2), g3.join(first3), piece4)
        g1.far_step(near1)
        g2.near_step(quad2)
        g3.across(pair3)
        g4.along(piece4)
        far1, third2, second3, first4 = order(g1.far, g2.third, g3.second, g4.first)
        near2, quad3, pair4, piece5 = order(g2.join3(third2), g3.join2(second3), g4.join(first4), piece5)
        g2.far_step(near2)
        g3.near_step(quad3)
        g4.across(pair4)
        g5.along(piece5)
        ways1 = (near1, far1)
    else:
        ways1 = ways[0]
    weight1, quarters = unpack(*ways1, route, shapes1)
    swap_halves = lambda tile: jnp.concatenate([tile[:, 128:], tile[:, :128]], axis=1)
    quarters = jnp.where(is_first, quarters, swap_halves(quarters))
    others = core_swap(quarters)
    h1 = dot(normed, weight1)
    c0 = jnp.where(first_core, quarters, others)
    c1 = jnp.where(first_core, others, quarters)
    weight_bc = jnp.concatenate([c0[:, :128], c1[:, :128]], axis=1)
    weight_kv = flips(jnp.concatenate([c0[:, 128:], c1[:, 128:]], axis=1))
    pair = dot(normed, weight_bc)
    keyvalue = short(dot(normed, weight_kv))
    if ringed:
        far2, third3, second4, first5, h1, pair, keyvalue = order(
            g2.far, g3.third, g4.second, g5.first, h1, pair, keyvalue)
        near3, quad4, pair5 = order(g3.join3(third3), g4.join2(second4), g5.join(first5))
        g3.far_step(near3)
        g4.near_step(quad4)
        g5.across(pair5)
        ways2 = (near2, far2)
    else:
        ways2 = ways[1]
    weight_z, weight_q = unpack(*ways2, route, shapes2)
    z = short(dot(normed, weight_z))
    qkv = jnp.concatenate([short(dot(normed, weight_q)), keyvalue], axis=1)

    attended, turned, lse = attention_forward(qkv, cosine, sine, aux, seg_line)
    if ringed:
        far3, third4, second5, attended, z = order(g3.far, g4.third, g5.second, attended, z)
        near4, quad5, z = order(g4.join3(third4), g5.join2(second5), z)
        g4.far_step(near4)
        g5.near_step(quad5)
        ways3 = (near3, far3)
    else:
        ways3 = ways[2]
    gated, scan, start = ssd_forward(h1, pair, z, aux, segrow, xpar, bcpar, hpar)
    weight_out, weight_o = unpack(*ways3, route, shapes3)
    mixed = products([gated, attended], [weight_out, weight_o], BF)
    mixed_got = core_swap(mixed)

    if ringed:
        third5, mixed = order(g5.third, mixed)
        near5 = order(g5.join3(third5))
        g5.far_step(near5)
        far4 = order(g4.far)
        ways4 = (near4, far4)
    else:
        ways4 = ways[3]
    weight_gate, weight_up = unpack(*ways4, route, shapes4)
    if ringed:
        weight_gate, weight_up, far5, mixed_got = order(weight_gate, weight_up, g5.far, mixed_got)
        ways5 = (near5, far5)
    else:
        ways5 = ways[4]
    (weight_down,) = unpack(*ways5, route, shapes5)
    state, normed_ffn_t, hidden, dgate, dup, whole, dnormed_part = feed_forward(
        rows_b, mixed, mixed_got, upstream, gain_ffn, weight_gate, weight_up, weight_down)
    whole_got = core_swap(whole)
    dnormed_got = core_swap(dnormed_part)
    down_pairs = [(upstream_t, hidden)]
    ffn_pairs = [(normed_ffn_t, dgate), (normed_ffn_t, dup)]
    if ringed:
        s5 = Scatter(down_pairs, route)
        send5, normed_ffn_t, whole_got = order(s5.send, normed_ffn_t, whole_got)
        s5.far_step(send5)
        ffn_pairs = [(normed_ffn_t, dgate), (normed_ffn_t, dup)]
        s4 = Scatter(ffn_pairs, route)
    out_mine = short(state + (long(whole) + long(whole_got)))
    if ringed:
        send4, got5, dnormed_got = order(s4.send, s5.got, dnormed_got)
        part5, send4, dnormed_got = order(s5.sum2(got5), send4, dnormed_got)
        s4.far_step(send4)
        s5.near_step(part5)
    dmixed, dgated, dz, datt, delta, gacc_ffn, dmixed_t = middle(
        state, upstream, dnormed_part, dnormed_got, gain_ffn, scan, z, attended, weight_out, weight_o)
    dqkv = attention_backward(qkv, turned, datt, lse, delta, cosine, sine, aux, seg_line)
    if ringed:
        dqkv, got4, got2_5, out_mine = order(dqkv, s4.got, s5.got2, out_mine)
        part4, dqkv, dz = order(s4.sum2(got4), dqkv, dz)
        s4.near_step(part4)
    dqry, dkv = dqkv[:, : 2 * qcols], dqkv[:, 2 * qcols :]
    second_pairs = [(dmixed_t, gated), (dmixed_t, attended), (normed_t, dz), (normed_t, dqry)]
    grad_kv = short(dot(normed_t, dkv))
    if ringed:
        s2 = Scatter(second_pairs, route)
        send2, got2_4, grad_kv = order(s2.send, s4.got2, grad_kv)
        third_4, send2, dgated = order(beside(s4.sum3(got2_4), s5.sum3(got2_5)), send2, dgated)
        s2.far_step(send2)
        got3_4 = dp_swap(third_4, BITS[1])
    dh1, dpair, acc = ssd_backward(
        h1, pair, z, dgated, start, aux, segrow, xpar, bcpar, hpar)
    if ringed:
        dh1, dpair, acc, got_2, got3_4 = order(dh1, dpair, acc, s2.got, got3_4)
        part2, fourth_4, dh1, dpair, out_part, acc = order(
            s2.sum2(got_2),
            beside(s4.sum4(got3_4[:, : 2 * hidden_cols]), s5.sum4(got3_4[:, 2 * hidden_cols :])),
            dh1, dpair, part_of(out_mine, core), jnp.concatenate([acc, gacc_ffn], axis=1))
        s2.near_step(part2)
        got4_4 = dp_swap(fourth_4, BITS[0])
        acc_got = dp_swap(acc, BITS[1])
    else:
        acc = jnp.concatenate([acc, gacc_ffn], axis=1)
        out_part = part_of(out_mine, core)
    out_got = half_swap(out_part)

    grad_bc = short(dot(normed_t, dpair))
    keep_shared, send_shared = shared_rows(grad_bc, flips(grad_kv), half, core, dp)
    shared_got = core_swap(send_shared)
    dnormed_part = products(
        [dh1, dpair, dz, dqry, dkv], [weight1, weight_bc, weight_z, weight_q, weight_kv], BF)
    dnormed_send = part_of(dnormed_part, 1 - core)
    dnormed_own = part_of(dnormed_part, core)
    if ringed:
        dnormed_send, dnormed_own, got2_2, got4_4, shared_got, acc = order(
            dnormed_send, dnormed_own, s2.got2, got4_4, shared_got, acc + acc_got)
        third_2, acc, dnormed_send = order(s2.sum3(got2_2), acc, dnormed_send)
        acc_got = dp_swap(acc, BITS[0])
        s2.across(third_2)
    dnormed_got = core_swap(dnormed_send)
    grad_shared = short(long(keep_shared) + long(shared_got))
    last_pairs = [(normed_t, dh1), (None, grad_shared)]
    if ringed:
        s1 = Scatter(last_pairs, route)
        send1, acc, out_got = order(s1.send, acc + acc_got, out_got)
        s1.far_step(send1)
        acc_got = half_swap(acc)
        sent4 = s4.result(got4_4[:, : 2 * hidden_cols])
        sent5 = s5.result(got4_4[:, 2 * hidden_cols :]).T
    grad_mine, gacc_in = last_norm(
        dnormed_own, dnormed_got, part_of(rows_b, core), part_of(dmixed, core), part_of(scale, core), gain_in)
    if ringed:
        grad_mine, gacc_in, sent4, sent5 = order(grad_mine, gacc_in, sent4, sent5)
        gacc_in, got3_2 = order(gacc_in + core_swap(gacc_in), s2.got3)
        fourth_2, gacc_in = order(s2.sum4(got3_2), gacc_in)
        s2.along(fourth_2)
        gains_got = half_swap(gacc_in)
        out_got2 = core_swap(out_got)
        output = store([out_mine, out_got, out_got2], half, core)
        got_1, output, acc, gacc_in = order(s1.got, output, own_sums(acc, acc_got), gacc_in + gains_got)
        part1, gacc_in, acc = order(s1.sum2(got_1), gacc_in, acc)
        gains_got = dp_swap(gacc_in, BITS[2])
        acc_got = dp_swap(acc, BITS[2])
        s1.near_step(part1)
        grad_got = half_swap(grad_mine)
        got2_1, gacc_in, acc = order(s1.got2, gacc_in + gains_got, acc + acc_got)
        bc_got = core_swap(acc[:, inner : inner + 2 * STATE])
        blocks = gacc_in[0].reshape(4, 2 * rows_here)
        gain_rows = jnp.concatenate([
            lax.dynamic_slice(blocks, ((place_dp // 2) ^ i, (place_dp % 2) * rows_here), (1, rows_here))
            for i in range(4)], axis=1).reshape(-1, 1)
        s1.extra = jnp.pad(gain_rows, ((0, 0), (inner + 2 * heads, 256 - 2 * heads - 1)))
        third_1 = order(s1.sum3(got2_1))
        s1.across(third_1)
        sent2 = s2.result(s2.got4)
        got3_1, sent2, grad_got, bc_got = order(s1.got3, sent2, grad_got, bc_got)
        fourth_1, grad_got = order(s1.sum4(got3_1), grad_got)
        s1.along(fourth_1)
        grad_near, grad_got2 = core_swap(grad_mine), core_swap(grad_got)
        grad_near, grad_got2 = order(grad_near, grad_got2)
        grad_tokens = store([grad_mine, grad_near, grad_got, grad_got2], half, core)
        sent1 = s1.result(s1.got4)
        gain_grads_in = sent1[:, inner + 2 * heads]
    else:
        acc = lax.psum(acc, "dp")
        acc = own_sums(acc, half_swap(acc))
        bc_got = core_swap(acc[:, inner : inner + 2 * STATE])
        gain_sums = lax.psum(gacc_in[0], ("dp", "head"))
        gain_grads_in = lax.dynamic_slice_in_dim(gain_sums, place_dp * rows_here, rows_here, 0)
        sent5, sent4, sent2, sent1 = [
            scatter_whole(pairs, dp, is_first)
            for pairs in (down_pairs, ffn_pairs, second_pairs, last_pairs)]
        sent5 = sent5.T
        grad_got = half_swap(grad_mine)
        output = store([out_mine, out_got, core_swap(out_got)], half, core)
        grad_tokens = store([grad_mine, core_swap(grad_mine), grad_got, core_swap(grad_got)], half, core)
    sent3, sent2 = sent2[:, : inner + qcols], sent2[:, inner + qcols :]
    steps_at = inner + 2 * STATE
    own = acc[:, :inner]
    skip = own[5].reshape(heads, HD).sum(axis=-1)
    rank = place_dp * 4 + slot
    many = conv_bc.shape[1] // (4 * dp)
    bc_own = lax.dynamic_slice_in_dim(acc[:, inner:steps_at] + bc_got, rank * many, many, 1)
    per = acc[:2, steps_at : steps_at + heads]
    gain_grads_ffn = lax.dynamic_slice_in_dim(acc[0, steps_at + 128 :], place_dp * rows_here, rows_here, 0)
    quarter_rows = rows_here // 4
    shared_own = sent1[:, inner + 128 :].reshape(4, quarter_rows, 128).swapaxes(0, 1).reshape(quarter_rows, -1)
    return (
        output,
        grad_tokens,
        gain_grads_in,
        sent2[:, :inner],
        sent1[:, :inner],
        sent1[:, inner : inner + heads] + sent1[:, inner + heads : inner + 2 * heads],
        shared_own[:, : 2 * STATE],
        own[:4],
        own[4],
        bc_own[:4],
        bc_own[4],
        per[0],
        per[1],
        skip,
        sent2[:, inner:],
        shared_own[:, 2 * STATE : 2 * STATE + 128],
        shared_own[:, 2 * STATE + 128 :],
        sent3[:, inner:].T,
        sent3[:, :inner].T,
        gain_grads_ffn,
        sent4[:, :hidden_cols],
        sent4[:, hidden_cols:],
        sent5,
    )


def solution(mesh):
    in_specs = (
        P("dp", None),
        P("dp", None),
        P("dp", None),
        P(),
        P("dp", "head"),
        P("dp", "head"),
        P("dp", "head"),
        P("dp", None),
        P(None, "head"),
        P("head"),
        P(),
        P(),
        P("head"),
        P("head"),
        P("head"),
        P("dp", "head"),
        P("dp", None),
        P("dp", None),
        P("head", "dp"),
        P("head", "dp"),
        P(),
        P("dp", "head"),
        P("dp", "head"),
        P("head", "dp"),
    )
    out_specs = (
        P("dp", None),
        P("dp", None),
        P("dp"),
        P("dp", "head"),
        P("dp", "head"),
        P("dp", "head"),
        P(("dp", "head"), None),
        P(None, "head"),
        P("head"),
        P(None, ("dp", "head")),
        P(("dp", "head")),
        P("head"),
        P("head"),
        P("head"),
        P("dp", "head"),
        P(("dp", "head"), None),
        P(("dp", "head"), None),
        P("head", "dp"),
        P("head", "dp"),
        P("dp"),
        P("dp", "head"),
        P("dp", "head"),
        P("head", "dp"),
    )
    return jax.shard_map(body, mesh=mesh, in_specs=in_specs, out_specs=out_specs, check_vma=False)
```
